32 devices in a mesh: dp: 2 (over core), tx: 4 (over y, x), ty: 4 (over z).
Axes of the slice: x: 2, y: 2, z: 4, core: 2. Of those that a mesh axis runs over, the one named last changes fastest.
Arguments:
- x_given: bfloat16 [4, 2048, 1536], P('tx', 'dp', 'ty'), may hold values from -6 to 6
- cotangent: bfloat16 [4, 2048, 1536], P('tx', 'dp', 'ty'), may hold values from -6 to 6
- seq_lengths: int32 [4, 4], replicated, may hold values from 128 to 896, as said below
- seq_deal: int32 [4, 4], replicated, may hold values from 0 to 3, as said below
- attn_gain: float32 [1536], P('ty'), may hold values from 0.5 to 1.5
- w_query: bfloat16 [1536, 1536], P('ty', 'tx'), may hold values from -0.15625 to 0.15625
- w_key: bfloat16 [1536, 1536], P('ty', 'tx'), may hold values from -0.15625 to 0.15625
- w_value: bfloat16 [1536, 1536], P('ty', 'tx'), may hold values from -0.15625 to 0.15625
- w_ogate: bfloat16 [1536, 1536], P('ty', 'tx'), may hold values from -0.15625 to 0.15625
- w_forget: bfloat16 [1536, 24], P('ty', 'tx'), may hold values from -0.21875 to 0.21875
- b_forget: float32 [24], P('tx'), may hold values from 2.5 to 9
- w_out: bfloat16 [1536, 1536], P('tx', 'ty'), may hold values from -0.625 to 0.625
- mlp_gain: float32 [1536], P('ty'), may hold values from 0.5 to 1.5
- w_gate: bfloat16 [1536, 4096], P('ty', 'tx'), may hold values from -0.15625 to 0.15625
- w_up: bfloat16 [1536, 4096], P('ty', 'tx'), may hold values from -0.15625 to 0.15625
- w_down: bfloat16 [4096, 1536], P('tx', 'ty'), may hold values from -0.09375 to 0.09375
Outputs:
- output: bfloat16 [4, 2048, 1536], P('tx', 'dp', 'ty')
- grad_input: bfloat16 [4, 2048, 1536], P('tx', 'dp', 'ty')
- grad_attn_gain: float32 [1536], P('ty')
- grad_w_query: float32 [1536, 1536], P('ty', 'tx')
- grad_w_key: float32 [1536, 1536], P('ty', 'tx')
- grad_w_value: float32 [1536, 1536], P('ty', 'tx')
- grad_w_ogate: float32 [1536, 1536], P('ty', 'tx')
- grad_w_forget: float32 [1536, 24], P('ty', 'tx')
- grad_b_forget: float32 [24], P('tx')
- grad_w_out: float32 [1536, 1536], P('tx', 'ty')
- grad_mlp_gain: float32 [1536], P('ty')
- grad_w_gate: float32 [1536, 4096], P('ty', 'tx')
- grad_w_up: float32 [1536, 4096], P('ty', 'tx')
- grad_w_down: float32 [4096, 1536], P('tx', 'ty')
The draws below stay inside these ranges and needn't reach their ends.
Inputs may be any that keep to these rules, and one draw needn't show every extreme that they name: `seq_lengths`: in every stream, dealt slots 2r and 2r + 1 hold block r's two sequences, whose lengths sum to 1024; in every stream some block holds a sequence of 128 tokens. `seq_deal`: each row is a permutation of 0 to 3.
All inputs are finite; a program needn't handle non-finite values.
Results may differ from the reference program's by a relative error of at most 0.017.
Values may be sent and summed in bfloat16 or wider, within the bound.
No kernel may reach another device: no remote copies, remote signals or barrier semaphores. Data moves between devices by JAX's collectives and lax.ppermute only.
A program may use at most 256 MiB of HBM per device.

```python
import jax
import jax.numpy as jnp
from jax import lax

D = 1536
H = 24
HEAD = 64
FF = 4096
Q = 1024
HD = 1536
COL_TOK = 2048
N_DP = 2
N_TX = 4


def seq_plan(key):
    cuts = jax.random.randint(jax.random.fold_in(key, 11), (N_TX, N_DP), Q // 8, Q - Q // 8 + 1)
    chosen = jax.random.randint(jax.random.fold_in(key, 12), (N_TX, 1), 0, N_DP)
    row_numbers = jnp.arange(N_DP, dtype=jnp.int32)[None, :]
    cuts = jnp.where(row_numbers == chosen, Q // 8, cuts).astype(jnp.int32)
    dealt_lengths = jnp.stack([cuts, Q - cuts], axis=-1).reshape(N_TX, 2 * N_DP).astype(jnp.int32)
    stream_keys = jax.random.split(jax.random.fold_in(key, 13), N_TX)

    def shuffle(item_key):
        return jax.random.permutation(item_key, 2 * N_DP)
    dealing = jax.vmap(shuffle)(stream_keys).astype(jnp.int32)
    lengths = jnp.take_along_axis(dealt_lengths, dealing, axis=1).astype(jnp.int32)
    return (lengths, dealing)


def draw_seq_lengths(key, part):
    plan = seq_plan(key)
    return plan[0]


def draw_seq_deal(key, part):
    plan = seq_plan(key)
    return plan[1]


def shard_levels(rng, extent, cuts, smallest, largest):
    def one(axis_at, blocks):
        draws = jax.random.uniform(jax.random.fold_in(jax.random.fold_in(rng, 6), axis_at), (blocks,), jnp.float32, smallest / len(cuts), largest / len(cuts))
        return jnp.repeat(jnp.exp(draws), extent[axis_at] // blocks).reshape((-1,) + (1,) * (len(extent) - axis_at - 1))

    level = one(*cuts[0])
    for cut in cuts[1:]:
        level = level * one(*cut)
    return level


def gaussian(stream_key, extent, scale, limit, cuts=(), kind=jnp.bfloat16):
    level = shard_levels(stream_key, extent, cuts, -0.22, 0.18) if cuts else 1.0
    values = jax.random.normal(stream_key, extent, jnp.float32) * scale * level
    return jnp.minimum(jnp.maximum(values, -limit), limit).astype(kind)


def setup_inputs(seed: int = 0) -> dict:
    key_list = jax.random.split(jax.random.key(seed), 17)
    x_given = gaussian(key_list[0], (N_TX, COL_TOK, D), 1.0, 6.0, ((0, 4), (1, 2), (2, 4)))
    cotangent = gaussian(key_list[1], (N_TX, COL_TOK, D), 1.0, 6.0, ((0, 4), (1, 2), (2, 4)))
    seq_lengths = draw_seq_lengths(jax.random.fold_in(key_list[16], 71), 0)
    seq_deal = draw_seq_deal(jax.random.fold_in(key_list[16], 71), 0)
    attn_gain = jnp.clip(1.0 + 0.1 * jax.random.normal(key_list[4], (D,), jnp.float32), 0.5, 1.5)
    w_query = gaussian(key_list[5], (D, HD), D ** -0.5, 0.15625, ((0, 4), (1, 4)))
    w_key = gaussian(key_list[6], (D, HD), D ** -0.5, 0.15625, ((0, 4), (1, 4)))
    w_value = gaussian(key_list[7], (D, HD), D ** -0.5, 0.15625, ((0, 4), (1, 4)))
    w_ogate = gaussian(key_list[8], (D, HD), D ** -0.5, 0.15625, ((0, 4), (1, 4)))
    w_forget = gaussian(key_list[9], (D, H), (D // 2) ** -0.5, 0.21875, ((0, 4), (1, 4)))
    b_forget = jnp.clip(2.5 + 6.5 * jax.random.uniform(key_list[10], (H,), jnp.float32) ** shard_levels(key_list[10], (H,), ((0, 4),), -0.2, 0.2), 2.5, 9.0)
    w_out = gaussian(key_list[11], (HD, D), (HD // 16) ** -0.5, 0.625, ((0, 4), (1, 4)))
    mlp_gain = jnp.clip(1.0 + 0.1 * jax.random.normal(key_list[12], (D,), jnp.float32), 0.5, 1.5)
    w_gate = gaussian(key_list[13], (D, FF), D ** -0.5, 0.15625, ((0, 4), (1, 4)))
    w_up = gaussian(key_list[14], (D, FF), D ** -0.5, 0.15625, ((0, 4), (1, 4)))
    w_down = gaussian(key_list[15], (FF, D), FF ** -0.5, 0.09375, ((0, 4), (1, 4)))
    return dict(x_given=x_given, cotangent=cotangent, seq_lengths=seq_lengths, seq_deal=seq_deal, attn_gain=attn_gain, w_query=w_query, w_key=w_key, w_value=w_value, w_ogate=w_ogate, w_forget=w_forget, b_forget=b_forget, w_out=w_out, mlp_gain=mlp_gain, w_gate=w_gate, w_up=w_up, w_down=w_down)


EPSILON = 1e-06
HIGHEST_PRECISION = lax.Precision.HIGHEST

@jax.custom_vjp
def low(v):
    return lax.optimization_barrier(v.astype(jnp.bfloat16)).astype(jnp.float32)

@jax.custom_vjp
def low_back(v):
    return v

def low_keep(v):
    return (low(v), None)

def low_pass(kept, grad):
    return (grad,)

def back_keep(v):
    return (v, None)

def back_low(kept, grad):
    return (low(grad),)
low.defvjp(low_keep, low_pass)
low_back.defvjp(back_keep, back_low)

def pick_small(lookup, indices):
    width = lookup.shape[0]
    matches = indices[:, None] == jnp.arange(width, dtype=jnp.int32)[None, :]
    return lax.optimization_barrier(jnp.sum(jnp.where(matches, lookup[None, :], 0), axis=1)).astype(jnp.int32)

def stream_tables(lengths, dealing):
    width = lengths.shape[0]
    numbers = jnp.arange(width, dtype=jnp.int32)
    given_start = (jnp.cumsum(lengths) - lengths).astype(jnp.int32)
    owners = lax.optimization_barrier(jnp.sum(jnp.where(dealing[None, :] == numbers[:, None], numbers[None, :], 0), axis=1)).astype(jnp.int32)
    dealt_length = pick_small(lengths, owners)
    dealt_start = (jnp.cumsum(dealt_length) - dealt_length).astype(jnp.int32)
    return (given_start, owners, dealt_start)

def dealt_sources(lengths, dealing, first_place, row_total):
    given_start, owners, dealt_start = stream_tables(lengths, dealing)
    places = first_place + jnp.arange(row_total, dtype=jnp.int32)
    slot_ids = (lax.optimization_barrier(jnp.sum((dealt_start[None, :] <= places[:, None]).astype(jnp.int32), axis=1)) - 1).astype(jnp.int32)
    source = pick_small(given_start, pick_small(owners, slot_ids)) + places - pick_small(dealt_start, slot_ids)
    return (source.astype(jnp.int32), slot_ids)

def given_targets(lengths, dealing, first_place, row_total):
    given_start, owners, dealt_start = stream_tables(lengths, dealing)
    places = first_place + jnp.arange(row_total, dtype=jnp.int32)
    member = (lax.optimization_barrier(jnp.sum((given_start[None, :] <= places[:, None]).astype(jnp.int32), axis=1)) - 1).astype(jnp.int32)
    target = pick_small(dealt_start, pick_small(dealing, member)) + places - pick_small(given_start, member)
    return target.astype(jnp.int32)

def product(left, right):
    return jnp.dot(left, right, precision=HIGHEST_PRECISION)

def rms_norm(values, gain):
    scale = lax.rsqrt(lax.optimization_barrier(jnp.mean(values * values, axis=-1, keepdims=True)) + EPSILON)
    return low(values * scale * gain)

def attention(queries, keys_in, values, decays, slot_ids):
    row_total = queries.shape[0]
    group_heads = H // N_TX
    places = jnp.arange(row_total, dtype=jnp.int32)
    allowed = (slot_ids[:, None] == slot_ids[None, :]) & (places[:, None] >= places[None, :])

    def one_group(inputs):
        group_q, group_k, group_v, group_decay = inputs
        raw_scores = jnp.einsum('qhd,khd->hqk', group_q, group_k, precision=HIGHEST_PRECISION) * HEAD ** (-0.5)
        raw_scores = raw_scores + group_decay.T[:, :, None] - group_decay.T[:, None, :]
        raw_scores = low_back(jnp.where(allowed[None], raw_scores, -1e+30))
        probabilities = jax.nn.softmax(raw_scores, axis=-1)
        return low_back(jnp.einsum('hqk,khd->qhd', low(probabilities), group_v, precision=HIGHEST_PRECISION))

    def split_heads(array):
        return array.reshape(row_total, N_TX, group_heads, HEAD).transpose(1, 0, 2, 3)
    grouped_decay = decays.reshape(row_total, N_TX, group_heads).transpose(1, 0, 2)
    outputs = lax.map(jax.checkpoint(one_group), (split_heads(queries), split_heads(keys_in), split_heads(values), grouped_decay))
    return outputs.transpose(1, 0, 2, 3).reshape(row_total, H * HEAD)

def layer_block(resid, slot_ids, params):
    attn_gain, w_query, w_key, w_value, w_ogate, w_forget, b_forget, w_out, mlp_gain, w_gate, w_up, w_down = params
    row_total = resid.shape[0]
    first_normed = rms_norm(resid, attn_gain)
    queries = low(low_back(product(first_normed, w_query))).reshape(row_total, H, HEAD)
    keys_in = low(low_back(product(first_normed, w_key))).reshape(row_total, H, HEAD)
    values = low(low_back(product(first_normed, w_value))).reshape(row_total, H, HEAD)
    out_gate = jax.nn.sigmoid(low_back(product(first_normed, w_ogate)))
    keep_log = jax.nn.log_sigmoid(low_back(product(first_normed, w_forget) + b_forget))
    decays = jnp.cumsum(keep_log, axis=0)
    mixed = low(attention(queries, keys_in, values, decays, slot_ids) * out_gate)
    second_resid = resid + low_back(product(mixed, w_out))
    second_normed = rms_norm(second_resid, mlp_gain)
    gate_pre = low_back(product(second_normed, w_gate))
    up_pre = low_back(product(second_normed, w_up))
    hidden = low(jax.nn.silu(gate_pre) * up_pre)
    return second_resid + low_back(product(hidden, w_down))

def forward(given, params, sources, targets, slot_table):
    dealt = jnp.take_along_axis(given, sources[:, :, None], axis=1)
    blocks = dealt.reshape(N_TX * N_DP, Q, D)
    slot_blocks = slot_table.reshape(N_TX * N_DP, Q)

    def step(carried, pair):
        return (carried, jax.checkpoint(layer_block)(pair[0], pair[1], params))
    unused_carry, outputs = lax.scan(step, jnp.float32(0.0), (blocks, slot_blocks))
    outputs = outputs.reshape(N_TX, COL_TOK, D)
    return jnp.take_along_axis(outputs, targets[:, :, None], axis=1)

def reference(x_given, cotangent, seq_lengths, seq_deal, attn_gain, w_query, w_key, w_value, w_ogate, w_forget, b_forget, w_out, mlp_gain, w_gate, w_up, w_down):

    def sources_of(lengths, dealing):
        return dealt_sources(lengths, dealing, 0, COL_TOK)

    def targets_of(lengths, dealing):
        return given_targets(lengths, dealing, 0, COL_TOK)
    sources, slot_table = jax.vmap(sources_of)(seq_lengths, seq_deal)
    targets = jax.vmap(targets_of)(seq_lengths, seq_deal)
    floats = (attn_gain.astype(jnp.float32), w_query.astype(jnp.float32), w_key.astype(jnp.float32), w_value.astype(jnp.float32), w_ogate.astype(jnp.float32), w_forget.astype(jnp.float32), b_forget.astype(jnp.float32), w_out.astype(jnp.float32), mlp_gain.astype(jnp.float32), w_gate.astype(jnp.float32), w_up.astype(jnp.float32), w_down.astype(jnp.float32))

    def run(given, *params):
        return forward(given, params, sources, targets, slot_table)
    result, pullback = jax.vjp(run, x_given.astype(jnp.float32), *floats)
    grads = pullback(cotangent.astype(jnp.float32))
    return (result.astype(jnp.bfloat16), grads[0].astype(jnp.bfloat16), grads[1], grads[2], grads[3], grads[4], grads[5], grads[6], grads[7], grads[8], grads[9], grads[10], grads[11], grads[12])
```

```python
import jax
import jax.numpy as jnp
from jax import lax
from jax.experimental import pallas as pl
from jax.experimental.pallas import tpu as pltpu
from jax.sharding import PartitionSpec as P

EPSILON = 1e-06
FAR = 1e30
LANES = 128
BF = jnp.bfloat16
F32 = jnp.float32


def dot(left, right, dims=((1,), (0,))):
    return lax.dot_general(left, right, (dims, ((), ())), preferred_element_type=F32)


NT = ((1,), (1,))
TN = ((0,), (0,))


def three_parts(values):
    one = lax.reduce_precision(values, 8, 7)
    two = lax.reduce_precision(values - one, 8, 7)
    three = lax.reduce_precision(values - one - two, 8, 7)
    return one, two, three


def pick_small(lookup, indices):
    width = lookup.shape[0]
    matches = indices[:, None] == jnp.arange(width, dtype=jnp.int32)[None, :]
    return jnp.sum(jnp.where(matches, lookup[None, :], 0), axis=1)


def stream_tables(lengths, dealing):
    width = lengths.shape[0]
    numbers = jnp.arange(width, dtype=jnp.int32)
    given_start = jnp.cumsum(lengths) - lengths
    owners = jnp.sum(jnp.where(dealing[None, :] == numbers[:, None], numbers[None, :], 0), axis=1)
    dealt_length = pick_small(lengths, owners)
    dealt_start = jnp.cumsum(dealt_length) - dealt_length
    return (given_start, owners, dealt_start, dealt_length)


def dealt_sources(lengths, dealing, places):
    given_start, owners, dealt_start, unused = stream_tables(lengths, dealing)
    slot_ids = jnp.sum((dealt_start[None, :] <= places[:, None]).astype(jnp.int32), axis=1) - 1
    return (
        pick_small(given_start, pick_small(owners, slot_ids))
        + places
        - pick_small(dealt_start, slot_ids)
    )


def given_targets(lengths, dealing, places):
    given_start, unused, dealt_start, unused = stream_tables(lengths, dealing)
    member = jnp.sum((given_start[None, :] <= places[:, None]).astype(jnp.int32), axis=1) - 1
    return (
        pick_small(dealt_start, pick_small(dealing, member))
        + places
        - pick_small(given_start, member)
    )


def swap(values, axis, step):
    return lax.ppermute(values, axis, [(at, at ^ step) for at in range(lax.axis_size(axis))])


def spread_plane(pieces):
    return [pieces[0]] + [swap(pieces[k], "tx", k) for k in (1, 2, 3)]


def spread_line(pieces):
    return [pieces[0]] + [swap(pieces[k], "ty", k) for k in (1, 2, 3)]


def mixed(pieces, start):
    stacked = jnp.stack(pieces)
    return [lax.dynamic_index_in_dim(stacked, start ^ k, 0, keepdims=False) for k in range(4)]


def to_plane(pieces, column, lane):
    pieces = spread_plane(pieces)
    pieces = spread_line(mixed(pieces, column ^ lane))
    return jnp.concatenate(mixed(pieces, lane), axis=1)


def from_plane(rows, column, lane):
    width = rows.shape[1] // 4
    pieces = [
        lax.dynamic_slice_in_dim(rows, (lane ^ k) * width, width, axis=1) for k in range(4)
    ]
    pieces = spread_line(pieces)
    return jnp.concatenate(spread_plane(mixed(pieces, column ^ lane)), axis=0)


def gather_rows(rows):
    half = rows.shape[0] // 2
    top, low = rows[:half], rows[half:]
    top_x, low_y = swap(top, "tx", 1), swap(low, "tx", 2)
    low_x, top_y = swap(low, "tx", 1), swap(top, "tx", 2)
    top_d, low_d = swap(top_x, "tx", 2), swap(low_y, "tx", 1)
    return jnp.concatenate([top, low, top_x, low_x, top_y, low_y, top_d, low_d], axis=0)


def scatter_product(rows, weights):
    piece = rows.shape[0] // 4
    half = weights.shape[0] // 2

    def part(k, w):
        return dot(rows[k * piece : (k + 1) * piece], w, NT)

    wa, wb = weights[:half], weights[half:]
    a3 = swap(part(3, wa).astype(BF), "tx", 1)
    b3 = swap(part(3, wb).astype(BF), "tx", 2)
    a1 = swap(part(1, wa).astype(BF), "tx", 1)
    b2 = swap(part(2, wb).astype(BF), "tx", 2)
    a2 = swap((part(2, wa) + a3.astype(F32)).astype(BF), "tx", 2)
    b1 = swap((part(1, wb) + b3.astype(F32)).astype(BF), "tx", 1)
    a0 = part(0, wa) + a1.astype(F32) + a2.astype(F32)
    b0 = part(0, wb) + b2.astype(F32) + b1.astype(F32)
    return jnp.concatenate([a0, b0], axis=1)


def pair_rows(piece):
    if lax.axis_size("dp") != 2:
        return lax.all_gather(piece, "dp", axis=0, tiled=True)
    other = swap(piece, "dp", 1)
    mine = lax.axis_index("dp") == 0
    return jnp.concatenate([jnp.where(mine, piece, other), jnp.where(mine, other, piece)], axis=0)


def pick_kernel(index_ref, *refs):
    count = len(refs) // 3
    row_total = refs[0].shape[0]
    places = lax.broadcasted_iota(jnp.int32, (index_ref.shape[0], 2 * row_total), 1)
    chosen = jnp.where(places == index_ref[...], 1.0, 0.0).astype(BF)
    for at in range(count):
        own, other, out = refs[2 * at], refs[2 * at + 1], refs[2 * count + at]
        picked = dot(chosen[:, :row_total], own[...]) + dot(chosen[:, row_total:], other[...])
        out[...] = picked.astype(BF)


def pick_rows(indices, pairs):
    row_total, width = pairs[0][0].shape
    block = row_total // 4
    whole = pl.BlockSpec((row_total, width), lambda i: (0, 0))
    return pl.pallas_call(
        pick_kernel,
        grid=(4,),
        in_specs=[pl.BlockSpec((block, 1), lambda i: (i, 0))] + [whole] * (2 * len(pairs)),
        out_specs=[pl.BlockSpec((block, width), lambda i: (i, 0))] * len(pairs),
        out_shape=[jax.ShapeDtypeStruct((row_total, width), BF)] * len(pairs),
        compiler_params=pltpu.CompilerParams(vmem_limit_bytes=32 * 2**20),
        cost_estimate=pl.CostEstimate(
            flops=4 * row_total * row_total * width * len(pairs),
            bytes_accessed=6 * row_total * width * len(pairs),
            transcendentals=0,
        ),
    )(indices[:, None], *[half for pair in pairs for half in pair])


def moved_rows(indices, arrays, first_place):
    row_total = arrays[0].shape[0]
    if lax.axis_size("dp") != 2:
        return [jnp.take(lax.all_gather(a, "dp", axis=0, tiled=True), indices, axis=0) for a in arrays]
    span = 2 * row_total
    near = lax.rem(indices - first_place + span, span)
    return pick_rows(near, [(a, swap(a, "dp", 1)) for a in arrays])


def lanes_of(rows):
    return lax.broadcasted_iota(jnp.int32, (rows, LANES), 1)


def split_column(column):
    one = column.astype(BF).astype(F32)
    two = (column - one).astype(BF).astype(F32)
    return one, two, column - one - two


def fill(lanes, base, columns, rest):
    for at, column in reversed(list(enumerate(columns))):
        rest = jnp.where(lanes == base + at, column, rest)
    return rest


def forward_kernel(
    meta, q_ref, k_ref, v_ref, gate_ref, keep_ref, y_ref, att_ref, qa_ref, ka_ref, c_ref, va_ref
):
    pair = pl.program_id(0)
    column, first_length = meta[0], meta[1]
    row_total = q_ref.shape[0]
    block = row_total // 4
    lanes = lanes_of(block)

    def rows_of(at):
        return pl.ds(pl.multiple_of((column ^ at) * block, block), block)

    @pl.when(pair == 0)
    def sum_keeps():
        below = lax.broadcasted_iota(jnp.int32, (block, block), 0)
        across = lax.broadcasted_iota(jnp.int32, (block, block), 1)
        ones = jnp.where(below >= across, 1.0, 0.0)
        running = jnp.zeros((1, LANES), F32)
        for at in range(4):
            sums = running + lax.dot_general(
                ones,
                keep_ref[rows_of(at), :],
                (((1,), (0,)), ((), ())),
                precision=lax.Precision.HIGHEST,
                preferred_element_type=F32,
            )
            c_ref[pl.ds(at * block, block), :] = sums
            running = sums[block - 1 :, :]

    for head in range(2):
        mine = (lanes < 64) if head == 0 else (lanes >= 64)
        base = 64 if head == 0 else 0
        for at in range(4):
            rows, own = rows_of(at), pl.ds(at * block, block)
            decay = jnp.sum(
                jnp.where(lanes == 2 * pair + head, c_ref[own, :], 0.0), axis=1, keepdims=True
            )
            one, two, three = split_column(decay)
            places = at * block + lax.broadcasted_iota(jnp.int32, (block, 1), 0)
            second = jnp.where(places >= first_length, 1.0, 0.0)
            q_side = fill(lanes, base, (1.0, 1.0, 1.0, second), 0.0)
            k_side = fill(
                lanes, base, (-one, -two, -three, (second - 1.0) * FAR, 1.0, 1.0, 1.0), 0.0
            )
            qa_ref[head, own, :] = jnp.where(
                mine, q_ref[rows, :].astype(F32) * 0.125, q_side
            ).astype(BF)
            ka_ref[head, own, :] = jnp.where(mine, k_ref[rows, :].astype(F32), k_side).astype(BF)
            va_ref[head, own, :] = jnp.where(mine, v_ref[rows, :].astype(F32), 1.0).astype(BF)

    below = lax.broadcasted_iota(jnp.int32, (block, block), 0)
    across = lax.broadcasted_iota(jnp.int32, (block, block), 1)
    for at in range(4):
        own = pl.ds(at * block, block)
        width = (at + 1) * block
        results = []
        for head in range(2):
            base = 64 if head == 0 else 0
            queries = qa_ref[head, own, :]
            last = jnp.where(
                below >= across, dot(queries, ka_ref[head, at * block : width, :], NT), -FAR
            )
            top = jnp.max(last, axis=1, keepdims=True)
            if at > 0:
                early = dot(queries, ka_ref[head, : at * block, :], NT)
                top = jnp.maximum(top, jnp.max(early, axis=1, keepdims=True))
            total = dot(jnp.exp(last - top).astype(BF), va_ref[head, at * block : width, :])
            if at > 0:
                total += dot(jnp.exp(early - top).astype(BF), va_ref[head, : at * block, :])
            weight = pltpu.roll(total, 64, 1)
            results.append(total / weight)
            log_total = top + jnp.log(total[:, base : base + 1])
            one, two, three = split_column(log_total)
            qa_ref[head, own, :] = fill(
                lanes, base + 4, (-one, -two, -three), queries.astype(F32)
            ).astype(BF)
        attended = jnp.where(lanes < 64, results[0], results[1])
        rows = rows_of(at)
        att_ref[rows, :] = attended
        y_ref[rows, :] = (attended * gate_ref[rows, :]).astype(BF)


def attend_forward(meta, qkv, out_gate, keep):
    row_total, width = out_gate.shape
    pairs = width // LANES
    heads = 2 * pairs

    def columns(first):
        return pl.BlockSpec((row_total, LANES), lambda p, m: (0, first + p))

    sided = pl.BlockSpec((2, row_total, LANES), lambda p, m: (p, 0, 0))
    return pl.pallas_call(
        forward_kernel,
        grid_spec=pltpu.PrefetchScalarGridSpec(
            num_scalar_prefetch=1,
            grid=(pairs,),
            in_specs=[
                columns(0),
                columns(pairs),
                columns(2 * pairs),
                columns(0),
                pl.BlockSpec((row_total, LANES), lambda p, m: (0, 0)),
            ],
            out_specs=[columns(0), columns(0), sided, sided],
            scratch_shapes=[
                pltpu.VMEM((row_total, LANES), F32),
                pltpu.VMEM((2, row_total, LANES), BF),
            ],
        ),
        out_shape=[
            jax.ShapeDtypeStruct((row_total, width), BF),
            jax.ShapeDtypeStruct((row_total, width), F32),
            jax.ShapeDtypeStruct((heads, row_total, LANES), BF),
            jax.ShapeDtypeStruct((heads, row_total, LANES), BF),
        ],
        compiler_params=pltpu.CompilerParams(vmem_limit_bytes=48 * 2**20),
        cost_estimate=pl.CostEstimate(
            flops=heads * row_total * row_total * 256,
            bytes_accessed=row_total * width * 16,
            transcendentals=heads * row_total * row_total // 2,
        ),
    )(meta, qkv, qkv, qkv, out_gate, keep)


def backward_kernel(
    meta,
    qa_ref,
    ka_ref,
    v_ref,
    dy_ref,
    gate_ref,
    att_ref,
    slope_ref,
    out_ref,
    va_ref,
    da_ref,
    kt_ref,
    dk_ref,
    dv_ref,
    dq_ref,
    dc_ref,
):
    pair = pl.program_id(0)
    pairs = pl.num_programs(0)
    column = meta[0]
    row_total = v_ref.shape[0]
    block = row_total // 4
    lanes = lanes_of(block)
    width = gate_ref.shape[1] * pairs

    def rows_of(at):
        return pl.ds(pl.multiple_of((column ^ at) * block, block), block)

    def lanes_at(group):
        return pl.ds(pl.multiple_of((group * pairs + pair) * LANES, LANES), LANES)

    @pl.when(pair == 0)
    def clear():
        dc_ref[...] = jnp.zeros_like(dc_ref)

    for at in range(4):
        rows, own = rows_of(at), pl.ds(at * block, block)
        gate, grad_y, attended = gate_ref[rows, :], dy_ref[rows, :], att_ref[rows, :]
        grad_att = (grad_y * gate).astype(BF).astype(F32)
        out_ref[rows, lanes_at(3)] = (grad_y * attended * gate * (1.0 - gate)).astype(BF)
        inner = grad_att * attended
        values = v_ref[rows, :].astype(F32)
        for head in range(2):
            mine = (lanes < 64) if head == 0 else (lanes >= 64)
            base = 64 if head == 0 else 0
            delta = jnp.sum(jnp.where(mine, inner, 0.0), axis=1, keepdims=True)
            one, two, three = split_column(delta)
            da_ref[head, own, :] = jnp.where(
                mine, grad_att, fill(lanes, base, (-one, -two, -three), 0.0)
            ).astype(BF)
            va_ref[head, own, :] = jnp.where(
                mine, values, fill(lanes, base, (1.0, 1.0, 1.0), 0.0)
            ).astype(BF)

    below = lax.broadcasted_iota(jnp.int32, (block, block), 0)
    across = lax.broadcasted_iota(jnp.int32, (block, block), 1)
    for head in range(2):
        for at in range(4):
            own = pl.ds(at * block, block)
            kt_ref[:, own] = ka_ref[head, own, :].astype(F32).T.astype(BF)
        for at in range(4):
            own = pl.ds(at * block, block)
            queries, grads = qa_ref[head, own, :], da_ref[head, own, :]
            dq_t = jnp.zeros((LANES, block), F32)
            for past in range(at + 1):
                keys = pl.ds(past * block, block)
                probs = jnp.exp(dot(ka_ref[head, keys, :], queries, NT))
                if past == at:
                    probs = jnp.where(below <= across, probs, 0.0)
                grad_scores = (probs * dot(va_ref[head, keys, :], grads, NT)).astype(BF)
                dv = dot(probs.astype(BF), grads)
                dk = dot(grad_scores, queries)
                dq_t += dot(kt_ref[:, keys], grad_scores)
                if past == at:
                    dv_ref[head, keys, :] = dv
                    dk_ref[head, keys, :] = dk
                else:
                    dv_ref[head, keys, :] += dv
                    dk_ref[head, keys, :] += dk
            dq_ref[head, own, :] = dq_t.T

    for at in range(4):
        rows, own = rows_of(at), pl.ds(at * block, block)
        for head in range(2):
            base = 64 if head == 0 else 0
            change = (
                dq_ref[head, own, base + 4 : base + 5] - dk_ref[head, own, base : base + 1]
            )
            dc_ref[own, :] += jnp.where(lanes == 2 * pair + head, change, 0.0)
        left = lanes < 64
        for group, ref, scale in ((0, dq_ref, 0.125), (1, dk_ref, 1.0), (2, dv_ref, 1.0)):
            both = jnp.where(left, ref[0, own, :], ref[1, own, :])
            out_ref[rows, lanes_at(group)] = (both * scale).astype(BF)

    @pl.when(pair == pairs - 1)
    def finish():
        ones = jnp.where(below <= across, 1.0, 0.0)
        running = jnp.zeros((1, LANES), F32)
        for at in reversed(range(4)):
            sums = running + lax.dot_general(
                ones,
                dc_ref[pl.ds(at * block, block), :],
                (((1,), (0,)), ((), ())),
                precision=lax.Precision.HIGHEST,
                preferred_element_type=F32,
            )
            running = sums[:1, :]
            rows = rows_of(at)
            out_ref[rows, 4 * width :] = (sums * slope_ref[rows, :]).astype(BF)


def attend_backward(meta, qa, ka, qkv, grad_y, out_gate, attended, slope):
    row_total, width = out_gate.shape
    pairs = width // LANES
    heads = 2 * pairs
    total = 4 * width + LANES

    def columns(first):
        return pl.BlockSpec((row_total, LANES), lambda p, m: (0, first + p))

    sided = pl.BlockSpec((2, row_total, LANES), lambda p, m: (p, 0, 0))
    both = (2, row_total, LANES)
    return pl.pallas_call(
        backward_kernel,
        grid_spec=pltpu.PrefetchScalarGridSpec(
            num_scalar_prefetch=1,
            grid=(pairs,),
            in_specs=[
                sided,
                sided,
                columns(2 * pairs),
                columns(0),
                columns(0),
                columns(0),
                pl.BlockSpec((row_total, LANES), lambda p, m: (0, 0)),
            ],
            out_specs=pl.BlockSpec((row_total, total), lambda p, m: (0, 0)),
            scratch_shapes=[
                pltpu.VMEM(both, BF),
                pltpu.VMEM(both, BF),
                pltpu.VMEM((LANES, row_total), BF),
                pltpu.VMEM(both, F32),
                pltpu.VMEM(both, F32),
                pltpu.VMEM(both, F32),
                pltpu.VMEM((row_total, LANES), F32),
            ],
        ),
        out_shape=jax.ShapeDtypeStruct((row_total, total), BF),
        compiler_params=pltpu.CompilerParams(vmem_limit_bytes=48 * 2**20),
        cost_estimate=pl.CostEstimate(
            flops=heads * row_total * row_total * 640,
            bytes_accessed=row_total * width * 20,
            transcendentals=heads * row_total * row_total // 2,
        ),
    )(meta, qa, ka, qkv, grad_y, out_gate, attended, slope)


def mean_scale(rows):
    return lax.rsqrt(jnp.mean(rows * rows, axis=1, keepdims=True) + EPSILON)


def norm_backward(grad, normed, scale, gain):
    grad_normed = grad * gain
    inner = jnp.mean(grad_normed * normed, axis=1, keepdims=True)
    return scale * (grad_normed - normed * inner), jnp.sum(grad * normed, axis=0)


def on_device(
    x_given,
    cotangent,
    seq_lengths,
    seq_deal,
    attn_gain,
    w_query,
    w_key,
    w_value,
    w_ogate,
    w_forget,
    b_forget,
    w_out,
    mlp_gain,
    w_gate,
    w_up,
    w_down,
):
    quarter = x_given.shape[1]
    piece = quarter // 4
    row, column, lane = lax.axis_index("dp"), lax.axis_index("tx"), lax.axis_index("ty")
    first_place = row * quarter
    heads = w_forget.shape[1]
    width = w_query.shape[1]
    hidden = w_gate.shape[1]
    share = w_query.shape[0] // lax.axis_size("dp")

    def own_share(weights):
        return lax.dynamic_slice_in_dim(weights, row * share, share, axis=0)

    def whole(weights):
        return lax.all_gather(weights, ("ty", "dp"), axis=0, tiled=True)

    gains = jnp.stack(three_parts(attn_gain) + three_parts(mlp_gain), axis=1).astype(BF)
    spare = jnp.zeros((w_query.shape[0], LANES - heads - 6), BF)
    w_first = whole(
        jnp.concatenate(
            [own_share(w) for w in (w_query, w_key, w_value, w_ogate, w_forget, gains, spare)],
            axis=1,
        )
    )
    w_out_t = whole(own_share(w_out.T))
    w_gate_up = whole(jnp.concatenate([own_share(w_gate), own_share(w_up)], axis=1))
    w_down_t = whole(own_share(w_down.T))

    local = jnp.arange(quarter, dtype=jnp.int32)
    swapped = (((local // piece) ^ column) * piece) + local % piece
    own_lengths = lax.dynamic_index_in_dim(seq_lengths, column, 0, keepdims=False)
    own_dealing = lax.dynamic_index_in_dim(seq_deal, column, 0, keepdims=False)
    sources = dealt_sources(own_lengths, own_dealing, first_place + swapped)
    x_dealt, grad_dealt = moved_rows(sources, (x_given[0], cotangent[0]), first_place)

    def cut(rows):
        return [rows[k * piece : (k + 1) * piece] for k in range(4)]

    x_rows = to_plane(cut(x_dealt), column, lane)
    x_full = gather_rows(x_rows)
    grad_rows = to_plane(cut(grad_dealt), column, lane)
    grad_full = gather_rows(grad_rows)

    gain_parts = w_first[:, 4 * width + heads : 4 * width + heads + 6].astype(F32).T
    gain_one = (gain_parts[0] + gain_parts[1] + gain_parts[2])[None]
    gain_two = (gain_parts[3] + gain_parts[4] + gain_parts[5])[None]

    x_wide = x_full.astype(F32)
    first_normed = (x_wide * mean_scale(x_wide) * gain_one).astype(BF)
    pre = dot(first_normed, w_first)
    qkv = pre[:, : 3 * width].astype(BF)
    out_gate = jax.nn.sigmoid(pre[:, 3 * width : 4 * width])
    real = jnp.arange(LANES) < heads
    forget_pre = jnp.where(
        real[None], pre[:, 4 * width :] + jnp.pad(b_forget, (0, LANES - heads))[None], 0.0
    )
    keep = jax.nn.log_sigmoid(forget_pre)
    slope = jnp.where(real[None], jax.nn.sigmoid(-forget_pre), 0.0)

    block_lengths = lax.dynamic_index_in_dim(seq_lengths, lane, 0, keepdims=False)
    block_dealing = lax.dynamic_index_in_dim(seq_deal, lane, 0, keepdims=False)
    slot_lengths = stream_tables(block_lengths, block_dealing)[3]
    first_length = lax.dynamic_index_in_dim(slot_lengths, 2 * row, 0, keepdims=False)
    meta = jnp.stack([column, first_length]).astype(jnp.int32)
    gated, attended, qa, ka = attend_forward(meta, qkv, out_gate, keep)

    x_own = x_rows.astype(F32)
    second = x_own + scatter_product(gated, w_out_t)

    scale_two = mean_scale(second)
    normed_two = second * scale_two
    h2_full = gather_rows((normed_two * gain_two).astype(BF))
    up_gate = dot(h2_full, w_gate_up)
    gate_pre, up_pre = up_gate[:, :hidden], up_gate[:, hidden:]
    grad_mid = dot(grad_full, w_down_t)
    gate_sig = jax.nn.sigmoid(gate_pre)
    gate_silu = gate_pre * gate_sig
    mid = (gate_silu * up_pre).astype(BF)
    grad_gate = (grad_mid * up_pre * gate_sig * (1.0 + gate_pre * (1.0 - gate_sig))).astype(BF)
    grad_up = (grad_mid * gate_silu).astype(BF)
    grad_gate_up = jnp.concatenate([grad_gate, grad_up], axis=1)
    grad_h2 = scatter_product(grad_gate_up, w_gate_up)
    result = second + scatter_product(mid, w_down_t)

    def summed(grads):
        return lax.psum_scatter(grads, ("ty", "dp"), scatter_dimension=0, tiled=True)

    grads_mlp = summed(
        jnp.concatenate(
            [dot(h2_full, grad_gate_up, TN).astype(BF), dot(grad_full, mid, TN).astype(BF)], axis=1
        )
    )

    grad_norm, gain_two_part = norm_backward(grad_h2, normed_two, scale_two, gain_two)
    grad_second = grad_rows.astype(F32) + grad_norm
    grad_z = gather_rows(grad_second.astype(BF))
    grad_y = dot(grad_z, w_out_t)
    grad_first = attend_backward(meta, qa, ka, qkv, grad_y, out_gate, attended, slope)
    grad_h1 = scatter_product(grad_first, w_first)
    grads_attn = summed(
        jnp.concatenate(
            [dot(first_normed, grad_first, TN).astype(BF), dot(grad_z, gated, TN).astype(BF)],
            axis=1,
        )
    )
    scale_one = mean_scale(x_own)
    grad_norm, gain_one_part = norm_backward(grad_h1, x_own * scale_one, scale_one, gain_one)
    grad_x = grad_second + grad_norm

    targets = given_targets(own_lengths, own_dealing, first_place + local)
    at = targets % quarter
    dealt_at = targets - at + ((at // piece) ^ column) * piece + at % piece
    output = moved_rows(
        dealt_at, (from_plane(result.astype(BF), column, lane),), first_place
    )[0]
    grad_input = moved_rows(
        dealt_at, (from_plane(grad_x.astype(BF), column, lane),), first_place
    )[0]

    bias_part = jnp.sum(grad_first[:, 4 * width :].astype(F32), axis=0)
    bias_slots = jnp.where(jnp.arange(4)[:, None] == column, bias_part[None], 0.0).reshape(-1)
    small = lax.psum(
        jnp.concatenate([gain_one_part, gain_two_part, bias_slots]), ("dp", "tx", "ty")
    )
    total = w_query.shape[0]
    full = total * 4
    grad_attn_gain = lax.dynamic_slice_in_dim(small, lane * total, total)
    grad_mlp_gain = lax.dynamic_slice_in_dim(small, full + lane * total, total)
    grad_b_forget = lax.dynamic_slice_in_dim(small, 2 * full + column * LANES, heads)

    mlp = pair_rows(grads_mlp).astype(F32)
    attn = pair_rows(grads_attn).astype(F32)
    last = 4 * width + LANES
    return (
        output[None],
        grad_input[None],
        grad_attn_gain,
        attn[:, :width],
        attn[:, width : 2 * width],
        attn[:, 2 * width : 3 * width],
        attn[:, 3 * width : 4 * width],
        attn[:, 4 * width : 4 * width + heads],
        grad_b_forget,
        attn[:, last:].T,
        grad_mlp_gain,
        mlp[:, :hidden],
        mlp[:, hidden : 2 * hidden],
        mlp[:, 2 * hidden :].T,
    )


def solution(mesh):
    tokens, feature, grid, flipped = P("tx", "dp", "ty"), P("ty"), P("ty", "tx"), P("tx", "ty")
    return jax.shard_map(
        on_device,
        mesh=mesh,
        in_specs=(
            tokens,
            tokens,
            P(),
            P(),
            feature,
            grid,
            grid,
            grid,
            grid,
            grid,
            P("tx"),
            flipped,
            feature,
            grid,
            grid,
            flipped,
        ),
        out_specs=(
            tokens,
            tokens,
            feature,
            grid,
            grid,
            grid,
            grid,
            grid,
            P("tx"),
            flipped,
            feature,
            grid,
            grid,
            flipped,
        ),
        check_vma=False,
    )
```

```python
import jax
import jax.numpy as jnp
from jax import lax
from jax.experimental import pallas as pl
from jax.experimental.pallas import tpu as pltpu
from jax.sharding import PartitionSpec as P

EPSILON = 1e-06
FAR = 1e30
LANES = 128
BF = jnp.bfloat16
F32 = jnp.float32


def dot(left, right, dims=((1,), (0,))):
    return lax.dot_general(left, right, (dims, ((), ())), preferred_element_type=F32)


NT = ((1,), (1,))
TN = ((0,), (0,))


def three_parts(values):
    one = lax.reduce_precision(values, 8, 7)
    two = lax.reduce_precision(values - one, 8, 7)
    three = lax.reduce_precision(values - one - two, 8, 7)
    return one, two, three


def pick_small(lookup, indices):
    width = lookup.shape[0]
    matches = indices[:, None] == jnp.arange(width, dtype=jnp.int32)[None, :]
    return jnp.sum(jnp.where(matches, lookup[None, :], 0), axis=1)


def stream_tables(lengths, dealing):
    width = lengths.shape[0]
    numbers = jnp.arange(width, dtype=jnp.int32)
    given_start = jnp.cumsum(lengths) - lengths
    owners = jnp.sum(jnp.where(dealing[None, :] == numbers[:, None], numbers[None, :], 0), axis=1)
    dealt_length = pick_small(lengths, owners)
    dealt_start = jnp.cumsum(dealt_length) - dealt_length
    return (given_start, owners, dealt_start, dealt_length)


def dealt_sources(lengths, dealing, places):
    given_start, owners, dealt_start, unused = stream_tables(lengths, dealing)
    slot_ids = jnp.sum((dealt_start[None, :] <= places[:, None]).astype(jnp.int32), axis=1) - 1
    return (
        pick_small(given_start, pick_small(owners, slot_ids))
        + places
        - pick_small(dealt_start, slot_ids)
    )


def given_targets(lengths, dealing, places):
    given_start, unused, dealt_start, unused = stream_tables(lengths, dealing)
    member = jnp.sum((given_start[None, :] <= places[:, None]).astype(jnp.int32), axis=1) - 1
    return (
        pick_small(dealt_start, pick_small(dealing, member))
        + places
        - pick_small(given_start, member)
    )


def swap(values, axis, step):
    return lax.ppermute(values, axis, [(at, at ^ step) for at in range(lax.axis_size(axis))])


def spread_plane(pieces):
    return [pieces[0]] + [swap(pieces[k], "tx", k) for k in (1, 2, 3)]


def spread_line(pieces):
    return [pieces[0]] + [swap(pieces[k], "ty", k) for k in (1, 2, 3)]


def pairs_sum(parts):
    return (parts[0] + parts[1]) + (parts[2] + parts[3])


def tie(*groups):
    return lax.optimization_barrier(groups)


def gather_rows(top, low, beside=None, ahead=None):
    top_x, low_y = swap(top, "tx", 1), swap(low, "tx", 2)
    low_x, top_y = swap(low, "tx", 1), swap(top, "tx", 2)
    top_x, low_y, ahead = tie(top_x, low_y, ahead)
    top_d, low_d = swap(top_x, "tx", 2), swap(low_y, "tx", 1)
    done = None if beside is None else beside((top_x, ahead))
    return [top, low, top_x, low_x, top_y, low_y, top_d, low_d], done


def scatter_products(lefts, weights, beside=None):
    a3, a1, a2, a0 = half_products(0, (3, 1, 2, 0), lefts, weights)
    arrays, a3, a1 = tie([array for array, unused in lefts], a3, a1)
    lefts = [(array, lead) for array, (unused, lead) in zip(arrays, lefts)]
    a3, a1 = swap(a3, "tx", 1), swap(a1, "tx", 1)
    b3, b2, b1, b0 = half_products(1, (3, 2, 1, 0), lefts, weights)
    a3, b3, b2 = tie(a3, b3, b2)
    b3, b2 = swap(b3, "tx", 2), swap(b2, "tx", 2)
    send_a2 = (a2 + a3.astype(F32)).astype(BF)
    send_b1 = (b1 + b3.astype(F32)).astype(BF)
    done = None if beside is None else beside(send_b1)
    a2, b1 = swap(send_a2, "tx", 2), swap(send_b1, "tx", 1)
    a1, a2, b1, b2, done = tie(a1, a2, b1, b2, done)
    return [a0, a1, a2, b0, b1, b2], done


def summed(part):
    return lax.psum_scatter(part, ("ty", "dp"), scatter_dimension=0, tiled=True)


def reduce_end(piece):
    if lax.axis_size("dp") != 2:
        return lax.all_gather(piece, "dp", axis=0, tiled=True).astype(F32)
    other = swap(piece, "dp", 1)
    lower = lax.axis_index("dp") == 0
    return jnp.concatenate(
        [jnp.where(lower, piece, other), jnp.where(lower, other, piece)], axis=0
    ).astype(F32)


def cost(flops, bytes_accessed):
    return pl.CostEstimate(flops=flops, bytes_accessed=bytes_accessed, transcendentals=0)


LIMIT = pltpu.CompilerParams(vmem_limit_bytes=50 * 2**20)
ALONE = pltpu.CompilerParams(vmem_limit_bytes=60 * 2**20)


def part_kernel(order, count, *refs):
    lefts, rights, outs = refs[:count], refs[count : 2 * count], refs[2 * count :]
    total = 0.0
    for left, right in zip(lefts, rights):
        rows = left[...]
        total += dot(rows.reshape(rows.shape[-2:]), right[...], NT)
    piece = outs[0].shape[0]
    for at, out in zip(order, outs):
        out[...] = total[at * piece : (at + 1) * piece].astype(out.dtype)


def half_products(half_at, order, lefts, weights):
    row_total, feature = lefts[0][0].shape[-2], weights[0][0].shape[0]
    piece, half, block = row_total // 4, feature // 2, 256
    first = half_at * half // block
    left_specs, right_specs = [], []
    flops = 0
    for (array, lead), (weight, width, at) in zip(lefts, weights):
        if lead is None:
            left_specs.append(pl.BlockSpec((row_total, width), lambda i: (0, 0)))
        else:
            left_specs.append(
                pl.BlockSpec((1, row_total, width), lambda i, lead=lead: (lead, 0, 0))
            )
        right_specs.append(pl.BlockSpec((block, width), lambda i, at=at: (first + i, at)))
        flops += 2 * row_total * half * width
    return pl.pallas_call(
        lambda *refs: part_kernel(order, len(lefts), *refs),
        grid=(half // block,),
        in_specs=left_specs + right_specs,
        out_specs=[pl.BlockSpec((piece, block), lambda i: (0, i))] * 4,
        out_shape=[jax.ShapeDtypeStruct((piece, half), BF)] * 2
        + [jax.ShapeDtypeStruct((piece, half), F32)] * 2,
        compiler_params=LIMIT,
        cost_estimate=cost(flops, flops // 500),
    )(*[a for a, unused in lefts], *[w for w, *unused in weights])


def row_kernel(left, right, out):
    width = right.shape[2]
    for n in range(2):
        out[:, n * width : (n + 1) * width] = dot(left[...], right[n], TN).astype(BF)


def row_products(left, right):
    row_total, feature = left.shape
    width, block = right.shape[2], 256
    flops = 4 * row_total * feature * width
    return pl.pallas_call(
        row_kernel,
        grid=(feature // block,),
        in_specs=[
            pl.BlockSpec((row_total, block), lambda i: (0, i)),
            pl.BlockSpec(right.shape, lambda i: (0, 0, 0)),
        ],
        out_specs=pl.BlockSpec((block, 2 * width), lambda i: (i, 0)),
        out_shape=jax.ShapeDtypeStruct((feature, 2 * width), BF),
        compiler_params=LIMIT,
        cost_estimate=cost(flops, flops // 500),
    )(left, right)


def join_kernel(*refs):
    join(refs[:8], refs[8])


def joined(pieces):
    rows, feature = pieces[0].shape
    block = feature // 4
    return pl.pallas_call(
        join_kernel,
        grid=(4,),
        in_specs=[pl.BlockSpec((rows, block), lambda i: (0, i))] * 8,
        out_specs=pl.BlockSpec((8 * rows, block), lambda i: (0, i)),
        out_shape=jax.ShapeDtypeStruct((8 * rows, feature), BF),
        compiler_params=ALONE,
        cost_estimate=cost(1, 6 * 2**20),
    )(*pieces)


def turned_kernel(left, right, out):
    out[...] = dot(left[...], right[...], TN).astype(BF)


def turned_products(left, right):
    row_total, feature = right.shape
    width, block = left.shape[1], feature // 4
    flops = 2 * row_total * feature * width
    return pl.pallas_call(
        turned_kernel,
        grid=(4,),
        in_specs=[
            pl.BlockSpec((row_total, width), lambda i: (0, 0)),
            pl.BlockSpec((row_total, block), lambda i: (0, i)),
        ],
        out_specs=pl.BlockSpec((width, block), lambda i: (i, 0)),
        out_shape=jax.ShapeDtypeStruct((4 * width, block), BF),
        compiler_params=LIMIT,
        cost_estimate=cost(flops, flops // 500),
    )(left, right)


def attn_kernel(h_ref, z_ref, d_ref, g_ref, y_ref, out):
    total, width = d_ref.shape[1], y_ref.shape[1]
    normed = h_ref[...]
    out[:, :total] = dot(normed, d_ref[...], TN).astype(BF)
    out[:, total : total + width] = dot(normed, g_ref[...], TN).astype(BF)
    out[:, total + width :] = dot(y_ref[...], z_ref[...], TN).astype(BF)


def attn_products(first_normed, grad_first, grad_gate, grad_z, gated):
    row_total, feature = first_normed.shape
    total, width = grad_first.shape[1], gated.shape[1]
    block = feature // 4
    column = pl.BlockSpec((row_total, block), lambda i: (0, i))

    def whole(columns):
        return pl.BlockSpec((row_total, columns), lambda i: (0, 0))

    return pl.pallas_call(
        attn_kernel,
        grid=(4,),
        in_specs=[column, column, whole(total), whole(width), whole(width)],
        out_specs=pl.BlockSpec((block, total + 2 * width), lambda i: (i, 0)),
        out_shape=jax.ShapeDtypeStruct((feature, total + 2 * width), BF),
        compiler_params=LIMIT,
        cost_estimate=cost(2 * row_total * feature * (total + 2 * width), 16 * 2**20),
    )(first_normed, grad_z, grad_first, grad_gate, gated)


def place_kernel(at, *refs):
    ins, outs = refs[:4], refs[4:]
    width, half = ins[0].shape[1], outs[0].shape[0]
    for k in range(4):
        columns = pl.ds(pl.multiple_of((at[0] ^ k) * width, LANES), width)
        for n, out in enumerate(outs):
            out[:, columns] = ins[k][n * half : (n + 1) * half, :]


def placed(pieces, start):
    rows, width = pieces[0].shape
    return pl.pallas_call(
        place_kernel,
        grid_spec=pltpu.PrefetchScalarGridSpec(
            num_scalar_prefetch=1,
            grid=(1,),
            in_specs=[pl.BlockSpec((rows, width), lambda i, at: (0, 0))] * 4,
            out_specs=[pl.BlockSpec((rows // 2, 4 * width), lambda i, at: (0, 0))] * 2,
        ),
        out_shape=[jax.ShapeDtypeStruct((rows // 2, 4 * width), BF)] * 2,
        compiler_params=ALONE,
        cost_estimate=cost(1, 4 * 2**20),
    )(start.astype(jnp.int32)[None], *pieces)


def reorder_kernel(at, *refs):
    count = len(refs) // 4 - 1
    rows = refs[0].shape[0]
    for k in range(4):
        for n in range(4):

            @pl.when((at[0] ^ k) == n)
            def copy(k=k, n=n):
                for m in range(count):
                    refs[4 * count + k][m * rows : (m + 1) * rows, :] = refs[4 * m + n][...]


def reordered(sets, start):
    rows, width = sets[0][0].shape
    total = rows * len(sets)
    return pl.pallas_call(
        reorder_kernel,
        grid_spec=pltpu.PrefetchScalarGridSpec(
            num_scalar_prefetch=1,
            grid=(1,),
            in_specs=[pl.BlockSpec((rows, width), lambda i, at: (0, 0))] * (4 * len(sets)),
            out_specs=[pl.BlockSpec((total, width), lambda i, at: (0, 0))] * 4,
        ),
        out_shape=[jax.ShapeDtypeStruct((total, width), BF)] * 4,
        compiler_params=ALONE,
        cost_estimate=cost(1, 4 * 2**20),
    )(start.astype(jnp.int32)[None], *[p for pieces in sets for p in pieces])


def half_sums(parts):
    a0, a1, a2, b0, b1, b2 = (p[...].astype(F32) for p in parts)
    return jnp.concatenate([a0 + a1 + a2, b0 + b1 + b2], axis=1)


def mean_scale(rows):
    return lax.rsqrt(jnp.mean(rows * rows, axis=1, keepdims=True) + EPSILON)


def norm_backward(grad, rows, gain):
    scale = mean_scale(rows)
    normed = rows * scale
    grad_normed = grad * gain
    inner = jnp.mean(grad_normed * normed, axis=1, keepdims=True)
    return scale * (grad_normed - normed * inner)


def put_halves(value, top, low):
    step = pl.program_id(0)

    @pl.when(step < 2)
    def first():
        top[...] = value

    @pl.when(step >= 2)
    def second():
        low[...] = value


def put_quarters(lane, value, outs, held):
    held[...] = value
    width = outs[0].shape[1]
    for k, out in enumerate(outs):
        out[...] = held[:, pl.ds(pl.multiple_of((lane ^ k) * width, LANES), width)]


def either(top, low):
    return jnp.where(pl.program_id(0) < 2, top[...].astype(F32), low[...].astype(F32))


def up_norm_kernel(where, x_top, x_low, gain_ref, *refs):
    second = either(x_top, x_low) + half_sums(refs[:6])
    refs[6][...] = second
    put_halves((second * mean_scale(second) * gain_ref[1:2, :]).astype(BF), refs[7], refs[8])


def down_norm_kernel(where, second_ref, grad_top, grad_low, gain_ref, *refs):
    grad = either(grad_top, grad_low) + norm_backward(
        half_sums(refs[:6]), second_ref[...], gain_ref[1:2, :]
    )
    refs[6][...] = grad
    put_halves(grad.astype(BF), refs[7], refs[8])


def result_kernel(where, second_ref, *refs):
    result = second_ref[...] + half_sums(refs[:6])
    put_quarters(where[2], result.astype(BF), refs[6:10], refs[10])


def input_norm_kernel(where, x_top, x_low, grad_ref, gain_ref, *refs):
    grad = grad_ref[...] + norm_backward(
        half_sums(refs[:6]), either(x_top, x_low), gain_ref[0:1, :]
    )
    put_quarters(where[2], grad.astype(BF), refs[6:10], refs[10])


def on_rows(kernel, where, rows, gains, parts, quarters):
    feature = gains.shape[1] if gains is not None else rows[0].shape[1]
    row_total = parts[0].shape[0]
    block = row_total // 4

    def spec(width):
        return pl.BlockSpec((block, width), lambda i, *_: (i, 0))

    top = pl.BlockSpec((block, feature), lambda i, *_: (jnp.minimum(i, 1), 0))
    low = pl.BlockSpec((block, feature), lambda i, *_: (jnp.maximum(i - 2, 0), 0))
    ins, args = [], []
    for r in rows:
        if isinstance(r, (list, tuple)):
            ins += [top, low]
            args += list(r)
        else:
            ins.append(spec(feature))
            args.append(r)
    if gains is not None:
        ins.append(pl.BlockSpec(gains.shape, lambda i, *_: (0, 0)))
    ins += [spec(feature // 2)] * 6
    if quarters:
        outs = [spec(feature // 4)] * 4
        shapes = [jax.ShapeDtypeStruct((row_total, feature // 4), BF)] * 4
        scratch = [pltpu.VMEM((block, feature), BF)]
    else:
        outs = [spec(feature), top, low]
        shapes = [jax.ShapeDtypeStruct((row_total, feature), F32)]
        shapes += [jax.ShapeDtypeStruct((2 * block, feature), BF)] * 2
        scratch = []
    return pl.pallas_call(
        kernel,
        grid_spec=pltpu.PrefetchScalarGridSpec(
            num_scalar_prefetch=1,
            grid=(4,),
            in_specs=ins,
            out_specs=outs,
            scratch_shapes=scratch,
        ),
        out_shape=shapes,
        compiler_params=ALONE,
        cost_estimate=cost(1, 6 * 2**20),
    )(where, *args, *([] if gains is None else [gains]), *parts)


def first_kernel(heads, pieces, w_ref, wf_ref, b_ref, h_ref, qkv_ref, keep_ref, slope_ref, gain_ref):
    step = pl.program_id(0)

    @pl.when(step == 0)
    def norm():
        turned = wf_ref[...].astype(F32).T
        for n in range(2):
            first = heads + 3 * n
            gain_ref[n : n + 1, :] = (
                turned[first : first + 1] + turned[first + 1 : first + 2] + turned[first + 2 : first + 3]
            )
        block = pieces[0].shape[0]
        for at in range(8):
            x = pieces[at][...].astype(F32)
            h_ref[pl.ds(at * block, block), :] = (x * mean_scale(x) * gain_ref[0:1, :]).astype(BF)

    pre = dot(h_ref[...], w_ref[...])
    qkv_ref[...] = pre.astype(BF)

    @pl.when(step == 4)
    def forget():
        real = lanes_of(pre.shape[0]) < heads
        forget_pre = jnp.where(real, pre[:, LANES:] + b_ref[...], 0.0)
        less = jnp.exp(-jnp.abs(forget_pre))
        keep_ref[...] = jnp.minimum(forget_pre, 0.0) - jnp.log1p(less)
        slope_ref[...] = jnp.where(
            real, jnp.where(forget_pre >= 0, less, 1.0) / (1.0 + less), 0.0
        )


def first_products(heads, pieces, weights, bias):
    row_total, feature = 8 * pieces[0].shape[0], pieces[0].shape[1]
    block = 256

    def whole_block(shape):
        return pl.BlockSpec(shape, lambda i: (0, 0))

    def spec(shape, at):
        return pl.BlockSpec(shape, at)

    def kernel(*refs):
        first_kernel(heads, refs[:8], *refs[8:])

    return pl.pallas_call(
        kernel,
        grid=(5,),
        in_specs=[whole_block(p.shape) for p in pieces]
        + [
            spec((feature, block), lambda i: (0, i)),
            spec((feature, LANES), lambda i: (0, 9)),
            whole_block((1, LANES)),
        ],
        out_specs=[
            whole_block((row_total, feature)),
            spec((row_total, block), lambda i: (0, i)),
            whole_block((row_total, LANES)),
            whole_block((row_total, LANES)),
            whole_block((8, feature)),
        ],
        out_shape=[
            jax.ShapeDtypeStruct((row_total, feature), BF),
            jax.ShapeDtypeStruct((row_total, 5 * block), BF),
            jax.ShapeDtypeStruct((row_total, LANES), F32),
            jax.ShapeDtypeStruct((row_total, LANES), F32),
            jax.ShapeDtypeStruct((8, feature), F32),
        ],
        compiler_params=ALONE,
        cost_estimate=cost(14 * row_total * feature * block, 16 * 2**20),
    )(*pieces, weights, weights, bias)


def gate_kernel(h_ref, w_ref, att_ref, gate_ref, y_ref):
    gate = jax.nn.sigmoid(dot(h_ref[...], w_ref[...]))
    gate_ref[...] = gate
    y_ref[...] = (att_ref[...] * gate).astype(BF)


def gate_products(first_normed, weights, attended):
    row_total, feature = first_normed.shape
    width = attended.shape[1]

    def by_rows(columns):
        return pl.BlockSpec((row_total // 4, columns), lambda i: (i, 0))

    return pl.pallas_call(
        gate_kernel,
        grid=(4,),
        in_specs=[
            by_rows(feature),
            pl.BlockSpec((feature, width), lambda i: (0, 0)),
            by_rows(width),
        ],
        out_specs=[by_rows(width)] * 2,
        out_shape=[
            jax.ShapeDtypeStruct((row_total, width), F32),
            jax.ShapeDtypeStruct((row_total, width), BF),
        ],
        compiler_params=LIMIT,
        cost_estimate=cost(2 * row_total * feature * width, 10 * 2**20),
    )(first_normed, weights, attended)


def join(pieces, whole):
    block = pieces[0].shape[0]
    for at in range(8):
        whole[pl.ds(at * block, block), :] = pieces[at][...]


def up_kernel(*refs):
    pieces, (g_ref, u_ref, h_ref, m_ref, to_gate_ref, to_up_ref) = refs[:8], refs[8:]

    @pl.when(pl.program_id(0) == 0)
    def first():
        join(pieces, h_ref)

    gate = dot(h_ref[...], g_ref[...])
    up = dot(h_ref[...], u_ref[...])
    sig = jax.nn.sigmoid(gate)
    silu = gate * sig
    m_ref[...] = (silu * up).astype(BF)
    to_gate_ref[...] = (up * sig * (1.0 + gate * (1.0 - sig))).astype(to_gate_ref.dtype)
    to_up_ref[...] = silu.astype(to_up_ref.dtype)


def up_products(pieces, weights):
    row_total, feature = 8 * pieces[0].shape[0], pieces[0].shape[1]
    hidden, block = weights.shape[1] // 2, 256
    steps = hidden // block
    out = pl.BlockSpec((row_total, block), lambda i: (0, i))
    return pl.pallas_call(
        up_kernel,
        grid=(steps,),
        in_specs=[pl.BlockSpec(p.shape, lambda i: (0, 0)) for p in pieces]
        + [
            pl.BlockSpec((feature, block), lambda i: (0, i)),
            pl.BlockSpec((feature, block), lambda i: (0, steps + i)),
        ],
        out_specs=[pl.BlockSpec((row_total, feature), lambda i: (0, 0))] + [out] * 3,
        out_shape=[
            jax.ShapeDtypeStruct((row_total, feature), BF),
            jax.ShapeDtypeStruct((row_total, hidden), BF),
            jax.ShapeDtypeStruct((row_total, hidden), BF),
            jax.ShapeDtypeStruct((row_total, hidden), BF),
        ],
        compiler_params=ALONE,
        cost_estimate=cost(4 * row_total * feature * hidden, 20 * 2**20),
    )(*pieces, weights, weights)


def down_kernel(g_ref, w_ref, to_gate_ref, to_up_ref, out_ref):
    grad = dot(g_ref[...], w_ref[...])
    out_ref[0] = (grad * to_gate_ref[...]).astype(BF)
    out_ref[1] = (grad * to_up_ref[...]).astype(BF)


def down_products(grad_out, weights, to_gate, to_up):
    row_total, feature = grad_out.shape
    hidden, block = weights.shape[1], 256
    column = pl.BlockSpec((row_total, block), lambda i: (0, i))
    return pl.pallas_call(
        down_kernel,
        grid=(hidden // block,),
        in_specs=[
            pl.BlockSpec((row_total, feature), lambda i: (0, 0)),
            pl.BlockSpec((feature, block), lambda i: (0, i)),
            column,
            column,
        ],
        out_specs=pl.BlockSpec((2, row_total, block), lambda i: (0, 0, i)),
        out_shape=jax.ShapeDtypeStruct((2, row_total, hidden), BF),
        compiler_params=LIMIT,
        cost_estimate=cost(2 * row_total * feature * hidden, 16 * 2**20),
    )(grad_out, weights, to_gate, to_up)


def back_kernel(*refs):
    pieces, (w_ref, gate_ref, att_ref, z_ref, datt_ref, dgate_ref) = refs[:8], refs[8:]
    block = pieces[0].shape[0]
    for at in range(4):

        @pl.when(pl.program_id(0) == at)
        def put(at=at):
            z_ref[:block, :] = pieces[2 * at][...]
            z_ref[block:, :] = pieces[2 * at + 1][...]

    grad = dot(z_ref[...], w_ref[...])
    gate = gate_ref[...]
    datt_ref[...] = (grad * gate).astype(BF)
    dgate_ref[...] = (grad * att_ref[...] * gate * (1.0 - gate)).astype(BF)


def back_products(pieces, weights, gate, attended):
    row_total, feature = 8 * pieces[0].shape[0], pieces[0].shape[1]
    width = attended.shape[1]

    def spec(shape, at=0):
        return pl.BlockSpec(shape, lambda i: (0, at))

    def by_rows(columns):
        return pl.BlockSpec((row_total // 4, columns), lambda i: (i, 0))

    return pl.pallas_call(
        back_kernel,
        grid=(4,),
        in_specs=[spec(p.shape) for p in pieces]
        + [spec((feature, width), 1), by_rows(width), by_rows(width)],
        out_specs=[by_rows(feature), by_rows(width), by_rows(width)],
        out_shape=[
            jax.ShapeDtypeStruct((row_total, feature), BF),
            jax.ShapeDtypeStruct((row_total, width), BF),
            jax.ShapeDtypeStruct((row_total, width), BF),
        ],
        compiler_params=ALONE,
        cost_estimate=cost(2 * row_total * feature * width, 10 * 2**20),
    )(*pieces, weights, gate, attended)


def slot_tables(lengths, dealing, stream):
    width = lengths.shape[1]
    given, slot_of = [], []
    start = jnp.int32(0)
    for g in range(width):
        given.append(start)
        start = start + lengths[stream, g]
        slot_of.append(dealing[stream, g])
    dealt, given_at = [], []
    start = jnp.int32(0)
    for k in range(width):
        dealt.append(start)
        here = jnp.int32(0)
        for g in range(width):
            here = jnp.where(slot_of[g] == k, given[g], here)
            start = start + jnp.where(slot_of[g] == k, lengths[stream, g], 0)
        given_at.append(here)
    return given, slot_of, dealt, given_at


def pick_kernel(backward, where, lengths, dealing, *refs):
    count = 2
    column, row = where[0], where[1]
    row_total = refs[0].shape[0] // (2 if backward else 1)
    block = row_total // 4
    step = pl.program_id(0)
    given, slot_of, dealt, given_at = slot_tables(lengths, dealing, column)
    within = lax.broadcasted_iota(jnp.int32, (block, 1), 0)
    if backward:
        places = row * row_total + step * block + within
        moves = []
        for g in range(len(given)):
            there = jnp.int32(0)
            for k in range(len(given)):
                there = jnp.where(slot_of[g] == k, dealt[k], there)
            moves.append((given[g], there - given[g]))
    else:
        places = row * row_total + (step ^ column) * block + within
        moves = [(s, g - s) for s, g in zip(dealt, given_at)]
    move = jnp.zeros_like(places) + moves[0][1]
    for first, by in moves[1:]:
        move = jnp.where(places >= first, by, move)
    near = places + move - row * row_total
    near = jnp.where(near < 0, near + 2 * row_total, near)
    if backward:
        other = jnp.where(near >= row_total, row_total, 0)
        local = near - other
        part = sum(jnp.where(local >= k * block, 1, 0) for k in (1, 2, 3))
        near = other + local + (jnp.bitwise_xor(part, column) - part) * block
    across = lax.broadcasted_iota(jnp.int32, (block, 2 * row_total), 1)
    chosen = jnp.where(across == near, 1.0, 0.0).astype(BF)
    for at in range(count):
        if backward:
            picked = 0.0
            for n in range(2):
                for k in range(4):
                    first = (4 * n + k) * block
                    picked += dot(
                        chosen[:, first : first + block],
                        refs[n][(2 * k + at) * block : (2 * k + at + 1) * block, :],
                    )
            refs[2 + at][...] = picked.astype(BF)
        else:
            own, other = refs[2 * at][...], refs[2 * at + 1][...]
            picked = dot(chosen[:, :row_total], own) + dot(chosen[:, row_total:], other)
            picked = picked.astype(BF)
            for k in range(4):

                @pl.when(step == k)
                def put(k=k, at=at, picked=picked):
                    refs[2 * count + 4 * at + k][...] = picked


def moved_rows(backward, where, lengths, dealing, arrays):
    row_total, width = arrays[0].shape
    if backward:
        row_total = row_total // 2
    block = row_total // 4
    if lax.axis_size("dp") != 2:
        column, row = where[0], where[1]
        local = jnp.arange(row_total, dtype=jnp.int32)
        own_lengths = lax.dynamic_index_in_dim(lengths, column, 0, keepdims=False)
        own_dealing = lax.dynamic_index_in_dim(dealing, column, 0, keepdims=False)
        if backward:
            to = given_targets(own_lengths, own_dealing, row * row_total + local)
            at = to % row_total
            to = to - at + ((at // block) ^ column) * block + at % block
            both = arrays[0].reshape(4, 2, block, width).transpose(1, 0, 2, 3)
            arrays = [half.reshape(row_total, width) for half in both]
        else:
            swapped = (((local // block) ^ column) * block) + local % block
            to = dealt_sources(own_lengths, own_dealing, row * row_total + swapped)
        moved = [jnp.take(lax.all_gather(a, "dp", axis=0, tiled=True), to, axis=0) for a in arrays]
        if backward:
            return moved
        return [m[k * block : (k + 1) * block] for m in moved for k in range(4)]
    if backward:
        outs = [pl.BlockSpec((block, width), lambda i, *_: (i, 0))] * 2
        shapes = [jax.ShapeDtypeStruct((row_total, width), BF)] * 2
    else:
        outs = [pl.BlockSpec((block, width), lambda i, *_: (0, 0))] * 8
        shapes = [jax.ShapeDtypeStruct((block, width), BF)] * 8
    return pl.pallas_call(
        lambda *refs: pick_kernel(backward, *refs),
        grid_spec=pltpu.PrefetchScalarGridSpec(
            num_scalar_prefetch=3,
            grid=(4,),
            in_specs=[pl.BlockSpec(arrays[0].shape, lambda i, *_: (0, 0))] * (2 * len(arrays)),
            out_specs=outs,
        ),
        out_shape=shapes,
        compiler_params=pltpu.CompilerParams(vmem_limit_bytes=40 * 2**20),
        cost_estimate=cost(8 * row_total * row_total * width * 2, 8 * 2**20),
    )(where, lengths, dealing, *[half for a in arrays for half in (a, swap(a, "dp", 1))])


def lanes_of(rows):
    return lax.broadcasted_iota(jnp.int32, (rows, LANES), 1)


def split_column(column):
    one = column.astype(BF).astype(F32)
    two = (column - one).astype(BF).astype(F32)
    return one, two, column - one - two


def fill(lanes, base, columns, rest):
    for at, column in reversed(list(enumerate(columns))):
        rest = jnp.where(lanes == base + at, column, rest)
    return rest


def forward_kernel(
    where,
    lengths,
    dealing,
    q_ref,
    k_ref,
    v_ref,
    keep_ref,
    att_ref,
    qa_ref,
    ka_ref,
    c_ref,
    va_ref,
):
    pair = pl.program_id(0)
    column, row, lane = where[0], where[1], where[2]
    first_length = jnp.int32(0)
    for g in range(lengths.shape[1]):
        first_length += jnp.where(dealing[lane, g] == 2 * row, lengths[lane, g], 0)
    row_total = q_ref.shape[0]
    block = row_total // 4
    lanes = lanes_of(block)

    def rows_of(at):
        return pl.ds(pl.multiple_of((column ^ at) * block, block), block)

    @pl.when(pair == 0)
    def sum_keeps():
        below = lax.broadcasted_iota(jnp.int32, (block, block), 0)
        across = lax.broadcasted_iota(jnp.int32, (block, block), 1)
        ones = jnp.where(below >= across, 1.0, 0.0)
        running = jnp.zeros((1, LANES), F32)
        for at in range(4):
            sums = running + lax.dot_general(
                ones,
                keep_ref[rows_of(at), :],
                (((1,), (0,)), ((), ())),
                precision=lax.Precision.HIGHEST,
                preferred_element_type=F32,
            )
            c_ref[pl.ds(at * block, block), :] = sums
            running = sums[block - 1 :, :]

    for head in range(2):
        mine = (lanes < 64) if head == 0 else (lanes >= 64)
        base = 64 if head == 0 else 0
        for at in range(4):
            rows, own = rows_of(at), pl.ds(at * block, block)
            decay = jnp.sum(
                jnp.where(lanes == 2 * pair + head, c_ref[own, :], 0.0), axis=1, keepdims=True
            )
            one, two, three = split_column(decay)
            places = at * block + lax.broadcasted_iota(jnp.int32, (block, 1), 0)
            second = jnp.where(places >= first_length, 1.0, 0.0)
            q_side = fill(lanes, base, (1.0, 1.0, 1.0, second), 0.0)
            k_side = fill(
                lanes, base, (-one, -two, -three, (second - 1.0) * FAR, 1.0, 1.0, 1.0), 0.0
            )
            qa_ref[head, own, :] = jnp.where(
                mine, q_ref[rows, :].astype(F32) * 0.125, q_side
            ).astype(BF)
            ka_ref[head, own, :] = jnp.where(mine, k_ref[rows, :].astype(F32), k_side).astype(BF)
            va_ref[head, own, :] = jnp.where(mine, v_ref[rows, :].astype(F32), 1.0).astype(BF)

    below = lax.broadcasted_iota(jnp.int32, (block, block), 0)
    across = lax.broadcasted_iota(jnp.int32, (block, block), 1)
    for at in range(4):
        own = pl.ds(at * block, block)
        width = (at + 1) * block
        results = []
        for head in range(2):
            base = 64 if head == 0 else 0
            queries = qa_ref[head, own, :]
            last = jnp.where(
                below >= across, dot(queries, ka_ref[head, at * block : width, :], NT), -FAR
            )
            top = jnp.max(last, axis=1, keepdims=True)
            if at > 0:
                early = dot(queries, ka_ref[head, : at * block, :], NT)
                top = jnp.maximum(top, jnp.max(early, axis=1, keepdims=True))
            total = dot(jnp.exp(last - top).astype(BF), va_ref[head, at * block : width, :])
            if at > 0:
                total += dot(jnp.exp(early - top).astype(BF), va_ref[head, : at * block, :])
            weight = pltpu.roll(total, 64, 1)
            results.append(total / weight)
            log_total = top + jnp.log(total[:, base : base + 1])
            one, two, three = split_column(log_total)
            qa_ref[head, own, :] = fill(
                lanes, base + 4, (-one, -two, -three), queries.astype(F32)
            ).astype(BF)
        attended = jnp.where(lanes < 64, results[0], results[1])
        att_ref[rows_of(at), :] = attended


def attend_forward(where, lengths, dealing, qkv, keep):
    row_total, width = qkv.shape[0], qkv.shape[1] // LANES // 3 * LANES
    pairs = width // LANES
    heads = 2 * pairs

    def columns(first):
        return pl.BlockSpec((row_total, LANES), lambda p, *_: (0, first + p))

    sided = pl.BlockSpec((2, row_total, LANES), lambda p, *_: (p, 0, 0))
    return pl.pallas_call(
        forward_kernel,
        grid_spec=pltpu.PrefetchScalarGridSpec(
            num_scalar_prefetch=3,
            grid=(pairs,),
            in_specs=[
                columns(0),
                columns(pairs),
                columns(2 * pairs),
                pl.BlockSpec((row_total, LANES), lambda p, *_: (0, 0)),
            ],
            out_specs=[columns(0), sided, sided],
            scratch_shapes=[
                pltpu.VMEM((row_total, LANES), F32),
                pltpu.VMEM((2, row_total, LANES), BF),
            ],
        ),
        out_shape=[
            jax.ShapeDtypeStruct((row_total, width), F32),
            jax.ShapeDtypeStruct((heads, row_total, LANES), BF),
            jax.ShapeDtypeStruct((heads, row_total, LANES), BF),
        ],
        compiler_params=pltpu.CompilerParams(vmem_limit_bytes=60 * 2**20),
        cost_estimate=cost(10 * 10**9, 8 * 2**20),
    )(where, lengths, dealing, qkv, qkv, qkv, keep)


def backward_kernel(
    where,
    qa_ref,
    ka_ref,
    v_ref,
    datt_ref,
    att_ref,
    slope_ref,
    out_ref,
    va_ref,
    da_ref,
    kt_ref,
    dk_ref,
    dv_ref,
    dq_ref,
    dc_ref,
):
    pair = pl.program_id(0)
    pairs = pl.num_programs(0)
    column = where[0]
    row_total = v_ref.shape[0]
    block = row_total // 4
    lanes = lanes_of(block)
    width = att_ref.shape[1] * pairs

    def rows_of(at):
        return pl.ds(pl.multiple_of((column ^ at) * block, block), block)

    def lanes_at(group):
        return pl.ds(pl.multiple_of((group * pairs + pair) * LANES, LANES), LANES)

    @pl.when(pair == 0)
    def clear():
        dc_ref[...] = jnp.zeros_like(dc_ref)

    for at in range(4):
        rows, own = rows_of(at), pl.ds(at * block, block)
        grad_att = datt_ref[rows, :].astype(F32)
        inner = grad_att * att_ref[rows, :]
        values = v_ref[rows, :].astype(F32)
        for head in range(2):
            mine = (lanes < 64) if head == 0 else (lanes >= 64)
            base = 64 if head == 0 else 0
            delta = jnp.sum(jnp.where(mine, inner, 0.0), axis=1, keepdims=True)
            one, two, three = split_column(delta)
            da_ref[head, own, :] = jnp.where(
                mine, grad_att, fill(lanes, base, (-one, -two, -three), 0.0)
            ).astype(BF)
            va_ref[head, own, :] = jnp.where(
                mine, values, fill(lanes, base, (1.0, 1.0, 1.0), 0.0)
            ).astype(BF)

    below = lax.broadcasted_iota(jnp.int32, (block, block), 0)
    across = lax.broadcasted_iota(jnp.int32, (block, block), 1)
    for head in range(2):
        for at in range(4):
            own = pl.ds(at * block, block)
            kt_ref[:, own] = ka_ref[head, own, :].astype(F32).T.astype(BF)
        for at in range(4):
            own = pl.ds(at * block, block)
            queries, grads = qa_ref[head, own, :], da_ref[head, own, :]
            dq_t = jnp.zeros((LANES, block), F32)
            for past in range(at + 1):
                keys = pl.ds(past * block, block)
                probs = jnp.exp(dot(ka_ref[head, keys, :], queries, NT))
                if past == at:
                    probs = jnp.where(below <= across, probs, 0.0)
                grad_scores = (probs * dot(va_ref[head, keys, :], grads, NT)).astype(BF)
                dv = dot(probs.astype(BF), grads)
                dk = dot(grad_scores, queries)
                dq_t += dot(kt_ref[:, keys], grad_scores)
                if past == at:
                    dv_ref[head, keys, :] = dv
                    dk_ref[head, keys, :] = dk
                else:
                    dv_ref[head, keys, :] += dv
                    dk_ref[head, keys, :] += dk
            dq_ref[head, own, :] = dq_t.T

    for at in range(4):
        rows, own = rows_of(at), pl.ds(at * block, block)
        for head in range(2):
            base = 64 if head == 0 else 0
            change = (
                dq_ref[head, own, base + 4 : base + 5] - dk_ref[head, own, base : base + 1]
            )
            dc_ref[own, :] += jnp.where(lanes == 2 * pair + head, change, 0.0)
        left = lanes < 64
        for group, ref, scale in ((0, dq_ref, 0.125), (1, dk_ref, 1.0), (2, dv_ref, 1.0)):
            both = jnp.where(left, ref[0, own, :], ref[1, own, :])
            out_ref[rows, lanes_at(group)] = (both * scale).astype(BF)

    @pl.when(pair == pairs - 1)
    def finish():
        ones = jnp.where(below <= across, 1.0, 0.0)
        running = jnp.zeros((1, LANES), F32)
        for at in reversed(range(4)):
            sums = running + lax.dot_general(
                ones,
                dc_ref[pl.ds(at * block, block), :],
                (((1,), (0,)), ((), ())),
                precision=lax.Precision.HIGHEST,
                preferred_element_type=F32,
            )
            running = sums[:1, :]
            rows = rows_of(at)
            out_ref[rows, 3 * width :] = (sums * slope_ref[rows, :]).astype(BF)


def attend_backward(where, qa, ka, qkv, grad_att, attended, slope):
    row_total, width = attended.shape
    pairs = width // LANES
    heads = 2 * pairs
    total = 3 * width + LANES

    def columns(first):
        return pl.BlockSpec((row_total, LANES), lambda p, *_: (0, first + p))

    sided = pl.BlockSpec((2, row_total, LANES), lambda p, *_: (p, 0, 0))
    both = (2, row_total, LANES)
    return pl.pallas_call(
        backward_kernel,
        grid_spec=pltpu.PrefetchScalarGridSpec(
            num_scalar_prefetch=1,
            grid=(pairs,),
            in_specs=[
                sided,
                sided,
                columns(2 * pairs),
                columns(0),
                columns(0),
                pl.BlockSpec((row_total, LANES), lambda p, *_: (0, 0)),
            ],
            out_specs=pl.BlockSpec((row_total, total), lambda p, *_: (0, 0)),
            scratch_shapes=[
                pltpu.VMEM(both, BF),
                pltpu.VMEM(both, BF),
                pltpu.VMEM((LANES, row_total), BF),
                pltpu.VMEM(both, F32),
                pltpu.VMEM(both, F32),
                pltpu.VMEM(both, F32),
                pltpu.VMEM((row_total, LANES), F32),
            ],
        ),
        out_shape=jax.ShapeDtypeStruct((row_total, total), BF),
        compiler_params=pltpu.CompilerParams(vmem_limit_bytes=60 * 2**20),
        cost_estimate=cost(12 * 10**9, 8 * 2**20),
    )(where, qa, ka, qkv, grad_att, attended, slope)


def on_device(
    x_given,
    cotangent,
    seq_lengths,
    seq_deal,
    attn_gain,
    w_query,
    w_key,
    w_value,
    w_ogate,
    w_forget,
    b_forget,
    w_out,
    mlp_gain,
    w_gate,
    w_up,
    w_down,
):
    quarter = x_given.shape[1]
    piece = quarter // 4
    row, column, lane = lax.axis_index("dp"), lax.axis_index("tx"), lax.axis_index("ty")
    heads = w_forget.shape[1]
    width = w_query.shape[1]
    hidden = w_gate.shape[1]
    share = w_query.shape[0] // lax.axis_size("dp")

    def own_share(weights):
        return lax.dynamic_slice_in_dim(weights, row * share, share, axis=0)

    def whole(weights):
        return lax.all_gather(weights, ("ty", "dp"), axis=0, tiled=True)

    gains = jnp.stack(three_parts(attn_gain) + three_parts(mlp_gain), axis=1).astype(BF)
    spare = jnp.zeros((w_query.shape[0], LANES - heads - 6), BF)
    side = 3 * width
    last = side + LANES
    w_first = whole(
        jnp.concatenate(
            [own_share(w) for w in (w_query, w_key, w_value, w_forget, gains, spare)], axis=1
        )
    )

    where = jnp.stack([column, row, lane]).astype(jnp.int32)
    paired = lax.axis_size("dp") == 2

    dealt = moved_rows(False, where, seq_lengths, seq_deal, (x_given[0], cotangent[0]))
    x_parts, grad_parts = tie(spread_plane(dealt[:4]), dealt[4:])
    x_parts, grad_parts = tie(
        spread_line(reordered([x_parts], column ^ lane)), spread_plane(grad_parts)
    )
    grad_parts, x_parts = tie(reordered([grad_parts], column ^ lane), x_parts)
    grad_parts = spread_line(grad_parts)
    x_full, unused = gather_rows(*placed(x_parts, lane), ahead=grad_parts[1])
    w_second = jnp.concatenate([own_share(w_ogate), own_share(w_out.T)], axis=1)
    w_gate_up = jnp.concatenate([own_share(w_gate), own_share(w_up)], axis=1)
    x_full, grad_parts, w_second, w_gate_up = tie(x_full, grad_parts, w_second, w_gate_up)
    w_second, w_gate_up = whole(w_second), whole(w_gate_up)
    grad_rows = placed(grad_parts, lane)

    bias = jnp.pad(b_forget, (0, LANES - heads))[None]
    first_normed, qkv, keep, slope, gains = first_products(heads, x_full, w_first, bias)
    grad_full, (attended, qa, ka) = gather_rows(
        *grad_rows,
        lambda ready: attend_forward(where, seq_lengths, seq_deal, ready[1], keep),
        qkv,
    )
    grad_full, attended = tie(grad_full, attended)
    w_down_t, attended = tie(own_share(w_down.T), attended)
    w_down_t = whole(w_down_t)
    out_gate, gated = gate_products(first_normed, w_second, attended)
    parts, unused = scatter_products([(gated, None)], [(w_second, width, 1)])
    second, top, low = on_rows(up_norm_kernel, where, [x_full[:2]], gains, parts, False)

    h2_parts, grad_full = gather_rows(
        top, low, lambda ready: joined(tie(grad_full, ready)[0])
    )
    h2_parts, w_gate_up = tie(h2_parts, w_gate_up)
    h2_full, mid, to_gate, to_up = up_products(h2_parts, w_gate_up)
    part, grad_full = tie(turned_products(mid, grad_full), grad_full)
    grads_down = summed(part)
    grad_gate_up = down_products(grad_full, w_down_t, to_gate, to_up)

    def gate_up_products(ready):
        left, unused = tie(h2_full, ready)
        return row_products(left, grad_gate_up)

    parts, part = scatter_products(
        [(grad_gate_up, 0), (grad_gate_up, 1)],
        [(w_gate_up, hidden, 0), (w_gate_up, hidden, 1)],
        gate_up_products,
    )
    part, parts = tie(part, parts)
    grads_gate_up = summed(part)
    grad_second, top, low = on_rows(
        down_norm_kernel, where, [second, grad_rows], gains, parts, False
    )

    def result_products(ready):
        left, unused = tie(mid, ready)
        return [
            half_products(at, order, [(left, None)], [(w_down_t, hidden, 0)])
            for at, order in ((0, (3, 1, 2, 0)), (1, (3, 2, 1, 0)))
        ]

    z_parts, ((a3, a1, a2, a0), (b3, b2, b1, b0)) = gather_rows(top, low, result_products)

    z_parts, a3, a1, b3, b2 = tie(z_parts, a3, a1, b3, b2)
    a3, a1 = swap(a3, "tx", 1), swap(a1, "tx", 1)
    b3, b2 = swap(b3, "tx", 2), swap(b2, "tx", 2)
    z_full, grad_att, grad_ogate = back_products(z_parts, w_second, out_gate, attended)
    a3, b3, grad_att = tie(a3, b3, grad_att)
    a2 = swap((a2 + a3.astype(F32)).astype(BF), "tx", 2)
    b1 = swap((b1 + b3.astype(F32)).astype(BF), "tx", 1)
    grad_first = attend_backward(where, qa, ka, qkv, grad_att, attended, slope)
    grad_first, a1, a2, b1, b2, grads_down = tie(grad_first, a1, a2, b1, b2, grads_down)
    output = on_rows(result_kernel, where, [second], None, [a0, a1, a2, b0, b1, b2], True)
    output, grad_first = tie(output, grad_first)
    output = spread_line(output)
    part = attn_products(first_normed, grad_first, grad_ogate, z_full, gated)
    part, grad_first, output = tie(part, grad_first, output)
    grads_attn = summed(part)
    parts, unused = scatter_products(
        [(grad_first, None), (grad_ogate, None)],
        [(w_first, last, 0), (w_second, width, 0)],
    )
    bias_grad = jnp.sum(grad_first[:, side:].astype(F32), axis=0, keepdims=True)
    if paired:
        bias_grad = bias_grad + swap(bias_grad, "dp", 1)
        bias_grad = pairs_sum(spread_line([bias_grad] * 4))
    else:
        bias_grad = lax.psum(bias_grad, ("dp", "ty"))
    parts, grads_gate_up, bias_grad = tie(parts, grads_gate_up, bias_grad)
    grad_x = on_rows(input_norm_kernel, where, [x_full[:2], grad_second], gains, parts, True)

    output, grad_x = tie(output, spread_line(grad_x))
    back = spread_plane(reordered([output, grad_x], column ^ lane))

    grad_down = reduce_end(grads_down)
    grad_gate_up = reduce_end(grads_gate_up)
    grad_attn = reduce_end(grads_attn)

    def row_dots(*sides):
        return sum(jnp.sum(w.astype(F32) * g, axis=1) for w, g in sides)

    grads = [
        grad_attn[:, :width],
        grad_attn[:, width : 2 * width],
        grad_attn[:, 2 * width : side],
        grad_attn[:, last : last + width],
        grad_attn[:, side : side + heads],
    ]
    own_gains = jnp.stack(
        [
            row_dots(*zip((w_query, w_key, w_value, w_ogate, w_forget), grads)) / attn_gain,
            row_dots((w_gate, grad_gate_up[:, :hidden]), (w_up, grad_gate_up[:, hidden:]))
            / mlp_gain,
        ]
    )
    grad_gains = spread_plane([own_gains] * 4)
    back, grad_gains, grads = tie(back, grad_gains, grads)
    grad_gains = pairs_sum(grad_gains)
    output, grad_input = moved_rows(
        True, where, seq_lengths, seq_deal, [jnp.concatenate(back, axis=0)]
    )
    return (
        output[None],
        grad_input[None],
        grad_gains[0],
        *grads,
        bias_grad[0, :heads],
        grad_attn[:, last + width :],
        grad_gains[1],
        grad_gate_up[:, :hidden],
        grad_gate_up[:, hidden:],
        grad_down,
    )


def solution(mesh):
    tokens, feature, grid, flipped = P("tx", "dp", "ty"), P("ty"), P("ty", "tx"), P("tx", "ty")
    return jax.shard_map(
        on_device,
        mesh=mesh,
        in_specs=(
            tokens,
            tokens,
            P(),
            P(),
            feature,
            grid,
            grid,
            grid,
            grid,
            grid,
            P("tx"),
            flipped,
            feature,
            grid,
            grid,
            flipped,
        ),
        out_specs=(
            tokens,
            tokens,
            feature,
            grid,
            grid,
            grid,
            grid,
            grid,
            P("tx"),
            flipped,
            feature,
            grid,
            grid,
            flipped,
        ),
        check_vma=False,
    )
```

```python
import jax
import jax.numpy as jnp
from jax import lax
from jax.experimental import pallas as pl
from jax.experimental.pallas import tpu as pltpu
from jax.sharding import PartitionSpec as P

EPSILON = 1e-06
FAR = 1e30
LANES = 128
BF = jnp.bfloat16
F32 = jnp.float32


def dot(left, right, dims=((1,), (0,))):
    return lax.dot_general(left, right, (dims, ((), ())), preferred_element_type=F32)


NT = ((1,), (1,))
TN = ((0,), (0,))


def three_parts(values):
    one = lax.reduce_precision(values, 8, 7)
    two = lax.reduce_precision(values - one, 8, 7)
    three = lax.reduce_precision(values - one - two, 8, 7)
    return one, two, three


def pick_small(lookup, indices):
    width = lookup.shape[0]
    matches = indices[:, None] == jnp.arange(width, dtype=jnp.int32)[None, :]
    return jnp.sum(jnp.where(matches, lookup[None, :], 0), axis=1)


def stream_tables(lengths, dealing):
    width = lengths.shape[0]
    numbers = jnp.arange(width, dtype=jnp.int32)
    given_start = jnp.cumsum(lengths) - lengths
    owners = jnp.sum(jnp.where(dealing[None, :] == numbers[:, None], numbers[None, :], 0), axis=1)
    dealt_length = pick_small(lengths, owners)
    dealt_start = jnp.cumsum(dealt_length) - dealt_length
    return (given_start, owners, dealt_start, dealt_length)


def dealt_sources(lengths, dealing, places):
    given_start, owners, dealt_start, unused = stream_tables(lengths, dealing)
    slot_ids = jnp.sum((dealt_start[None, :] <= places[:, None]).astype(jnp.int32), axis=1) - 1
    return (
        pick_small(given_start, pick_small(owners, slot_ids))
        + places
        - pick_small(dealt_start, slot_ids)
    )


def given_targets(lengths, dealing, places):
    given_start, unused, dealt_start, unused = stream_tables(lengths, dealing)
    member = jnp.sum((given_start[None, :] <= places[:, None]).astype(jnp.int32), axis=1) - 1
    return (
        pick_small(dealt_start, pick_small(dealing, member))
        + places
        - pick_small(given_start, member)
    )


def swap(values, axis, step):
    return lax.ppermute(values, axis, [(at, at ^ step) for at in range(lax.axis_size(axis))])


def spread_plane(pieces):
    return [pieces[0]] + [swap(pieces[k], "tx", k) for k in (1, 2, 3)]


def spread_line(pieces):
    return [pieces[0]] + [swap(pieces[k], "ty", k) for k in (1, 2, 3)]


def pairs_sum(parts):
    return (parts[0] + parts[1]) + (parts[2] + parts[3])


def tie(*groups):
    return lax.optimization_barrier(groups)


UPPER, LOWER = (0, 2, 5, 6), (1, 4, 3, 7)


def gather_rows(top, low, beside=None, ahead=None):
    top_x, low_y = swap(top, "tx", 1), swap(low, "tx", 2)
    low_x, top_y = swap(low, "tx", 1), swap(top, "tx", 2)
    top_x, low_y, ahead = tie(top_x, low_y, ahead)
    top_d, low_d = swap(top_x, "tx", 2), swap(low_y, "tx", 1)
    done = None if beside is None else beside([top, low, top_x, low_y], ahead)
    return [top, low, top_x, low_y, low_x, top_y, top_d, low_d], done


def scatter_products(lefts, weights, beside=None):
    a3, a1, a2, a0 = part_products(0, (3, 1, 2, 0), lefts, weights)
    arrays, a3, a1 = tie([array for array, unused in lefts], a3, a1)
    lefts = [(array, lead) for array, (unused, lead) in zip(arrays, lefts)]
    a3, a1 = swap(a3, "tx", 1), swap(a1, "tx", 1)
    b3, b2, b1, b0 = part_products(1, (3, 2, 1, 0), lefts, weights)
    a3, b3, b2 = tie(a3, b3, b2)
    b3, b2 = swap(b3, "tx", 2), swap(b2, "tx", 2)
    send_a2 = (a2 + a3.astype(F32)).astype(BF)
    send_b1 = (b1 + b3.astype(F32)).astype(BF)
    done = None if beside is None else beside(send_b1)
    a2, b1 = swap(send_a2, "tx", 2), swap(send_b1, "tx", 1)
    a1, a2, b1, b2, done = tie(a1, a2, b1, b2, done)
    return [a0, a1, a2, b0, b1, b2], done


def summed(part):
    return lax.psum_scatter(part, ("ty", "dp"), scatter_dimension=0, tiled=True)


def reduce_end(piece):
    if lax.axis_size("dp") != 2:
        return lax.all_gather(piece, "dp", axis=0, tiled=True).astype(F32)
    other = swap(piece, "dp", 1)
    lower = lax.axis_index("dp") == 0
    return jnp.concatenate(
        [jnp.where(lower, piece, other), jnp.where(lower, other, piece)], axis=0
    ).astype(F32)


def cost(flops, bytes_accessed):
    return pl.CostEstimate(flops=flops, bytes_accessed=bytes_accessed, transcendentals=0)


LIMIT = pltpu.CompilerParams(vmem_limit_bytes=50 * 2**20)
ALONE = pltpu.CompilerParams(vmem_limit_bytes=60 * 2**20)


def part_kernel(order, count, *refs):
    lefts, rights, outs = refs[:count], refs[count : 2 * count], refs[2 * count :]
    total = 0.0
    for left, right in zip(lefts, rights):
        rows = left[...]
        total += dot(rows.reshape(rows.shape[-2:]), right[...], NT)
    half = outs[0].shape[0] // 2
    for at, out in zip(order, outs):
        for n, place in enumerate((UPPER[at], LOWER[at])):
            out[n * half : (n + 1) * half, :] = total[place * half : (place + 1) * half].astype(
                out.dtype
            )


def part_products(half_at, order, lefts, weights):
    row_total, feature = lefts[0][0].shape[-2], weights[0][0].shape[0]
    piece, block = row_total // 4, 256
    half = feature if half_at is None else feature // 2
    first = (half_at or 0) * half // block
    sent = 3 if half_at is None else 2
    left_specs, right_specs = [], []
    flops = 0
    for (array, place), (weight, width, at) in zip(lefts, weights):
        if array.ndim == 2:
            left_specs.append(pl.BlockSpec((row_total, width), lambda i, place=place: (0, place)))
        else:
            left_specs.append(
                pl.BlockSpec((1, row_total, width), lambda i, place=place: (place, 0, 0))
            )
        right_specs.append(pl.BlockSpec((block, width), lambda i, at=at: (first + i, at)))
        flops += 2 * row_total * half * width
    return pl.pallas_call(
        lambda *refs: part_kernel(order, len(lefts), *refs),
        grid=(half // block,),
        in_specs=left_specs + right_specs,
        out_specs=[pl.BlockSpec((piece, block), lambda i: (0, i))] * 4,
        out_shape=[jax.ShapeDtypeStruct((piece, half), BF)] * sent
        + [jax.ShapeDtypeStruct((piece, half), F32)] * (4 - sent),
        compiler_params=LIMIT,
        cost_estimate=cost(flops, flops // 500),
    )(*[a for a, unused in lefts], *[w for w, *unused in weights])


def row_kernel(left, right, out):
    width = right.shape[2]
    for n in range(2):
        out[:, n * width : (n + 1) * width] = dot(left[...], right[n], TN).astype(BF)


def row_products(left, right):
    row_total, feature = left.shape
    width, block = right.shape[2], 256
    flops = 4 * row_total * feature * width
    return pl.pallas_call(
        row_kernel,
        grid=(feature // block,),
        in_specs=[
            pl.BlockSpec((row_total, block), lambda i: (0, i)),
            pl.BlockSpec(right.shape, lambda i: (0, 0, 0)),
        ],
        out_specs=pl.BlockSpec((block, 2 * width), lambda i: (i, 0)),
        out_shape=jax.ShapeDtypeStruct((feature, 2 * width), BF),
        compiler_params=LIMIT,
        cost_estimate=cost(flops, flops // 500),
    )(left, right)


def turned_kernel(left, *refs):
    out, right = refs[8:]
    join(refs[:8], right)
    out[...] = dot(left[...], right[...], TN).astype(BF)


def turned_products(left, pieces):
    row_total, feature = left.shape[0], pieces[0].shape[1]
    width, block = left.shape[1], feature // 4
    flops = 2 * row_total * feature * width
    return pl.pallas_call(
        turned_kernel,
        grid=(4,),
        in_specs=[pl.BlockSpec((row_total, width), lambda i: (0, 0))]
        + [pl.BlockSpec((p.shape[0], block), lambda i: (0, i)) for p in pieces],
        out_specs=[
            pl.BlockSpec((width, block), lambda i: (i, 0)),
            pl.BlockSpec((row_total, block), lambda i: (0, i)),
        ],
        out_shape=[
            jax.ShapeDtypeStruct((4 * width, block), BF),
            jax.ShapeDtypeStruct((row_total, feature), BF),
        ],
        compiler_params=LIMIT,
        cost_estimate=cost(flops, flops // 500),
    )(left, *pieces)


def attn_kernel(h_ref, d_ref, g_ref, y_ref, *refs):
    out, z_ref = refs[8:]
    join(refs[:8], z_ref)
    total, width = d_ref.shape[1], y_ref.shape[1]
    normed = h_ref[...]
    out[:, :total] = dot(normed, d_ref[...], TN).astype(BF)
    out[:, total : total + width] = dot(normed, g_ref[...], TN).astype(BF)
    out[:, total + width :] = dot(y_ref[...], z_ref[...], TN).astype(BF)


def attn_products(first_normed, grad_first, grad_gate, pieces, gated):
    row_total, feature = first_normed.shape
    total, width = grad_first.shape[1], gated.shape[1]
    block = feature // 4

    def column(rows):
        return pl.BlockSpec((rows, block), lambda i: (0, i))

    def whole(columns):
        return pl.BlockSpec((row_total, columns), lambda i: (0, 0))

    return pl.pallas_call(
        attn_kernel,
        grid=(4,),
        in_specs=[column(row_total), whole(total), whole(width), whole(width)]
        + [column(p.shape[0]) for p in pieces],
        out_specs=pl.BlockSpec((block, total + 2 * width), lambda i: (i, 0)),
        out_shape=jax.ShapeDtypeStruct((feature, total + 2 * width), BF),
        scratch_shapes=[pltpu.VMEM((row_total, block), BF)],
        compiler_params=LIMIT,
        cost_estimate=cost(2 * row_total * feature * (total + 2 * width), 16 * 2**20),
    )(first_normed, grad_first, grad_gate, gated, *pieces)


def place_kernel(at, *refs):
    ins, outs = refs[:4], refs[4:]
    width, half = ins[0].shape[1], outs[0].shape[0]
    for k in range(4):
        columns = pl.ds(pl.multiple_of((at[0] ^ k) * width, LANES), width)
        for n, out in enumerate(outs):
            out[:, columns] = ins[k][n * half : (n + 1) * half, :]


def placed(pieces, start):
    rows, width = pieces[0].shape
    return pl.pallas_call(
        place_kernel,
        grid_spec=pltpu.PrefetchScalarGridSpec(
            num_scalar_prefetch=1,
            grid=(1,),
            in_specs=[pl.BlockSpec((rows, width), lambda i, at: (0, 0))] * 4,
            out_specs=[pl.BlockSpec((rows // 2, 4 * width), lambda i, at: (0, 0))] * 2,
        ),
        out_shape=[jax.ShapeDtypeStruct((rows // 2, 4 * width), BF)] * 2,
        compiler_params=ALONE,
        cost_estimate=cost(1, 4 * 2**20),
    )(start.astype(jnp.int32)[None], *pieces)


def reorder_kernel(at, *refs):
    count = len(refs) // 4 - 1
    width = refs[0].shape[1]
    for k in range(4):
        for n in range(4):

            @pl.when((at[0] ^ k) == n)
            def copy(k=k, n=n):
                for m in range(count):
                    refs[4 * count + k][:, m * width : (m + 1) * width] = refs[4 * m + n][...]


def reordered(sets, start):
    rows, width = sets[0][0].shape
    total = width * len(sets)
    return pl.pallas_call(
        reorder_kernel,
        grid_spec=pltpu.PrefetchScalarGridSpec(
            num_scalar_prefetch=1,
            grid=(1,),
            in_specs=[pl.BlockSpec((rows, width), lambda i, at: (0, 0))] * (4 * len(sets)),
            out_specs=[pl.BlockSpec((rows, total), lambda i, at: (0, 0))] * 4,
        ),
        out_shape=[jax.ShapeDtypeStruct((rows, total), BF)] * 4,
        compiler_params=ALONE,
        cost_estimate=cost(1, 4 * 2**20),
    )(start.astype(jnp.int32)[None], *[p for pieces in sets for p in pieces])


def half_sums(parts):
    a0, a1, a2, b0, b1, b2 = (p[...].astype(F32) for p in parts)
    return jnp.concatenate([a0 + a1 + a2, b0 + b1 + b2], axis=1)


def mean_scale(rows):
    return lax.rsqrt(jnp.mean(rows * rows, axis=1, keepdims=True) + EPSILON)


def norm_backward(grad, rows, gain):
    scale = mean_scale(rows)
    normed = rows * scale
    grad_normed = grad * gain
    inner = jnp.mean(grad_normed * normed, axis=1, keepdims=True)
    return scale * (grad_normed - normed * inner)


def put_halves(value, top, low):
    step = pl.program_id(0)

    @pl.when(step == 0)
    def first():
        top[...] = value

    @pl.when(step == 1)
    def second():
        low[...] = value


def put_quarters(lane, value, outs, held):
    held[...] = value
    width = outs[0].shape[1]
    for k, out in enumerate(outs):
        out[...] = held[:, pl.ds(pl.multiple_of((lane ^ k) * width, LANES), width)]


def either(top, low):
    return jnp.where(pl.program_id(0) == 0, top[...].astype(F32), low[...].astype(F32))


def up_norm_kernel(where, x_top, x_low, gain_ref, *refs):
    second = either(x_top, x_low) + half_sums(refs[:6])
    refs[6][...] = second
    put_halves((second * mean_scale(second) * gain_ref[1:2, :]).astype(BF), refs[7], refs[8])


def down_norm_kernel(where, second_ref, grad_top, grad_low, gain_ref, *refs):
    grad = either(grad_top, grad_low) + norm_backward(
        half_sums(refs[:6]), second_ref[...], gain_ref[1:2, :]
    )
    refs[6][...] = grad
    put_halves(grad.astype(BF), refs[7], refs[8])


def result_kernel(where, second_ref, own_ref, one, two, three, *refs):
    result = second_ref[...] + own_ref[...]
    for part in (one, two, three):
        result += part[...].astype(F32)
    put_quarters(where[2], result.astype(BF), refs[:4], refs[4])


def input_norm_kernel(where, x_top, x_low, grad_ref, gain_ref, *refs):
    grad = grad_ref[...] + norm_backward(
        half_sums(refs[:6]), either(x_top, x_low), gain_ref[0:1, :]
    )
    put_quarters(where[2], grad.astype(BF), refs[6:10], refs[10])


def on_rows(kernel, where, rows, gains, parts, quarters):
    feature = 2 * parts[0].shape[1] if parts else rows[0].shape[1]
    row_total = rows[-1].shape[0] if not parts else parts[0].shape[0]
    block = row_total // 2

    def spec(width):
        return pl.BlockSpec((block, width), lambda i, *_: (i, 0))

    top = low = pl.BlockSpec((block, feature), lambda i, *_: (0, 0))
    ins, args = [], []
    for r in rows:
        if isinstance(r, (list, tuple)):
            ins += [top, low]
            args += list(r)
        else:
            ins.append(spec(feature))
            args.append(r)
    if gains is not None:
        ins.append(pl.BlockSpec(gains.shape, lambda i, *_: (0, 0)))
    ins += [spec(feature // 2)] * len(parts)
    if quarters:
        outs = [spec(feature // 4)] * 4
        shapes = [jax.ShapeDtypeStruct((row_total, feature // 4), BF)] * 4
        scratch = [pltpu.VMEM((block, feature), BF)]
    else:
        outs = [spec(feature), top, low]
        shapes = [jax.ShapeDtypeStruct((row_total, feature), F32)]
        shapes += [jax.ShapeDtypeStruct((block, feature), BF)] * 2
        scratch = []
    return pl.pallas_call(
        kernel,
        grid_spec=pltpu.PrefetchScalarGridSpec(
            num_scalar_prefetch=1,
            grid=(2,),
            in_specs=ins,
            out_specs=outs,
            scratch_shapes=scratch,
        ),
        out_shape=shapes,
        compiler_params=ALONE,
        cost_estimate=cost(1, 6 * 2**20),
    )(where, *args, *([] if gains is None else [gains]), *parts)


def first_kernel(heads, pieces, w_ref, v_ref, wf_ref, b_ref, h_ref, qkv_ref, keep_ref, slope_ref, gain_ref):
    step = pl.program_id(0)

    @pl.when(step == 0)
    def norm():
        turned = wf_ref[...].astype(F32).T
        for n in range(2):
            first = heads + 3 * n
            gain_ref[n : n + 1, :] = (
                turned[first : first + 1] + turned[first + 1 : first + 2] + turned[first + 2 : first + 3]
            )
        block = pieces[0].shape[0]
        for at, piece in enumerate(pieces):
            x = piece[...].astype(F32)
            h_ref[pl.ds(at * block, block), :] = (x * mean_scale(x) * gain_ref[0:1, :]).astype(BF)

    @pl.when(step < 3)
    def query_key():
        qkv_ref[...] = dot(h_ref[...], w_ref[...]).astype(BF)

    @pl.when(step >= 3)
    def value_forget():
        pre = dot(h_ref[...], v_ref[...])
        qkv_ref[...] = pre.astype(BF)

        @pl.when(step == 4)
        def forget():
            real = lanes_of(pre.shape[0]) < heads
            forget_pre = jnp.where(real, pre[:, LANES:] + b_ref[...], 0.0)
            less = jnp.exp(-jnp.abs(forget_pre))
            keep_ref[...] = jnp.minimum(forget_pre, 0.0) - jnp.log1p(less)
            slope_ref[...] = jnp.where(
                real, jnp.where(forget_pre >= 0, less, 1.0) / (1.0 + less), 0.0
            )


def first_products(heads, pieces, weights, bias):
    row_total, feature = 8 * pieces[0].shape[0], pieces[0].shape[1]
    block = 256

    def whole_block(shape):
        return pl.BlockSpec(shape, lambda i: (0, 0))

    def kernel(*refs):
        first_kernel(heads, refs[:8], *refs[8:])

    return pl.pallas_call(
        kernel,
        grid=(5,),
        in_specs=[whole_block(p.shape) for p in pieces]
        + [
            pl.BlockSpec((feature, block), lambda i: (0, jnp.minimum(i, 2))),
            pl.BlockSpec((feature, block), lambda i: (0, jnp.maximum(i - 3, 0))),
            pl.BlockSpec((feature, LANES), lambda i: (0, 3)),
            whole_block((1, LANES)),
        ],
        out_specs=[
            whole_block((row_total, feature)),
            pl.BlockSpec((row_total, block), lambda i: (0, i)),
            whole_block((row_total, LANES)),
            whole_block((row_total, LANES)),
            whole_block((8, feature)),
        ],
        out_shape=[
            jax.ShapeDtypeStruct((row_total, feature), BF),
            jax.ShapeDtypeStruct((row_total, 5 * block), BF),
            jax.ShapeDtypeStruct((row_total, LANES), F32),
            jax.ShapeDtypeStruct((row_total, LANES), F32),
            jax.ShapeDtypeStruct((8, feature), F32),
        ],
        compiler_params=ALONE,
        cost_estimate=cost(10 * row_total * feature * block, 12 * 2**20),
    )(*pieces, weights[0], weights[1], weights[1], bias)


def gate_kernel(h_ref, w_ref, att_ref, gate_ref, y_ref):
    gate = jax.nn.sigmoid(dot(h_ref[...], w_ref[...]))
    gate_ref[...] = gate
    y_ref[...] = (att_ref[...] * gate).astype(BF)


def gate_products(first_normed, weights, attended):
    row_total, feature = first_normed.shape
    width = attended.shape[1]

    def by_rows(columns):
        return pl.BlockSpec((row_total // 4, columns), lambda i: (i, 0))

    return pl.pallas_call(
        gate_kernel,
        grid=(4,),
        in_specs=[
            by_rows(feature),
            pl.BlockSpec((feature, width), lambda i: (0, 0)),
            by_rows(width),
        ],
        out_specs=[by_rows(width)] * 2,
        out_shape=[
            jax.ShapeDtypeStruct((row_total, width), F32),
            jax.ShapeDtypeStruct((row_total, width), BF),
        ],
        compiler_params=LIMIT,
        cost_estimate=cost(2 * row_total * feature * width, 10 * 2**20),
    )(first_normed, weights, attended)


def join(pieces, whole):
    block = pieces[0].shape[0]
    for at, piece in enumerate(pieces):
        whole[pl.ds(at * block, block), :] = piece[...]


def up_kernel(*refs):
    pieces, g_ref, u_ref = refs[:4], refs[4], refs[5]
    h_ref, m_ref, to_gate_ref, to_up_ref = refs[-4:]

    @pl.when(pl.program_id(0) == 0)
    def first():
        join(pieces, h_ref)

    gate = dot(h_ref[...], g_ref[...])
    up = dot(h_ref[...], u_ref[...])
    sig = jax.nn.sigmoid(gate)
    silu = gate * sig
    m_ref[...] = (silu * up).astype(BF)
    to_gate_ref[...] = (up * sig * (1.0 + gate * (1.0 - sig))).astype(to_gate_ref.dtype)
    to_up_ref[...] = silu.astype(to_up_ref.dtype)


def up_products(half, held, pieces, weights):
    rows, feature = 4 * pieces[0].shape[0], pieces[0].shape[1]
    hidden, block = weights.shape[1] // 2, 256
    steps = hidden // block
    return pl.pallas_call(
        up_kernel,
        grid=(steps,),
        in_specs=[pl.BlockSpec(p.shape, lambda i: (0, 0)) for p in pieces]
        + [
            pl.BlockSpec((feature, block), lambda i: (0, i)),
            pl.BlockSpec((feature, block), lambda i: (0, steps + i)),
        ]
        + [pl.BlockSpec(memory_space=pl.ANY)] * len(held),
        out_specs=[pl.BlockSpec((rows, feature), lambda i: (half, 0))]
        + [pl.BlockSpec((rows, block), lambda i: (half, i))] * 3,
        out_shape=[jax.ShapeDtypeStruct((2 * rows, feature), BF)]
        + [jax.ShapeDtypeStruct((2 * rows, hidden), BF)] * 3,
        input_output_aliases={6 + n: n for n in range(len(held))},
        compiler_params=ALONE,
        cost_estimate=cost(4 * rows * feature * hidden, 16 * 2**20),
    )(*pieces, weights, weights, *held)


def down_kernel(g_ref, w_ref, to_gate_ref, to_up_ref, out_ref):
    grad = dot(g_ref[...], w_ref[...])
    out_ref[0] = (grad * to_gate_ref[...]).astype(BF)
    out_ref[1] = (grad * to_up_ref[...]).astype(BF)


def down_products(grad_out, weights, to_gate, to_up):
    row_total, feature = grad_out.shape
    hidden, block = weights.shape[1], 256
    column = pl.BlockSpec((row_total, block), lambda i: (0, i))
    return pl.pallas_call(
        down_kernel,
        grid=(hidden // block,),
        in_specs=[
            pl.BlockSpec((row_total, feature), lambda i: (0, 0)),
            pl.BlockSpec((feature, block), lambda i: (0, i)),
            column,
            column,
        ],
        out_specs=pl.BlockSpec((2, row_total, block), lambda i: (0, 0, i)),
        out_shape=jax.ShapeDtypeStruct((2, row_total, hidden), BF),
        compiler_params=LIMIT,
        cost_estimate=cost(2 * row_total * feature * hidden, 16 * 2**20),
    )(grad_out, weights, to_gate, to_up)


def back_kernel(*refs):
    pieces, (w_ref, gate_ref, att_ref, datt_ref, dgate_ref, z_ref) = refs[:8], refs[8:]
    block = pieces[0].shape[0]
    for at in range(4):

        @pl.when(pl.program_id(0) == at)
        def put(at=at):
            z_ref[:block, :] = pieces[2 * at][...]
            z_ref[block:, :] = pieces[2 * at + 1][...]

    grad = dot(z_ref[...], w_ref[...])
    gate = gate_ref[...]
    datt_ref[...] = (grad * gate).astype(BF)
    dgate_ref[...] = (grad * att_ref[...] * gate * (1.0 - gate)).astype(BF)


def back_products(pieces, weights, gate, attended):
    row_total, feature = 8 * pieces[0].shape[0], pieces[0].shape[1]
    width = attended.shape[1]

    def spec(shape, at=0):
        return pl.BlockSpec(shape, lambda i: (0, at))

    def by_rows(columns):
        return pl.BlockSpec((row_total // 4, columns), lambda i: (i, 0))

    return pl.pallas_call(
        back_kernel,
        grid=(4,),
        in_specs=[spec(p.shape) for p in pieces]
        + [spec((feature, width), 1), by_rows(width), by_rows(width)],
        out_specs=[by_rows(width)] * 2,
        out_shape=[jax.ShapeDtypeStruct((row_total, width), BF)] * 2,
        scratch_shapes=[pltpu.VMEM((row_total // 4, feature), BF)],
        compiler_params=ALONE,
        cost_estimate=cost(2 * row_total * feature * width, 10 * 2**20),
    )(*pieces, weights, gate, attended)


def slot_tables(lengths, dealing, stream):
    width = lengths.shape[1]
    given, slot_of = [], []
    start = jnp.int32(0)
    for g in range(width):
        given.append(start)
        start = start + lengths[stream, g]
        slot_of.append(dealing[stream, g])
    dealt, given_at = [], []
    start = jnp.int32(0)
    for k in range(width):
        dealt.append(start)
        here = jnp.int32(0)
        for g in range(width):
            here = jnp.where(slot_of[g] == k, given[g], here)
            start = start + jnp.where(slot_of[g] == k, lengths[stream, g], 0)
        given_at.append(here)
    return given, slot_of, dealt, given_at


def pick_kernel(backward, where, lengths, dealing, *refs):
    column, row = where[0], where[1]
    block = refs[0].shape[0] // (1 if backward else 4)
    row_total = 4 * block
    step = pl.program_id(0)
    given, slot_of, dealt, given_at = slot_tables(lengths, dealing, column)
    within = lax.broadcasted_iota(jnp.int32, (block, 1), 0)
    if backward:
        places = row * row_total + step * block + within
        moves = []
        for g in range(len(given)):
            there = jnp.int32(0)
            for k in range(len(given)):
                there = jnp.where(slot_of[g] == k, dealt[k], there)
            moves.append((given[g], there - given[g]))
    else:
        places = row * row_total + (step ^ column) * block + within
        moves = [(s, g - s) for s, g in zip(dealt, given_at)]
    move = jnp.zeros_like(places) + moves[0][1]
    for first, by in moves[1:]:
        move = jnp.where(places >= first, by, move)
    near = places + move - row * row_total
    near = jnp.where(near < 0, near + 2 * row_total, near)
    if backward:
        other = jnp.where(near >= row_total, row_total, 0)
        local = near - other
        part = sum(jnp.where(local >= k * block, 1, 0) for k in (1, 2, 3))
        near = other + local + (jnp.bitwise_xor(part, column) - part) * block
    across = lax.broadcasted_iota(jnp.int32, (block, 2 * row_total), 1)
    chosen = jnp.where(across == near, 1.0, 0.0).astype(BF)
    if backward:
        picked = 0.0
        for k in range(8):
            picked += dot(chosen[:, k * block : (k + 1) * block], refs[k][...])
        refs[8][...] = picked.astype(BF)
        return
    for at in range(2):
        own, other = refs[2 * at][...], refs[2 * at + 1][...]
        picked = dot(chosen[:, :row_total], own) + dot(chosen[:, row_total:], other)
        picked = picked.astype(BF)
        for k in range(4):

            @pl.when(step == k)
            def put(k=k, at=at, picked=picked):
                refs[4 + 4 * at + k][...] = picked


def moved_rows(backward, where, lengths, dealing, arrays):
    if backward:
        block, width = arrays[0].shape
        row_total = 4 * block
    else:
        row_total, width = arrays[0].shape
        block = row_total // 4
    if lax.axis_size("dp") != 2:
        column, row = where[0], where[1]
        local = jnp.arange(row_total, dtype=jnp.int32)
        own_lengths = lax.dynamic_index_in_dim(lengths, column, 0, keepdims=False)
        own_dealing = lax.dynamic_index_in_dim(dealing, column, 0, keepdims=False)
        if backward:
            to = given_targets(own_lengths, own_dealing, row * row_total + local)
            at = to % row_total
            to = to - at + ((at // block) ^ column) * block + at % block
            arrays = [jnp.concatenate(arrays, axis=0)]
        else:
            swapped = (((local // block) ^ column) * block) + local % block
            to = dealt_sources(own_lengths, own_dealing, row * row_total + swapped)
        moved = [jnp.take(lax.all_gather(a, "dp", axis=0, tiled=True), to, axis=0) for a in arrays]
        if backward:
            return moved
        return [m[k * block : (k + 1) * block] for m in moved for k in range(4)]
    others = [swap(a, "dp", 1) for a in arrays]
    if backward:
        outs = [pl.BlockSpec((block, width), lambda i, *_: (i, 0))]
        shapes = [jax.ShapeDtypeStruct((row_total, width), BF)]
        ins = [*arrays, *others]
    else:
        outs = [pl.BlockSpec((block, width), lambda i, *_: (0, 0))] * 8
        shapes = [jax.ShapeDtypeStruct((block, width), BF)] * 8
        ins = [arrays[0], others[0], arrays[1], others[1]]
    return pl.pallas_call(
        lambda *refs: pick_kernel(backward, *refs),
        grid_spec=pltpu.PrefetchScalarGridSpec(
            num_scalar_prefetch=3,
            grid=(4,),
            in_specs=[pl.BlockSpec(a.shape, lambda i, *_: (0, 0)) for a in ins],
            out_specs=outs,
        ),
        out_shape=shapes,
        compiler_params=pltpu.CompilerParams(vmem_limit_bytes=40 * 2**20),
        cost_estimate=cost(16 * row_total * row_total * width, 8 * 2**20),
    )(where, lengths, dealing, *ins)


def piece_rows(piece, half):
    rows = []
    for places in (UPPER, LOWER):
        place = jnp.int32(places[0])
        for k in (1, 2, 3):
            place = jnp.where(piece == k, places[k], place)
        rows.append(pl.ds(pl.multiple_of(place * half, half), half))
    return rows


def get_rows(ref, rows):
    return jnp.concatenate([ref[part, :] for part in rows], axis=0)


def put_rows(ref, rows, columns, value):
    half = value.shape[0] // 2
    for n, part in enumerate(rows):
        ref[part, columns] = value[n * half : (n + 1) * half]


def lanes_of(rows):
    return lax.broadcasted_iota(jnp.int32, (rows, LANES), 1)


def split_column(column):
    one = column.astype(BF).astype(F32)
    two = (column - one).astype(BF).astype(F32)
    return one, two, column - one - two


def fill(lanes, base, columns, rest):
    for at, column in reversed(list(enumerate(columns))):
        rest = jnp.where(lanes == base + at, column, rest)
    return rest


def forward_kernel(
    where,
    lengths,
    dealing,
    q_ref,
    k_ref,
    v_ref,
    keep_ref,
    att_ref,
    qa_ref,
    ka_ref,
    c_ref,
    va_ref,
):
    pair = pl.program_id(0)
    column, row, lane = where[0], where[1], where[2]
    first_length = jnp.int32(0)
    for g in range(lengths.shape[1]):
        first_length += jnp.where(dealing[lane, g] == 2 * row, lengths[lane, g], 0)
    row_total = q_ref.shape[0]
    block = row_total // 4
    lanes = lanes_of(block)

    def rows_of(at):
        return piece_rows(column ^ at, block // 2)

    @pl.when(pair == 0)
    def sum_keeps():
        below = lax.broadcasted_iota(jnp.int32, (block, block), 0)
        across = lax.broadcasted_iota(jnp.int32, (block, block), 1)
        ones = jnp.where(below >= across, 1.0, 0.0)
        running = jnp.zeros((1, LANES), F32)
        for at in range(4):
            sums = running + lax.dot_general(
                ones,
                get_rows(keep_ref, rows_of(at)),
                (((1,), (0,)), ((), ())),
                precision=lax.Precision.HIGHEST,
                preferred_element_type=F32,
            )
            c_ref[pl.ds(at * block, block), :] = sums
            running = sums[block - 1 :, :]

    for head in range(2):
        mine = (lanes < 64) if head == 0 else (lanes >= 64)
        base = 64 if head == 0 else 0
        for at in range(4):
            rows, own = rows_of(at), pl.ds(at * block, block)
            decay = jnp.sum(
                jnp.where(lanes == 2 * pair + head, c_ref[own, :], 0.0), axis=1, keepdims=True
            )
            one, two, three = split_column(decay)
            places = at * block + lax.broadcasted_iota(jnp.int32, (block, 1), 0)
            second = jnp.where(places >= first_length, 1.0, 0.0)
            q_side = fill(lanes, base, (1.0, 1.0, 1.0, second), 0.0)
            k_side = fill(
                lanes, base, (-one, -two, -three, (second - 1.0) * FAR, 1.0, 1.0, 1.0), 0.0
            )
            qa_ref[head, own, :] = jnp.where(
                mine, get_rows(q_ref, rows).astype(F32) * 0.125, q_side
            ).astype(BF)
            ka_ref[head, own, :] = jnp.where(mine, get_rows(k_ref, rows).astype(F32), k_side).astype(BF)
            va_ref[head, own, :] = jnp.where(mine, get_rows(v_ref, rows).astype(F32), 1.0).astype(BF)

    below = lax.broadcasted_iota(jnp.int32, (block, block), 0)
    across = lax.broadcasted_iota(jnp.int32, (block, block), 1)
    for at in range(4):
        own = pl.ds(at * block, block)
        width = (at + 1) * block
        results = []
        for head in range(2):
            base = 64 if head == 0 else 0
            queries = qa_ref[head, own, :]
            last = jnp.where(
                below >= across, dot(queries, ka_ref[head, at * block : width, :], NT), -FAR
            )
            top = jnp.max(last, axis=1, keepdims=True)
            if at > 0:
                early = dot(queries, ka_ref[head, : at * block, :], NT)
                top = jnp.maximum(top, jnp.max(early, axis=1, keepdims=True))
            total = dot(jnp.exp(last - top).astype(BF), va_ref[head, at * block : width, :])
            if at > 0:
                total += dot(jnp.exp(early - top).astype(BF), va_ref[head, : at * block, :])
            weight = pltpu.roll(total, 64, 1)
            results.append(total / weight)
            log_total = top + jnp.log(total[:, base : base + 1])
            one, two, three = split_column(log_total)
            qa_ref[head, own, :] = fill(
                lanes, base + 4, (-one, -two, -three), queries.astype(F32)
            ).astype(BF)
        attended = jnp.where(lanes < 64, results[0], results[1])
        put_rows(att_ref, rows_of(at), slice(None), attended)


def attend_forward(where, lengths, dealing, qkv, keep):
    row_total, width = qkv.shape[0], qkv.shape[1] // LANES // 3 * LANES
    pairs = width // LANES
    heads = 2 * pairs

    def columns(first):
        return pl.BlockSpec((row_total, LANES), lambda p, *_: (0, first + p))

    sided = pl.BlockSpec((2, row_total, LANES), lambda p, *_: (p, 0, 0))
    return pl.pallas_call(
        forward_kernel,
        grid_spec=pltpu.PrefetchScalarGridSpec(
            num_scalar_prefetch=3,
            grid=(pairs,),
            in_specs=[
                columns(0),
                columns(pairs),
                columns(2 * pairs),
                pl.BlockSpec((row_total, LANES), lambda p, *_: (0, 0)),
            ],
            out_specs=[columns(0), sided, sided],
            scratch_shapes=[
                pltpu.VMEM((row_total, LANES), F32),
                pltpu.VMEM((2, row_total, LANES), BF),
            ],
        ),
        out_shape=[
            jax.ShapeDtypeStruct((row_total, width), F32),
            jax.ShapeDtypeStruct((heads, row_total, LANES), BF),
            jax.ShapeDtypeStruct((heads, row_total, LANES), BF),
        ],
        compiler_params=pltpu.CompilerParams(vmem_limit_bytes=60 * 2**20),
        cost_estimate=cost(10 * 10**9, 8 * 2**20),
    )(where, lengths, dealing, qkv, qkv, qkv, keep)


def backward_kernel(
    where,
    qa_ref,
    ka_ref,
    v_ref,
    datt_ref,
    att_ref,
    slope_ref,
    out_ref,
    va_ref,
    da_ref,
    kt_ref,
    dk_ref,
    dv_ref,
    dq_ref,
    dc_ref,
):
    pair = pl.program_id(0)
    pairs = pl.num_programs(0)
    column = where[0]
    row_total = v_ref.shape[0]
    block = row_total // 4
    lanes = lanes_of(block)
    width = att_ref.shape[1] * pairs

    def rows_of(at):
        return piece_rows(column ^ at, block // 2)

    def lanes_at(group):
        return pl.ds(pl.multiple_of((group * pairs + pair) * LANES, LANES), LANES)

    @pl.when(pair == 0)
    def clear():
        dc_ref[...] = jnp.zeros_like(dc_ref)

    for at in range(4):
        rows, own = rows_of(at), pl.ds(at * block, block)
        grad_att = get_rows(datt_ref, rows).astype(F32)
        inner = grad_att * get_rows(att_ref, rows)
        values = get_rows(v_ref, rows).astype(F32)
        for head in range(2):
            mine = (lanes < 64) if head == 0 else (lanes >= 64)
            base = 64 if head == 0 else 0
            delta = jnp.sum(jnp.where(mine, inner, 0.0), axis=1, keepdims=True)
            one, two, three = split_column(delta)
            da_ref[head, own, :] = jnp.where(
                mine, grad_att, fill(lanes, base, (-one, -two, -three), 0.0)
            ).astype(BF)
            va_ref[head, own, :] = jnp.where(
                mine, values, fill(lanes, base, (1.0, 1.0, 1.0), 0.0)
            ).astype(BF)

    below = lax.broadcasted_iota(jnp.int32, (block, block), 0)
    across = lax.broadcasted_iota(jnp.int32, (block, block), 1)
    for head in range(2):
        for at in range(4):
            own = pl.ds(at * block, block)
            kt_ref[:, own] = ka_ref[head, own, :].astype(F32).T.astype(BF)
        for at in range(4):
            own = pl.ds(at * block, block)
            queries, grads = qa_ref[head, own, :], da_ref[head, own, :]
            dq_t = jnp.zeros((LANES, block), F32)
            for past in range(at + 1):
                keys = pl.ds(past * block, block)
                probs = jnp.exp(dot(ka_ref[head, keys, :], queries, NT))
                if past == at:
                    probs = jnp.where(below <= across, probs, 0.0)
                grad_scores = (probs * dot(va_ref[head, keys, :], grads, NT)).astype(BF)
                dv = dot(probs.astype(BF), grads)
                dk = dot(grad_scores, queries)
                dq_t += dot(kt_ref[:, keys], grad_scores)
                if past == at:
                    dv_ref[head, keys, :] = dv
                    dk_ref[head, keys, :] = dk
                else:
                    dv_ref[head, keys, :] += dv
                    dk_ref[head, keys, :] += dk
            dq_ref[head, own, :] = dq_t.T

    for at in range(4):
        rows, own = rows_of(at), pl.ds(at * block, block)
        for head in range(2):
            base = 64 if head == 0 else 0
            change = (
                dq_ref[head, own, base + 4 : base + 5] - dk_ref[head, own, base : base + 1]
            )
            dc_ref[own, :] += jnp.where(lanes == 2 * pair + head, change, 0.0)
        left = lanes < 64
        for group, ref, scale in ((0, dq_ref, 0.125), (1, dk_ref, 1.0), (2, dv_ref, 1.0)):
            both = jnp.where(left, ref[0, own, :], ref[1, own, :])
            put_rows(out_ref, rows, lanes_at(group), (both * scale).astype(BF))

    @pl.when(pair == pairs - 1)
    def finish():
        ones = jnp.where(below <= across, 1.0, 0.0)
        running = jnp.zeros((1, LANES), F32)
        for at in reversed(range(4)):
            sums = running + lax.dot_general(
                ones,
                dc_ref[pl.ds(at * block, block), :],
                (((1,), (0,)), ((), ())),
                precision=lax.Precision.HIGHEST,
                preferred_element_type=F32,
            )
            running = sums[:1, :]
            rows = rows_of(at)
            put_rows(
                out_ref,
                rows,
                slice(3 * width, None),
                (sums * get_rows(slope_ref, rows)).astype(BF),
            )


def attend_backward(where, qa, ka, qkv, grad_att, attended, slope):
    row_total, width = attended.shape
    pairs = width // LANES
    heads = 2 * pairs
    total = 3 * width + LANES

    def columns(first):
        return pl.BlockSpec((row_total, LANES), lambda p, *_: (0, first + p))

    sided = pl.BlockSpec((2, row_total, LANES), lambda p, *_: (p, 0, 0))
    both = (2, row_total, LANES)
    return pl.pallas_call(
        backward_kernel,
        grid_spec=pltpu.PrefetchScalarGridSpec(
            num_scalar_prefetch=1,
            grid=(pairs,),
            in_specs=[
                sided,
                sided,
                columns(2 * pairs),
                columns(0),
                columns(0),
                pl.BlockSpec((row_total, LANES), lambda p, *_: (0, 0)),
            ],
            out_specs=pl.BlockSpec((row_total, total), lambda p, *_: (0, 0)),
            scratch_shapes=[
                pltpu.VMEM(both, BF),
                pltpu.VMEM(both, BF),
                pltpu.VMEM((LANES, row_total), BF),
                pltpu.VMEM(both, F32),
                pltpu.VMEM(both, F32),
                pltpu.VMEM(both, F32),
                pltpu.VMEM((row_total, LANES), F32),
            ],
        ),
        out_shape=jax.ShapeDtypeStruct((row_total, total), BF),
        compiler_params=pltpu.CompilerParams(vmem_limit_bytes=60 * 2**20),
        cost_estimate=cost(12 * 10**9, 8 * 2**20),
    )(where, qa, ka, qkv, grad_att, attended, slope)


def on_device(
    x_given,
    cotangent,
    seq_lengths,
    seq_deal,
    attn_gain,
    w_query,
    w_key,
    w_value,
    w_ogate,
    w_forget,
    b_forget,
    w_out,
    mlp_gain,
    w_gate,
    w_up,
    w_down,
):
    quarter = x_given.shape[1]
    piece = quarter // 4
    row, column, lane = lax.axis_index("dp"), lax.axis_index("tx"), lax.axis_index("ty")
    heads = w_forget.shape[1]
    width = w_query.shape[1]
    hidden = w_gate.shape[1]
    share = w_query.shape[0] // lax.axis_size("dp")

    def own_share(weights):
        return lax.dynamic_slice_in_dim(weights, row * share, share, axis=0)

    def whole(weights):
        return lax.all_gather(weights, ("ty", "dp"), axis=0, tiled=True)

    gains = jnp.stack(three_parts(attn_gain) + three_parts(mlp_gain), axis=1).astype(BF)
    spare = jnp.zeros((w_query.shape[0], LANES - heads - 6), BF)
    side = 3 * width
    last = side + LANES
    def side_by_side(*weights):
        return jnp.concatenate([own_share(w) for w in weights], axis=1)

    w_first = [whole(side_by_side(w_query, w_key))]

    where = jnp.stack([column, row, lane]).astype(jnp.int32)
    paired = lax.axis_size("dp") == 2

    dealt = moved_rows(False, where, seq_lengths, seq_deal, (x_given[0], cotangent[0]))
    x_parts, grad_parts = tie(spread_plane(dealt[:4]), dealt[4:])
    x_parts, grad_parts = tie(
        spread_line(reordered([x_parts], column ^ lane)), spread_plane(grad_parts)
    )
    grad_parts, x_parts = tie(reordered([grad_parts], column ^ lane), x_parts)
    w_first.append(whole(side_by_side(w_value, w_forget, gains, spare)))
    later = [side_by_side(w_ogate, w_out.T), side_by_side(w_gate, w_up)]
    x_parts, later, w_first[0] = tie(x_parts, later, w_first[0])
    w_second, w_gate_up = [whole(w) for w in later]
    grad_parts = spread_line(grad_parts)
    x_full, unused = gather_rows(*placed(x_parts, lane), ahead=(grad_parts[1], w_first[1]))

    bias = jnp.pad(b_forget, (0, LANES - heads))[None]
    first_normed, qkv, keep, slope, gains = first_products(heads, x_full, w_first, bias)
    grad_parts, qkv = tie(grad_parts, qkv)
    top, low = placed(grad_parts, lane)
    grad_rows = [top, low]
    qkv, top, low = tie(qkv, top, low)
    top_x, low_y = swap(top, "tx", 1), swap(low, "tx", 2)
    low_x, top_y = swap(low, "tx", 1), swap(top, "tx", 2)
    attended, qa, ka = attend_forward(where, seq_lengths, seq_deal, qkv, keep)
    attended, top_x, low_y, low_x, top_y = tie(attended, top_x, low_y, low_x, top_y)
    top_d, low_d = swap(top_x, "tx", 2), swap(low_y, "tx", 1)
    grad_full = [top, low, top_x, low_y, low_x, top_y, top_d, low_d]
    w_down_t, attended = tie(own_share(w_down.T), attended)
    w_down_t = whole(w_down_t)
    out_gate, gated = gate_products(first_normed, w_second, attended)
    gated, grad_full[6:] = tie(gated, grad_full[6:])
    parts, unused = scatter_products([(gated, 0)], [(w_second, width, 1)])
    second, top, low = on_rows(up_norm_kernel, where, [x_full[:2]], gains, parts, False)

    def up_half(pieces, ahead):
        return up_products(0, [], pieces, w_gate_up)

    h2_parts, held = gather_rows(top, low, up_half)
    h2_full, mid, to_gate, to_up = up_products(1, held, h2_parts[4:], w_gate_up)
    part, grad_full = turned_products(mid, grad_full)
    part, grad_full = tie(part, grad_full)
    grads_down = summed(part)
    grad_gate_up = down_products(grad_full, w_down_t, to_gate, to_up)

    def gate_up_products(ready):
        left, unused = tie(h2_full, ready)
        return row_products(left, grad_gate_up)

    parts, part = scatter_products(
        [(grad_gate_up, 0), (grad_gate_up, 1)],
        [(w_gate_up, hidden, 0), (w_gate_up, hidden, 1)],
        gate_up_products,
    )
    part, parts = tie(part, parts)
    grads_gate_up = summed(part)
    grad_second, top, low = on_rows(
        down_norm_kernel, where, [second, grad_rows], gains, parts, False
    )

    def result_products(pieces, ahead):
        left, unused = tie(mid, pieces)
        return part_products(None, (1, 2, 3, 0), [(left, 0)], [(w_down_t, hidden, 0)])

    z_parts, (*sent, own) = gather_rows(top, low, result_products)

    sent = [swap(piece, "tx", k + 1) for k, piece in enumerate(sent)]
    grad_att, grad_ogate = back_products(z_parts, w_second, out_gate, attended)
    grad_first = attend_backward(where, qa, ka, qkv, grad_att, attended, slope)
    grad_first, sent, grads_down = tie(grad_first, sent, grads_down)
    output = on_rows(result_kernel, where, [second, own, *sent], None, [], True)
    output, grad_first = tie(output, grad_first)
    output = spread_line(output)
    part = attn_products(first_normed, grad_first, grad_ogate, z_parts, gated)
    part, grad_first, output = tie(part, grad_first, output)
    grads_attn = summed(part)

    def row_dots(*sides):
        return sum(jnp.sum(w.astype(F32) * g, axis=1) for w, g in sides)

    def finish(ready):
        down, gate_up, bias, unused = tie(
            grads_down, grads_gate_up, grad_first[:, side:], ready
        )
        bias = jnp.sum(bias.astype(F32), axis=0, keepdims=True)
        bias = bias + swap(bias, "dp", 1) if paired else lax.psum(bias, ("dp", "ty"))
        down, gate_up = reduce_end(down), reduce_end(gate_up)
        mlp = [gate_up[:, :hidden], gate_up[:, hidden:], down]
        return mlp, row_dots((w_gate, mlp[0]), (w_up, mlp[1])) / mlp_gain, bias

    parts, (grads_mlp, own_mlp_gain, bias_grad) = scatter_products(
        [(grad_first, 0), (grad_first, 3), (grad_first, 4), (grad_ogate, 0)],
        [(w_first[0], 2 * width, 0), (w_first[1], 256, 0), (w_first[1], 256, 1), (w_second, width, 0)],
        finish,
    )
    grad_x = on_rows(input_norm_kernel, where, [x_full[:2], grad_second], gains, parts, True)

    def given(pieces):
        return moved_rows(True, where, seq_lengths, seq_deal, pieces)[0]

    output, grad_x = tie(output, grad_x)
    grad_x = spread_line(grad_x)
    output = spread_plane(reordered([output], column ^ lane))
    if paired:
        bias_grad = pairs_sum(spread_line([bias_grad] * 4))
    output, grad_x[1] = tie(output, grad_x[1])
    output, grad_x, bias_grad = tie(given(output), grad_x, bias_grad)
    grad_x = spread_plane(reordered([grad_x], column ^ lane))

    grad_attn = reduce_end(grads_attn)
    grads = [
        grad_attn[:, :width],
        grad_attn[:, width : 2 * width],
        grad_attn[:, 2 * width : side],
        grad_attn[:, last : last + width],
        grad_attn[:, side : side + heads],
    ]
    own_gain = row_dots(*zip((w_query, w_key, w_value, w_ogate, w_forget), grads)) / attn_gain
    grad_gains = spread_plane([jnp.stack([own_gain, own_mlp_gain])] * 4)
    grad_x, output, grad_gains, grads = tie(grad_x, output, grad_gains, grads)
    grad_gains = pairs_sum(grad_gains)
    grad_input = given(grad_x)
    return (
        output[None],
        grad_input[None],
        grad_gains[0],
        *grads,
        bias_grad[0, :heads],
        grad_attn[:, last + width :],
        grad_gains[1],
        *grads_mlp,
    )


def solution(mesh):
    tokens, feature, grid, flipped = P("tx", "dp", "ty"), P("ty"), P("ty", "tx"), P("tx", "ty")
    return jax.shard_map(
        on_device,
        mesh=mesh,
        in_specs=(
            tokens,
            tokens,
            P(),
            P(),
            feature,
            grid,
            grid,
            grid,
            grid,
            grid,
            P("tx"),
            flipped,
            feature,
            grid,
            grid,
            flipped,
        ),
        out_specs=(
            tokens,
            tokens,
            feature,
            grid,
            grid,
            grid,
            grid,
            grid,
            P("tx"),
            flipped,
            feature,
            grid,
            grid,
            flipped,
        ),
        check_vma=False,
    )
```

```python
import jax
import jax.numpy as jnp
from jax import lax
from jax.experimental import pallas as pl
from jax.experimental.pallas import tpu as pltpu
from jax.sharding import PartitionSpec as P

EPSILON = 1e-06
FAR = 1e30
LANES = 128
BF = jnp.bfloat16
F32 = jnp.float32


def dot(left, right, dims=((1,), (0,))):
    return lax.dot_general(left, right, (dims, ((), ())), preferred_element_type=F32)


NT = ((1,), (1,))
TN = ((0,), (0,))


def three_parts(values):
    one = lax.reduce_precision(values, 8, 7)
    two = lax.reduce_precision(values - one, 8, 7)
    three = lax.reduce_precision(values - one - two, 8, 7)
    return one, two, three


def pick_small(lookup, indices):
    width = lookup.shape[0]
    matches = indices[:, None] == jnp.arange(width, dtype=jnp.int32)[None, :]
    return jnp.sum(jnp.where(matches, lookup[None, :], 0), axis=1)


def stream_tables(lengths, dealing):
    width = lengths.shape[0]
    numbers = jnp.arange(width, dtype=jnp.int32)
    given_start = jnp.cumsum(lengths) - lengths
    owners = jnp.sum(jnp.where(dealing[None, :] == numbers[:, None], numbers[None, :], 0), axis=1)
    dealt_length = pick_small(lengths, owners)
    dealt_start = jnp.cumsum(dealt_length) - dealt_length
    return (given_start, owners, dealt_start, dealt_length)


def dealt_sources(lengths, dealing, places):
    given_start, owners, dealt_start, unused = stream_tables(lengths, dealing)
    slot_ids = jnp.sum((dealt_start[None, :] <= places[:, None]).astype(jnp.int32), axis=1) - 1
    return (
        pick_small(given_start, pick_small(owners, slot_ids))
        + places
        - pick_small(dealt_start, slot_ids)
    )


def given_targets(lengths, dealing, places):
    given_start, unused, dealt_start, unused = stream_tables(lengths, dealing)
    member = jnp.sum((given_start[None, :] <= places[:, None]).astype(jnp.int32), axis=1) - 1
    return (
        pick_small(dealt_start, pick_small(dealing, member))
        + places
        - pick_small(given_start, member)
    )


def swap(values, axis, step):
    return lax.ppermute(values, axis, [(at, at ^ step) for at in range(lax.axis_size(axis))])


def spread_plane(pieces):
    return [pieces[0]] + [swap(pieces[k], "tx", k) for k in (1, 2, 3)]


def spread_line(pieces):
    return [pieces[0]] + [swap(pieces[k], "ty", k) for k in (1, 2, 3)]


def pairs_sum(parts):
    return (parts[0] + parts[1]) + (parts[2] + parts[3])


def tie(*groups):
    return lax.optimization_barrier(groups)


UPPER, LOWER = (0, 2, 5, 6), (1, 4, 3, 7)


def gather_rows(top, low, beside=None, ahead=None):
    top_x, low_y = swap(top, "tx", 1), swap(low, "tx", 2)
    low_x, top_y = swap(low, "tx", 1), swap(top, "tx", 2)
    top_x, low_y, ahead = tie(top_x, low_y, ahead)
    top_d, low_d = swap(top_x, "tx", 2), swap(low_y, "tx", 1)
    done = None if beside is None else beside([top, low, top_x, low_y], ahead)
    return [top, low, top_x, low_y, low_x, top_y, top_d, low_d], done


def scatter_products(lefts, weights, beside=None, ahead=None):
    a3, b3 = part_products((3,), [BF, BF], True, lefts, weights)
    arrays, a3, b3, ahead = tie([array for array, unused in lefts], a3, b3, ahead)
    lefts = [(array, place) for array, (unused, place) in zip(arrays, lefts)]
    a3, b3 = swap(a3, "tx", 1), swap(b3, "tx", 2)
    rest = part_products((1, 2, 0), [BF, F32, F32, F32, BF, F32], True, lefts, weights)
    a3, b3, (a1, a2, a0, b1, b2, b0) = tie(a3, b3, rest)
    a1, b2 = swap(a1, "tx", 1), swap(b2, "tx", 2)
    send_a2 = (a2 + a3.astype(F32)).astype(BF)
    send_b1 = (b1 + b3.astype(F32)).astype(BF)
    done = None if beside is None else beside((send_b1, ahead))
    a2, b1 = swap(send_a2, "tx", 2), swap(send_b1, "tx", 1)
    a1, a2, b1, b2, done = tie(a1, a2, b1, b2, done)
    return [a0, a1, a2, b0, b1, b2], done


def summed(part):
    return lax.psum_scatter(part, ("ty", "dp"), scatter_dimension=0, tiled=True)


def reduce_end(piece):
    if lax.axis_size("dp") != 2:
        return lax.all_gather(piece, "dp", axis=0, tiled=True).astype(F32)
    other = swap(piece, "dp", 1)
    lower = lax.axis_index("dp") == 0
    return jnp.concatenate(
        [jnp.where(lower, piece, other), jnp.where(lower, other, piece)], axis=0
    ).astype(F32)


def cost(flops, bytes_accessed):
    return pl.CostEstimate(flops=flops, bytes_accessed=bytes_accessed, transcendentals=0)


LIMIT = pltpu.CompilerParams(vmem_limit_bytes=50 * 2**20)
ALONE = pltpu.CompilerParams(vmem_limit_bytes=60 * 2**20)


def part_kernel(order, split, count, *refs):
    lefts, rights, outs = refs[:count], refs[count : 2 * count], refs[2 * count :]
    total = 0.0
    for left, right in zip(lefts, rights):
        rows = left[...]
        total += dot(rows.reshape(rows.shape[-2:]), right[...], NT)
    half = outs[0].shape[0] // 2
    low = min(min(UPPER[at], LOWER[at]) for at in order)

    def put(outs):
        for at, out in zip(order, outs):
            for n, place in enumerate((UPPER[at] - low, LOWER[at] - low)):
                out[n * half : (n + 1) * half, :] = total[
                    place * half : (place + 1) * half
                ].astype(out.dtype)

    if not split:
        put(outs)
        return
    step, steps = pl.program_id(0), pl.num_programs(0)

    @pl.when(step < steps // 2)
    def first():
        put(outs[: len(order)])

    @pl.when(step >= steps // 2)
    def second():
        put(outs[len(order) :])


def part_products(order, dtypes, split, lefts, weights):
    row_total, feature = lefts[0][0].shape[-2], weights[0][0].shape[0]
    piece, block = row_total // 4, 256
    steps = feature // block
    rows, first_rows = (piece, 3) if order == (3,) else (len(order) * piece, 0)
    left_specs, right_specs = [], []
    flops = 0
    for (array, place), (weight, width, at) in zip(lefts, weights):
        if array.ndim == 2:
            left_specs.append(pl.BlockSpec((rows, width), lambda i, place=place: (first_rows, place)))
        else:
            left_specs.append(
                pl.BlockSpec((1, rows, width), lambda i, place=place: (place, first_rows, 0))
            )
        right_specs.append(pl.BlockSpec((block, width), lambda i, at=at: (i, at)))
        flops += 2 * rows * feature * width
    if split:
        outs = [pl.BlockSpec((piece, block), lambda i: (0, jnp.minimum(i, steps // 2 - 1)))] * len(order)
        outs += [pl.BlockSpec((piece, block), lambda i: (0, jnp.maximum(i - steps // 2, 0)))] * len(order)
    else:
        outs = [pl.BlockSpec((piece, block), lambda i: (0, i))] * len(order)
    return pl.pallas_call(
        lambda *refs: part_kernel(order, split, len(lefts), *refs),
        grid=(steps,),
        in_specs=left_specs + right_specs,
        out_specs=outs,
        out_shape=[
            jax.ShapeDtypeStruct((piece, feature // 2 if split else feature), dtype)
            for dtype in dtypes
        ],
        compiler_params=LIMIT,
        cost_estimate=cost(flops, flops // 500),
    )(*[a for a, unused in lefts], *[w for w, *unused in weights])


def row_kernel(left, right, out):
    width = right.shape[2]
    for n in range(2):
        out[:, n * width : (n + 1) * width] = dot(left[...], right[n], TN).astype(BF)


def row_products(left, right):
    row_total, feature = left.shape
    width, block = right.shape[2], 256
    flops = 4 * row_total * feature * width
    return pl.pallas_call(
        row_kernel,
        grid=(feature // block,),
        in_specs=[
            pl.BlockSpec((row_total, block), lambda i: (0, i)),
            pl.BlockSpec(right.shape, lambda i: (0, 0, 0)),
        ],
        out_specs=pl.BlockSpec((block, 2 * width), lambda i: (i, 0)),
        out_shape=jax.ShapeDtypeStruct((feature, 2 * width), BF),
        compiler_params=LIMIT,
        cost_estimate=cost(flops, flops // 500),
    )(left, right)


def turned_kernel(left, *refs):
    out, right = refs[8:]
    join(refs[:8], right)
    out[...] = dot(left[...], right[...], TN).astype(BF)


def turned_products(left, pieces):
    row_total, feature = left.shape[0], pieces[0].shape[1]
    width, block = left.shape[1], feature // 4
    flops = 2 * row_total * feature * width
    return pl.pallas_call(
        turned_kernel,
        grid=(4,),
        in_specs=[pl.BlockSpec((row_total, width), lambda i: (0, 0))]
        + [pl.BlockSpec((p.shape[0], block), lambda i: (0, i)) for p in pieces],
        out_specs=[
            pl.BlockSpec((width, block), lambda i: (i, 0)),
            pl.BlockSpec((row_total, block), lambda i: (0, i)),
        ],
        out_shape=[
            jax.ShapeDtypeStruct((4 * width, block), BF),
            jax.ShapeDtypeStruct((row_total, feature), BF),
        ],
        compiler_params=LIMIT,
        cost_estimate=cost(flops, flops // 500),
    )(left, *pieces)


def attn_kernel(h_ref, d_ref, g_ref, y_ref, *refs):
    out, z_ref = refs[8:]
    join(refs[:8], z_ref)
    total, width = d_ref.shape[1], y_ref.shape[1]
    normed = h_ref[...]
    out[:, :total] = dot(normed, d_ref[...], TN).astype(BF)
    out[:, total : total + width] = dot(normed, g_ref[...], TN).astype(BF)
    out[:, total + width :] = dot(y_ref[...], z_ref[...], TN).astype(BF)


def attn_products(first_normed, grad_first, grad_gate, pieces, gated):
    row_total, feature = first_normed.shape
    total, width = grad_first.shape[1], gated.shape[1]
    block = feature // 4

    def column(rows):
        return pl.BlockSpec((rows, block), lambda i: (0, i))

    def whole(columns):
        return pl.BlockSpec((row_total, columns), lambda i: (0, 0))

    return pl.pallas_call(
        attn_kernel,
        grid=(4,),
        in_specs=[column(row_total), whole(total), whole(width), whole(width)]
        + [column(p.shape[0]) for p in pieces],
        out_specs=pl.BlockSpec((block, total + 2 * width), lambda i: (i, 0)),
        out_shape=jax.ShapeDtypeStruct((feature, total + 2 * width), BF),
        scratch_shapes=[pltpu.VMEM((row_total, block), BF)],
        compiler_params=LIMIT,
        cost_estimate=cost(2 * row_total * feature * (total + 2 * width), 16 * 2**20),
    )(first_normed, grad_first, grad_gate, gated, *pieces)


def place_kernel(at, *refs):
    ins, outs = refs[:4], refs[4:]
    width, half = ins[0].shape[1], outs[0].shape[0]
    for k in range(4):
        columns = pl.ds(pl.multiple_of((at[0] ^ k) * width, LANES), width)
        for n, out in enumerate(outs):
            out[:, columns] = ins[k][n * half : (n + 1) * half, :]


def placed(pieces, start):
    rows, width = pieces[0].shape
    return pl.pallas_call(
        place_kernel,
        grid_spec=pltpu.PrefetchScalarGridSpec(
            num_scalar_prefetch=1,
            grid=(1,),
            in_specs=[pl.BlockSpec((rows, width), lambda i, at: (0, 0))] * 4,
            out_specs=[pl.BlockSpec((rows // 2, 4 * width), lambda i, at: (0, 0))] * 2,
        ),
        out_shape=[jax.ShapeDtypeStruct((rows // 2, 4 * width), BF)] * 2,
        compiler_params=ALONE,
        cost_estimate=cost(1, 4 * 2**20),
    )(start.astype(jnp.int32)[None], *pieces)


def reorder_kernel(at, *refs):
    count = len(refs) // 4 - 1
    width = refs[0].shape[1]
    for k in range(4):
        for n in range(4):

            @pl.when((at[0] ^ k) == n)
            def copy(k=k, n=n):
                for m in range(count):
                    refs[4 * count + k][:, m * width : (m + 1) * width] = refs[4 * m + n][...]


def reordered(sets, start):
    rows, width = sets[0][0].shape
    total = width * len(sets)
    return pl.pallas_call(
        reorder_kernel,
        grid_spec=pltpu.PrefetchScalarGridSpec(
            num_scalar_prefetch=1,
            grid=(1,),
            in_specs=[pl.BlockSpec((rows, width), lambda i, at: (0, 0))] * (4 * len(sets)),
            out_specs=[pl.BlockSpec((rows, total), lambda i, at: (0, 0))] * 4,
        ),
        out_shape=[jax.ShapeDtypeStruct((rows, total), BF)] * 4,
        compiler_params=ALONE,
        cost_estimate=cost(1, 4 * 2**20),
    )(start.astype(jnp.int32)[None], *[p for pieces in sets for p in pieces])


def half_sums(parts):
    a0, a1, a2, b0, b1, b2 = (p[...].astype(F32) for p in parts)
    return jnp.concatenate([a0 + a1 + a2, b0 + b1 + b2], axis=1)


def mean_scale(rows):
    return lax.rsqrt(jnp.mean(rows * rows, axis=1, keepdims=True) + EPSILON)


def norm_backward(grad, rows, gain):
    scale = mean_scale(rows)
    normed = rows * scale
    grad_normed = grad * gain
    inner = jnp.mean(grad_normed * normed, axis=1, keepdims=True)
    return scale * (grad_normed - normed * inner)


def put_halves(value, top, low):
    step = pl.program_id(0)

    @pl.when(step == 0)
    def first():
        top[...] = value

    @pl.when(step == 1)
    def second():
        low[...] = value


def put_quarters(lane, value, outs, held):
    held[...] = value
    width = outs[0].shape[1]
    for k, out in enumerate(outs):
        out[...] = held[:, pl.ds(pl.multiple_of((lane ^ k) * width, LANES), width)]


def either(top, low):
    return jnp.where(pl.program_id(0) == 0, top[...].astype(F32), low[...].astype(F32))


def up_norm_kernel(where, x_top, x_low, gain_ref, *refs):
    second = either(x_top, x_low) + half_sums(refs[:6])
    refs[6][...] = second
    put_halves((second * mean_scale(second) * gain_ref[1:2, :]).astype(BF), refs[7], refs[8])


def down_norm_kernel(where, second_ref, grad_top, grad_low, gain_ref, *refs):
    grad = either(grad_top, grad_low) + norm_backward(
        half_sums(refs[:6]), second_ref[...], gain_ref[1:2, :]
    )
    refs[6][...] = grad
    put_halves(grad.astype(BF), refs[7], refs[8])


def result_kernel(where, second_ref, own_ref, one, two, three, *refs):
    result = second_ref[...] + own_ref[...]
    for part in (one, two, three):
        result += part[...].astype(F32)
    put_quarters(where[2], result.astype(BF), refs[:4], refs[4])


def input_norm_kernel(where, x_top, x_low, grad_ref, gain_ref, *refs):
    grad = grad_ref[...] + norm_backward(
        half_sums(refs[:6]), either(x_top, x_low), gain_ref[0:1, :]
    )
    put_quarters(where[2], grad.astype(BF), refs[6:10], refs[10])


def on_rows(kernel, where, rows, gains, parts, quarters):
    feature = 2 * parts[0].shape[1] if parts else rows[0].shape[1]
    row_total = rows[-1].shape[0] if not parts else parts[0].shape[0]
    block = row_total // 2

    def spec(width):
        return pl.BlockSpec((block, width), lambda i, *_: (i, 0))

    top = low = pl.BlockSpec((block, feature), lambda i, *_: (0, 0))
    ins, args = [], []
    for r in rows:
        if isinstance(r, (list, tuple)):
            ins += [top, low]
            args += list(r)
        else:
            ins.append(spec(feature))
            args.append(r)
    if gains is not None:
        ins.append(pl.BlockSpec(gains.shape, lambda i, *_: (0, 0)))
    ins += [spec(feature // 2)] * len(parts)
    if quarters:
        outs = [spec(feature // 4)] * 4
        shapes = [jax.ShapeDtypeStruct((row_total, feature // 4), BF)] * 4
        scratch = [pltpu.VMEM((block, feature), BF)]
    else:
        outs = [spec(feature), top, low]
        shapes = [jax.ShapeDtypeStruct((row_total, feature), F32)]
        shapes += [jax.ShapeDtypeStruct((block, feature), BF)] * 2
        scratch = []
    return pl.pallas_call(
        kernel,
        grid_spec=pltpu.PrefetchScalarGridSpec(
            num_scalar_prefetch=1,
            grid=(2,),
            in_specs=ins,
            out_specs=outs,
            scratch_shapes=scratch,
        ),
        out_shape=shapes,
        compiler_params=ALONE,
        cost_estimate=cost(1, 6 * 2**20),
    )(where, *args, *([] if gains is None else [gains]), *parts)


def first_kernel(heads, pieces, w_ref, v_ref, wf_ref, b_ref, h_ref, qkv_ref, keep_ref, slope_ref, gain_ref):
    step = pl.program_id(0)

    @pl.when(step == 0)
    def norm():
        turned = wf_ref[...].astype(F32).T
        for n in range(2):
            first = heads + 3 * n
            gain_ref[n : n + 1, :] = (
                turned[first : first + 1] + turned[first + 1 : first + 2] + turned[first + 2 : first + 3]
            )
        block = pieces[0].shape[0]
        for at, piece in enumerate(pieces):
            x = piece[...].astype(F32)
            h_ref[pl.ds(at * block, block), :] = (x * mean_scale(x) * gain_ref[0:1, :]).astype(BF)

    @pl.when(step < 3)
    def query_key():
        qkv_ref[...] = dot(h_ref[...], w_ref[...]).astype(BF)

    @pl.when(step >= 3)
    def value_forget():
        pre = dot(h_ref[...], v_ref[...])
        qkv_ref[...] = pre.astype(BF)

        @pl.when(step == 4)
        def forget():
            real = lanes_of(pre.shape[0]) < heads
            forget_pre = jnp.where(real, pre[:, LANES:] + b_ref[...], 0.0)
            less = jnp.exp(-jnp.abs(forget_pre))
            keep_ref[...] = jnp.minimum(forget_pre, 0.0) - jnp.log1p(less)
            slope_ref[...] = jnp.where(
                real, jnp.where(forget_pre >= 0, less, 1.0) / (1.0 + less), 0.0
            )


def first_products(heads, pieces, weights, bias):
    row_total, feature = 8 * pieces[0].shape[0], pieces[0].shape[1]
    block = 256

    def whole_block(shape):
        return pl.BlockSpec(shape, lambda i: (0, 0))

    def kernel(*refs):
        first_kernel(heads, refs[:8], *refs[8:])

    return pl.pallas_call(
        kernel,
        grid=(5,),
        in_specs=[whole_block(p.shape) for p in pieces]
        + [
            pl.BlockSpec((feature, block), lambda i: (0, jnp.minimum(i, 2))),
            pl.BlockSpec((feature, block), lambda i: (0, jnp.maximum(i - 3, 0))),
            pl.BlockSpec((feature, LANES), lambda i: (0, 3)),
            whole_block((1, LANES)),
        ],
        out_specs=[
            whole_block((row_total, feature)),
            pl.BlockSpec((row_total, block), lambda i: (0, i)),
            whole_block((row_total, LANES)),
            whole_block((row_total, LANES)),
            whole_block((8, feature)),
        ],
        out_shape=[
            jax.ShapeDtypeStruct((row_total, feature), BF),
            jax.ShapeDtypeStruct((row_total, 5 * block), BF),
            jax.ShapeDtypeStruct((row_total, LANES), F32),
            jax.ShapeDtypeStruct((row_total, LANES), F32),
            jax.ShapeDtypeStruct((8, feature), F32),
        ],
        compiler_params=ALONE,
        cost_estimate=cost(10 * row_total * feature * block, 12 * 2**20),
    )(*pieces, weights[0], weights[1], weights[1], bias)


def gate_kernel(h_ref, w_ref, att_ref, gate_ref, y_ref):
    gate = jax.nn.sigmoid(dot(h_ref[...], w_ref[...]))
    gate_ref[...] = gate
    y_ref[...] = (att_ref[...] * gate).astype(BF)


def gate_products(first_normed, weights, attended):
    row_total, feature = first_normed.shape
    width = attended.shape[1]

    def by_rows(columns):
        return pl.BlockSpec((row_total // 4, columns), lambda i: (i, 0))

    return pl.pallas_call(
        gate_kernel,
        grid=(4,),
        in_specs=[
            by_rows(feature),
            pl.BlockSpec((feature, width), lambda i: (0, 0)),
            by_rows(width),
        ],
        out_specs=[by_rows(width)] * 2,
        out_shape=[
            jax.ShapeDtypeStruct((row_total, width), F32),
            jax.ShapeDtypeStruct((row_total, width), BF),
        ],
        compiler_params=LIMIT,
        cost_estimate=cost(2 * row_total * feature * width, 10 * 2**20),
    )(first_normed, weights, attended)


def join(pieces, whole):
    block = pieces[0].shape[0]
    for at, piece in enumerate(pieces):
        whole[pl.ds(at * block, block), :] = piece[...]


def up_kernel(*refs):
    pieces, g_ref, u_ref = refs[:4], refs[4], refs[5]
    h_ref, m_ref, to_gate_ref, to_up_ref = refs[-4:]

    @pl.when(pl.program_id(0) == 0)
    def first():
        join(pieces, h_ref)

    gate = dot(h_ref[...], g_ref[...])
    up = dot(h_ref[...], u_ref[...])
    sig = jax.nn.sigmoid(gate)
    silu = gate * sig
    m_ref[...] = (silu * up).astype(BF)
    to_gate_ref[...] = (up * sig * (1.0 + gate * (1.0 - sig))).astype(to_gate_ref.dtype)
    to_up_ref[...] = silu.astype(to_up_ref.dtype)


def up_products(half, held, pieces, weights):
    rows, feature = 4 * pieces[0].shape[0], pieces[0].shape[1]
    hidden, block = weights.shape[1] // 2, 256
    steps = hidden // block
    return pl.pallas_call(
        up_kernel,
        grid=(steps,),
        in_specs=[pl.BlockSpec(p.shape, lambda i: (0, 0)) for p in pieces]
        + [
            pl.BlockSpec((feature, block), lambda i: (0, i)),
            pl.BlockSpec((feature, block), lambda i: (0, steps + i)),
        ]
        + [pl.BlockSpec(memory_space=pl.ANY)] * len(held),
        out_specs=[pl.BlockSpec((rows, feature), lambda i: (half, 0))]
        + [pl.BlockSpec((rows, block), lambda i: (half, i))] * 3,
        out_shape=[jax.ShapeDtypeStruct((2 * rows, feature), BF)]
        + [jax.ShapeDtypeStruct((2 * rows, hidden), BF)] * 3,
        input_output_aliases={6 + n: n for n in range(len(held))},
        compiler_params=ALONE,
        cost_estimate=cost(4 * rows * feature * hidden, 16 * 2**20),
    )(*pieces, weights, weights, *held)


def down_kernel(g_ref, w_ref, to_gate_ref, to_up_ref, out_ref):
    grad = dot(g_ref[...], w_ref[...])
    out_ref[0] = (grad * to_gate_ref[...]).astype(BF)
    out_ref[1] = (grad * to_up_ref[...]).astype(BF)


def down_products(grad_out, weights, to_gate, to_up):
    row_total, feature = grad_out.shape
    hidden, block = weights.shape[1], 256
    column = pl.BlockSpec((row_total, block), lambda i: (0, i))
    return pl.pallas_call(
        down_kernel,
        grid=(hidden // block,),
        in_specs=[
            pl.BlockSpec((row_total, feature), lambda i: (0, 0)),
            pl.BlockSpec((feature, block), lambda i: (0, i)),
            column,
            column,
        ],
        out_specs=pl.BlockSpec((2, row_total, block), lambda i: (0, 0, i)),
        out_shape=jax.ShapeDtypeStruct((2, row_total, hidden), BF),
        compiler_params=LIMIT,
        cost_estimate=cost(2 * row_total * feature * hidden, 16 * 2**20),
    )(grad_out, weights, to_gate, to_up)


def back_kernel(*refs):
    pieces, (w_ref, gate_ref, att_ref, datt_ref, dgate_ref, z_ref) = refs[:8], refs[8:]
    block = pieces[0].shape[0]
    for at in range(4):

        @pl.when(pl.program_id(0) == at)
        def put(at=at):
            z_ref[:block, :] = pieces[2 * at][...]
            z_ref[block:, :] = pieces[2 * at + 1][...]

    grad = dot(z_ref[...], w_ref[...])
    gate = gate_ref[...]
    datt_ref[...] = (grad * gate).astype(BF)
    dgate_ref[...] = (grad * att_ref[...] * gate * (1.0 - gate)).astype(BF)


def back_products(pieces, weights, gate, attended):
    row_total, feature = 8 * pieces[0].shape[0], pieces[0].shape[1]
    width = attended.shape[1]

    def spec(shape, at=0):
        return pl.BlockSpec(shape, lambda i: (0, at))

    def by_rows(columns):
        return pl.BlockSpec((row_total // 4, columns), lambda i: (i, 0))

    return pl.pallas_call(
        back_kernel,
        grid=(4,),
        in_specs=[spec(p.shape) for p in pieces]
        + [spec((feature, width), 1), by_rows(width), by_rows(width)],
        out_specs=[by_rows(width)] * 2,
        out_shape=[jax.ShapeDtypeStruct((row_total, width), BF)] * 2,
        scratch_shapes=[pltpu.VMEM((row_total // 4, feature), BF)],
        compiler_params=ALONE,
        cost_estimate=cost(2 * row_total * feature * width, 10 * 2**20),
    )(*pieces, weights, gate, attended)


def slot_tables(lengths, dealing, stream):
    width = lengths.shape[1]
    given, slot_of = [], []
    start = jnp.int32(0)
    for g in range(width):
        given.append(start)
        start = start + lengths[stream, g]
        slot_of.append(dealing[stream, g])
    dealt, given_at = [], []
    start = jnp.int32(0)
    for k in range(width):
        dealt.append(start)
        here = jnp.int32(0)
        for g in range(width):
            here = jnp.where(slot_of[g] == k, given[g], here)
            start = start + jnp.where(slot_of[g] == k, lengths[stream, g], 0)
        given_at.append(here)
    return given, slot_of, dealt, given_at


def pick_kernel(backward, where, lengths, dealing, *refs):
    column, row = where[0], where[1]
    block = refs[0].shape[0] // (1 if backward else 4)
    row_total = 4 * block
    step = pl.program_id(0)
    given, slot_of, dealt, given_at = slot_tables(lengths, dealing, column)
    within = lax.broadcasted_iota(jnp.int32, (block, 1), 0)
    if backward:
        places = row * row_total + step * block + within
        moves = []
        for g in range(len(given)):
            there = jnp.int32(0)
            for k in range(len(given)):
                there = jnp.where(slot_of[g] == k, dealt[k], there)
            moves.append((given[g], there - given[g]))
    else:
        places = row * row_total + (step ^ column) * block + within
        moves = [(s, g - s) for s, g in zip(dealt, given_at)]
    move = jnp.zeros_like(places) + moves[0][1]
    for first, by in moves[1:]:
        move = jnp.where(places >= first, by, move)
    near = places + move - row * row_total
    near = jnp.where(near < 0, near + 2 * row_total, near)
    if backward:
        other = jnp.where(near >= row_total, row_total, 0)
        local = near - other
        part = sum(jnp.where(local >= k * block, 1, 0) for k in (1, 2, 3))
        near = other + local + (jnp.bitwise_xor(part, column) - part) * block
    start = row * row_total + (step if backward else step ^ column) * block
    held = refs[-1]
    held[...] = jnp.zeros_like(held)
    across = lax.broadcasted_iota(jnp.int32, (block, block), 1)
    for part in range(8):
        if backward:
            place = 4 * ((part // 4) ^ row) + ((part % 4) ^ column)
        else:
            place = (part + 4 * row) & 7
        met = jnp.bool_(False)
        for n, (first, by) in enumerate(moves):
            low = jnp.maximum(start, first) + by
            high = start + block
            if n + 1 < len(moves):
                high = jnp.minimum(high, moves[n + 1][0])
            high = high + by
            met |= (low < high) & (low < (place + 1) * block) & (high > place * block)

        @pl.when(met)
        def add(part=part):
            chosen = jnp.where(across == near - part * block, 1.0, 0.0).astype(BF)
            if backward:
                held[...] += dot(chosen, refs[part][...])
            else:
                rows = pl.ds(part % 4 * block, block)
                width = refs[0].shape[1]
                for at in range(2):
                    held[:, at * width : (at + 1) * width] += dot(
                        chosen, refs[2 * at + part // 4][rows, :]
                    )

    if backward:
        refs[8][...] = held[...].astype(BF)
        return
    width = refs[0].shape[1]
    for at in range(2):
        for k in range(4):

            @pl.when(step == k)
            def put(k=k, at=at):
                refs[4 + 4 * at + k][...] = held[:, at * width : (at + 1) * width].astype(BF)


def moved_rows(backward, where, lengths, dealing, arrays):
    if backward:
        block, width = arrays[0].shape
        row_total = 4 * block
    else:
        row_total, width = arrays[0].shape
        block = row_total // 4
    if lax.axis_size("dp") != 2:
        column, row = where[0], where[1]
        local = jnp.arange(row_total, dtype=jnp.int32)
        own_lengths = lax.dynamic_index_in_dim(lengths, column, 0, keepdims=False)
        own_dealing = lax.dynamic_index_in_dim(dealing, column, 0, keepdims=False)
        if backward:
            to = given_targets(own_lengths, own_dealing, row * row_total + local)
            at = to % row_total
            to = to - at + ((at // block) ^ column) * block + at % block
            arrays = [jnp.concatenate(arrays, axis=0)]
        else:
            swapped = (((local // block) ^ column) * block) + local % block
            to = dealt_sources(own_lengths, own_dealing, row * row_total + swapped)
        moved = [jnp.take(lax.all_gather(a, "dp", axis=0, tiled=True), to, axis=0) for a in arrays]
        if backward:
            return moved
        return [m[k * block : (k + 1) * block] for m in moved for k in range(4)]
    others = [swap(a, "dp", 1) for a in arrays]
    if backward:
        outs = [pl.BlockSpec((block, width), lambda i, *_: (i, 0))]
        shapes = [jax.ShapeDtypeStruct((row_total, width), BF)]
        ins = [*arrays, *others]
    else:
        outs = [pl.BlockSpec((block, width), lambda i, *_: (0, 0))] * 8
        shapes = [jax.ShapeDtypeStruct((block, width), BF)] * 8
        ins = [arrays[0], others[0], arrays[1], others[1]]
    return pl.pallas_call(
        lambda *refs: pick_kernel(backward, *refs),
        grid_spec=pltpu.PrefetchScalarGridSpec(
            num_scalar_prefetch=3,
            grid=(4,),
            in_specs=[pl.BlockSpec(a.shape, lambda i, *_: (0, 0)) for a in ins],
            out_specs=outs,
            scratch_shapes=[pltpu.VMEM((block, width if backward else 2 * width), F32)],
        ),
        out_shape=shapes,
        compiler_params=pltpu.CompilerParams(vmem_limit_bytes=40 * 2**20),
        cost_estimate=cost(16 * row_total * row_total * width, 8 * 2**20),
    )(where, lengths, dealing, *ins)


def piece_rows(piece, half):
    rows = []
    for places in (UPPER, LOWER):
        place = jnp.int32(places[0])
        for k in (1, 2, 3):
            place = jnp.where(piece == k, places[k], place)
        rows.append(pl.ds(pl.multiple_of(place * half, half), half))
    return rows


def get_rows(ref, rows):
    return jnp.concatenate([ref[part, :] for part in rows], axis=0)


def put_rows(ref, rows, columns, value):
    half = value.shape[0] // 2
    for n, part in enumerate(rows):
        ref[part, columns] = value[n * half : (n + 1) * half]


def lanes_of(rows):
    return lax.broadcasted_iota(jnp.int32, (rows, LANES), 1)


def split_column(column):
    one = column.astype(BF).astype(F32)
    two = (column - one).astype(BF).astype(F32)
    return one, two, column - one - two


def fill(lanes, base, columns, rest):
    for at, column in reversed(list(enumerate(columns))):
        rest = jnp.where(lanes == base + at, column, rest)
    return rest


def forward_kernel(
    where,
    lengths,
    dealing,
    q_ref,
    k_ref,
    v_ref,
    keep_ref,
    att_ref,
    qa_ref,
    ka_ref,
    c_ref,
    va_ref,
):
    pair = pl.program_id(0)
    column, row, lane = where[0], where[1], where[2]
    first_length = jnp.int32(0)
    for g in range(lengths.shape[1]):
        first_length += jnp.where(dealing[lane, g] == 2 * row, lengths[lane, g], 0)
    row_total = q_ref.shape[0]
    block = row_total // 4
    lanes = lanes_of(block)

    def rows_of(at):
        return piece_rows(column ^ at, block // 2)

    @pl.when(pair == 0)
    def sum_keeps():
        below = lax.broadcasted_iota(jnp.int32, (block, block), 0)
        across = lax.broadcasted_iota(jnp.int32, (block, block), 1)
        ones = jnp.where(below >= across, 1.0, 0.0)
        running = jnp.zeros((1, LANES), F32)
        for at in range(4):
            sums = running + lax.dot_general(
                ones,
                get_rows(keep_ref, rows_of(at)),
                (((1,), (0,)), ((), ())),
                precision=lax.Precision.HIGHEST,
                preferred_element_type=F32,
            )
            c_ref[pl.ds(at * block, block), :] = sums
            running = sums[block - 1 :, :]

    for head in range(2):
        mine = (lanes < 64) if head == 0 else (lanes >= 64)
        base = 64 if head == 0 else 0
        for at in range(4):
            rows, own = rows_of(at), pl.ds(at * block, block)
            decay = jnp.sum(
                jnp.where(lanes == 2 * pair + head, c_ref[own, :], 0.0), axis=1, keepdims=True
            )
            one, two, three = split_column(decay)
            places = at * block + lax.broadcasted_iota(jnp.int32, (block, 1), 0)
            second = jnp.where(places >= first_length, 1.0, 0.0)
            q_side = fill(lanes, base, (1.0, 1.0, 1.0, second), 0.0)
            k_side = fill(
                lanes, base, (-one, -two, -three, (second - 1.0) * FAR, 1.0, 1.0, 1.0), 0.0
            )
            qa_ref[head, own, :] = jnp.where(
                mine, get_rows(q_ref, rows).astype(F32) * 0.125, q_side
            ).astype(BF)
            ka_ref[head, own, :] = jnp.where(mine, get_rows(k_ref, rows).astype(F32), k_side).astype(BF)
            va_ref[head, own, :] = jnp.where(mine, get_rows(v_ref, rows).astype(F32), 1.0).astype(BF)

    below = lax.broadcasted_iota(jnp.int32, (block, block), 0)
    across = lax.broadcasted_iota(jnp.int32, (block, block), 1)
    for at in range(4):
        own = pl.ds(at * block, block)
        width = (at + 1) * block
        results = []
        for head in range(2):
            base = 64 if head == 0 else 0
            queries = qa_ref[head, own, :]
            last = jnp.where(
                below >= across, dot(queries, ka_ref[head, at * block : width, :], NT), -FAR
            )
            top = jnp.max(last, axis=1, keepdims=True)
            if at > 0:
                early = dot(queries, ka_ref[head, : at * block, :], NT)
                top = jnp.maximum(top, jnp.max(early, axis=1, keepdims=True))
            total = dot(jnp.exp(last - top).astype(BF), va_ref[head, at * block : width, :])
            if at > 0:
                total += dot(jnp.exp(early - top).astype(BF), va_ref[head, : at * block, :])
            weight = pltpu.roll(total, 64, 1)
            results.append(total / weight)
            log_total = top + jnp.log(total[:, base : base + 1])
            one, two, three = split_column(log_total)
            qa_ref[head, own, :] = fill(
                lanes, base + 4, (-one, -two, -three), queries.astype(F32)
            ).astype(BF)
        attended = jnp.where(lanes < 64, results[0], results[1])
        put_rows(att_ref, rows_of(at), slice(None), attended)


def attend_forward(where, lengths, dealing, qkv, keep):
    row_total, width = qkv.shape[0], qkv.shape[1] // LANES // 3 * LANES
    pairs = width // LANES
    heads = 2 * pairs

    def columns(first):
        return pl.BlockSpec((row_total, LANES), lambda p, *_: (0, first + p))

    sided = pl.BlockSpec((2, row_total, LANES), lambda p, *_: (p, 0, 0))
    return pl.pallas_call(
        forward_kernel,
        grid_spec=pltpu.PrefetchScalarGridSpec(
            num_scalar_prefetch=3,
            grid=(pairs,),
            in_specs=[
                columns(0),
                columns(pairs),
                columns(2 * pairs),
                pl.BlockSpec((row_total, LANES), lambda p, *_: (0, 0)),
            ],
            out_specs=[columns(0), sided, sided],
            scratch_shapes=[
                pltpu.VMEM((row_total, LANES), F32),
                pltpu.VMEM((2, row_total, LANES), BF),
            ],
        ),
        out_shape=[
            jax.ShapeDtypeStruct((row_total, width), F32),
            jax.ShapeDtypeStruct((heads, row_total, LANES), BF),
            jax.ShapeDtypeStruct((heads, row_total, LANES), BF),
        ],
        compiler_params=pltpu.CompilerParams(vmem_limit_bytes=60 * 2**20),
        cost_estimate=cost(10 * 10**9, 8 * 2**20),
    )(where, lengths, dealing, qkv, qkv, qkv, keep)


def backward_kernel(
    where,
    qa_ref,
    ka_ref,
    v_ref,
    datt_ref,
    att_ref,
    slope_ref,
    out_ref,
    va_ref,
    da_ref,
    kt_ref,
    dk_ref,
    dv_ref,
    dq_ref,
    dc_ref,
):
    pair = pl.program_id(0)
    pairs = pl.num_programs(0)
    column = where[0]
    row_total = v_ref.shape[0]
    block = row_total // 4
    lanes = lanes_of(block)
    width = att_ref.shape[1] * pairs

    def rows_of(at):
        return piece_rows(column ^ at, block // 2)

    def lanes_at(group):
        return pl.ds(pl.multiple_of((group * pairs + pair) * LANES, LANES), LANES)

    @pl.when(pair == 0)
    def clear():
        dc_ref[...] = jnp.zeros_like(dc_ref)

    for at in range(4):
        rows, own = rows_of(at), pl.ds(at * block, block)
        grad_att = get_rows(datt_ref, rows).astype(F32)
        inner = grad_att * get_rows(att_ref, rows)
        values = get_rows(v_ref, rows).astype(F32)
        for head in range(2):
            mine = (lanes < 64) if head == 0 else (lanes >= 64)
            base = 64 if head == 0 else 0
            delta = jnp.sum(jnp.where(mine, inner, 0.0), axis=1, keepdims=True)
            one, two, three = split_column(delta)
            da_ref[head, own, :] = jnp.where(
                mine, grad_att, fill(lanes, base, (-one, -two, -three), 0.0)
            ).astype(BF)
            va_ref[head, own, :] = jnp.where(
                mine, values, fill(lanes, base, (1.0, 1.0, 1.0), 0.0)
            ).astype(BF)

    below = lax.broadcasted_iota(jnp.int32, (block, block), 0)
    across = lax.broadcasted_iota(jnp.int32, (block, block), 1)
    for head in range(2):
        for at in range(4):
            own = pl.ds(at * block, block)
            kt_ref[:, own] = ka_ref[head, own, :].astype(F32).T.astype(BF)
        for at in range(4):
            own = pl.ds(at * block, block)
            queries, grads = qa_ref[head, own, :], da_ref[head, own, :]
            dq_t = jnp.zeros((LANES, block), F32)
            for past in range(at + 1):
                keys = pl.ds(past * block, block)
                probs = jnp.exp(dot(ka_ref[head, keys, :], queries, NT))
                if past == at:
                    probs = jnp.where(below <= across, probs, 0.0)
                grad_scores = (probs * dot(va_ref[head, keys, :], grads, NT)).astype(BF)
                dv = dot(probs.astype(BF), grads)
                dk = dot(grad_scores, queries)
                dq_t += dot(kt_ref[:, keys], grad_scores)
                if past == at:
                    dv_ref[head, keys, :] = dv
                    dk_ref[head, keys, :] = dk
                else:
                    dv_ref[head, keys, :] += dv
                    dk_ref[head, keys, :] += dk
            dq_ref[head, own, :] = dq_t.T

    for at in range(4):
        rows, own = rows_of(at), pl.ds(at * block, block)
        for head in range(2):
            base = 64 if head == 0 else 0
            change = (
                dq_ref[head, own, base + 4 : base + 5] - dk_ref[head, own, base : base + 1]
            )
            dc_ref[own, :] += jnp.where(lanes == 2 * pair + head, change, 0.0)
        left = lanes < 64
        for group, ref, scale in ((0, dq_ref, 0.125), (1, dk_ref, 1.0), (2, dv_ref, 1.0)):
            both = jnp.where(left, ref[0, own, :], ref[1, own, :])
            put_rows(out_ref, rows, lanes_at(group), (both * scale).astype(BF))

    @pl.when(pair == pairs - 1)
    def finish():
        ones = jnp.where(below <= across, 1.0, 0.0)
        running = jnp.zeros((1, LANES), F32)
        for at in reversed(range(4)):
            sums = running + lax.dot_general(
                ones,
                dc_ref[pl.ds(at * block, block), :],
                (((1,), (0,)), ((), ())),
                precision=lax.Precision.HIGHEST,
                preferred_element_type=F32,
            )
            running = sums[:1, :]
            rows = rows_of(at)
            put_rows(
                out_ref,
                rows,
                slice(3 * width, None),
                (sums * get_rows(slope_ref, rows)).astype(BF),
            )


def attend_backward(where, qa, ka, qkv, grad_att, attended, slope):
    row_total, width = attended.shape
    pairs = width // LANES
    heads = 2 * pairs
    total = 3 * width + LANES

    def columns(first):
        return pl.BlockSpec((row_total, LANES), lambda p, *_: (0, first + p))

    sided = pl.BlockSpec((2, row_total, LANES), lambda p, *_: (p, 0, 0))
    both = (2, row_total, LANES)
    return pl.pallas_call(
        backward_kernel,
        grid_spec=pltpu.PrefetchScalarGridSpec(
            num_scalar_prefetch=1,
            grid=(pairs,),
            in_specs=[
                sided,
                sided,
                columns(2 * pairs),
                columns(0),
                columns(0),
                pl.BlockSpec((row_total, LANES), lambda p, *_: (0, 0)),
            ],
            out_specs=pl.BlockSpec((row_total, total), lambda p, *_: (0, 0)),
            scratch_shapes=[
                pltpu.VMEM(both, BF),
                pltpu.VMEM(both, BF),
                pltpu.VMEM((LANES, row_total), BF),
                pltpu.VMEM(both, F32),
                pltpu.VMEM(both, F32),
                pltpu.VMEM(both, F32),
                pltpu.VMEM((row_total, LANES), F32),
            ],
        ),
        out_shape=jax.ShapeDtypeStruct((row_total, total), BF),
        compiler_params=pltpu.CompilerParams(vmem_limit_bytes=60 * 2**20),
        cost_estimate=cost(12 * 10**9, 8 * 2**20),
    )(where, qa, ka, qkv, grad_att, attended, slope)


def on_device(
    x_given,
    cotangent,
    seq_lengths,
    seq_deal,
    attn_gain,
    w_query,
    w_key,
    w_value,
    w_ogate,
    w_forget,
    b_forget,
    w_out,
    mlp_gain,
    w_gate,
    w_up,
    w_down,
):
    quarter = x_given.shape[1]
    piece = quarter // 4
    row, column, lane = lax.axis_index("dp"), lax.axis_index("tx"), lax.axis_index("ty")
    heads = w_forget.shape[1]
    width = w_query.shape[1]
    hidden = w_gate.shape[1]
    share = w_query.shape[0] // lax.axis_size("dp")

    def own_share(weights):
        return lax.dynamic_slice_in_dim(weights, row * share, share, axis=0)

    def whole(weights):
        return lax.all_gather(weights, ("ty", "dp"), axis=0, tiled=True)

    gains = jnp.stack(three_parts(attn_gain) + three_parts(mlp_gain), axis=1).astype(BF)
    spare = jnp.zeros((w_query.shape[0], LANES - heads - 6), BF)
    side = 3 * width
    last = side + LANES
    def side_by_side(*weights):
        return jnp.concatenate([own_share(w) for w in weights], axis=1)

    w_first = [whole(side_by_side(w_query, w_key))]

    where = jnp.stack([column, row, lane]).astype(jnp.int32)
    paired = lax.axis_size("dp") == 2

    dealt = moved_rows(False, where, seq_lengths, seq_deal, (x_given[0], cotangent[0]))
    x_parts, grad_parts = tie(spread_plane(dealt[:4]), dealt[4:])
    x_parts, grad_parts = tie(
        spread_line(reordered([x_parts], column ^ lane)), spread_plane(grad_parts)
    )
    grad_parts, x_parts = tie(reordered([grad_parts], column ^ lane), x_parts)
    w_first.append(whole(side_by_side(w_value, w_forget, gains, spare)))
    later = [side_by_side(w_ogate, w_out.T), side_by_side(w_gate, w_up)]
    x_parts, later, w_first[0] = tie(x_parts, later, w_first[0])
    w_second, w_gate_up = [whole(w) for w in later]
    grad_parts = spread_line(grad_parts)
    x_full, unused = gather_rows(*placed(x_parts, lane), ahead=(grad_parts[1], w_first[1]))

    bias = jnp.pad(b_forget, (0, LANES - heads))[None]
    first_normed, qkv, keep, slope, gains = first_products(heads, x_full, w_first, bias)
    grad_parts, qkv = tie(grad_parts, qkv)
    top, low = placed(grad_parts, lane)
    grad_rows = [top, low]
    qkv, top, low = tie(qkv, top, low)
    top_x, low_y = swap(top, "tx", 1), swap(low, "tx", 2)
    low_x, top_y = swap(low, "tx", 1), swap(top, "tx", 2)
    attended, qa, ka = attend_forward(where, seq_lengths, seq_deal, qkv, keep)
    attended, top_x, low_y, low_x, top_y = tie(attended, top_x, low_y, low_x, top_y)
    top_d, low_d = swap(top_x, "tx", 2), swap(low_y, "tx", 1)
    grad_full = [top, low, top_x, low_y, low_x, top_y, top_d, low_d]
    w_down_t, attended = tie(own_share(w_down.T), attended)
    w_down_t = whole(w_down_t)
    out_gate, gated = gate_products(first_normed, w_second, attended)
    gated, grad_full[6:] = tie(gated, grad_full[6:])
    parts, unused = scatter_products([(gated, 0)], [(w_second, width, 1)])
    second, top, low = on_rows(up_norm_kernel, where, [x_full[:2]], gains, parts, False)

    def up_half(pieces, ahead):
        return up_products(0, [], pieces, w_gate_up)

    h2_parts, held = gather_rows(top, low, up_half)
    h2_full, mid, to_gate, to_up = up_products(1, held, h2_parts[4:], w_gate_up)
    part, grad_full = turned_products(mid, grad_full)
    part, grad_full = tie(part, grad_full)
    grads_down = summed(part)
    grad_gate_up = down_products(grad_full, w_down_t, to_gate, to_up)

    def gate_up_products(ready):
        left, unused = tie(h2_full, ready[0])
        return row_products(left, grad_gate_up)

    parts, part = scatter_products(
        [(grad_gate_up, 0), (grad_gate_up, 1)],
        [(w_gate_up, hidden, 0), (w_gate_up, hidden, 1)],
        gate_up_products,
    )
    part, parts = tie(part, parts)
    grads_gate_up = summed(part)
    grad_second, top, low = on_rows(
        down_norm_kernel, where, [second, grad_rows], gains, parts, False
    )

    def result_products(pieces, ahead):
        left, unused = tie(mid, pieces)
        return part_products(
            (1, 2, 3, 0), [BF, BF, BF, F32], False, [(left, 0)], [(w_down_t, hidden, 0)]
        )

    z_parts, (*sent, own) = gather_rows(top, low, result_products)

    sent = [swap(piece, "tx", k + 1) for k, piece in enumerate(sent)]
    grad_att, grad_ogate = back_products(z_parts, w_second, out_gate, attended)
    grad_first = attend_backward(where, qa, ka, qkv, grad_att, attended, slope)
    grad_first, sent, grads_down = tie(grad_first, sent, grads_down)
    output = on_rows(result_kernel, where, [second, own, *sent], None, [], True)
    output, grad_first = tie(output, grad_first)
    output = spread_line(output)
    part = attn_products(first_normed, grad_first, grad_ogate, z_parts, gated)
    part, grad_first, output = tie(part, grad_first, output)
    grads_attn = summed(part)

    def given(pieces):
        return moved_rows(True, where, seq_lengths, seq_deal, pieces)[0]

    def row_dots(*sides):
        return sum(jnp.sum(w.astype(F32) * g, axis=1) for w, g in sides)

    def finish(ready):
        down, gate_up, bias, (unused, rows) = tie(
            grads_down, grads_gate_up, grad_first[:, side:], ready
        )
        bias = jnp.sum(bias.astype(F32), axis=0, keepdims=True)
        if paired:
            bias = bias + swap(bias, "dp", 1)
            bias = pairs_sum(spread_line([bias] * 4))
        else:
            bias = lax.psum(bias, ("dp", "ty"))
        down, gate_up = reduce_end(down), reduce_end(gate_up)
        mlp = [gate_up[:, :hidden], gate_up[:, hidden:], down]
        return mlp, row_dots((w_gate, mlp[0]), (w_up, mlp[1])) / mlp_gain, bias, given(rows)

    parts, (grads_mlp, own_mlp_gain, bias_grad, output) = scatter_products(
        [(grad_first, 0), (grad_first, 3), (grad_first, 4), (grad_ogate, 0)],
        [(w_first[0], 2 * width, 0), (w_first[1], 256, 0), (w_first[1], 256, 1), (w_second, width, 0)],
        finish,
        spread_plane(reordered([output], column ^ lane)),
    )
    grad_x = on_rows(input_norm_kernel, where, [x_full[:2], grad_second], gains, parts, True)

    grad_x = spread_line(grad_x)
    grad_x, grads_attn = tie(grad_x, grads_attn)
    grad_x = spread_plane(reordered([grad_x], column ^ lane))

    grad_attn = reduce_end(grads_attn)
    grads = [
        grad_attn[:, :width],
        grad_attn[:, width : 2 * width],
        grad_attn[:, 2 * width : side],
        grad_attn[:, last : last + width],
        grad_attn[:, side : side + heads],
    ]
    own_gain = row_dots(*zip((w_query, w_key, w_value, w_ogate, w_forget), grads)) / attn_gain
    grad_gains = spread_plane([jnp.stack([own_gain, own_mlp_gain])] * 4)
    grad_x, grad_gains, grads = tie(grad_x, grad_gains, grads)
    grad_gains = pairs_sum(grad_gains)
    grad_input = given(grad_x)
    return (
        output[None],
        grad_input[None],
        grad_gains[0],
        *grads,
        bias_grad[0, :heads],
        grad_attn[:, last + width :],
        grad_gains[1],
        *grads_mlp,
    )


def solution(mesh):
    tokens, feature, grid, flipped = P("tx", "dp", "ty"), P("ty"), P("ty", "tx"), P("tx", "ty")
    return jax.shard_map(
        on_device,
        mesh=mesh,
        in_specs=(
            tokens,
            tokens,
            P(),
            P(),
            feature,
            grid,
            grid,
            grid,
            grid,
            grid,
            P("tx"),
            flipped,
            feature,
            grid,
            grid,
            flipped,
        ),
        out_specs=(
            tokens,
            tokens,
            feature,
            grid,
            grid,
            grid,
            grid,
            grid,
            P("tx"),
            flipped,
            feature,
            grid,
            grid,
            flipped,
        ),
        check_vma=False,
    )
```

```python
import jax
import jax.numpy as jnp
from jax import lax
from jax.experimental import pallas as pl
from jax.experimental.pallas import tpu as pltpu
from jax.sharding import PartitionSpec as P

EPSILON = 1e-06
FAR = 2.0**100
LANES = 128
BF = jnp.bfloat16
F32 = jnp.float32


def dot(left, right, dims=((1,), (0,))):
    return lax.dot_general(left, right, (dims, ((), ())), preferred_element_type=F32)


NT = ((1,), (1,))
TN = ((0,), (0,))


def three_parts(values):
    one = lax.reduce_precision(values, 8, 7)
    two = lax.reduce_precision(values - one, 8, 7)
    three = lax.reduce_precision(values - one - two, 8, 7)
    return one, two, three


def pick_small(lookup, indices):
    width = lookup.shape[0]
    matches = indices[:, None] == jnp.arange(width, dtype=jnp.int32)[None, :]
    return jnp.sum(jnp.where(matches, lookup[None, :], 0), axis=1)


def stream_tables(lengths, dealing):
    width = lengths.shape[0]
    numbers = jnp.arange(width, dtype=jnp.int32)
    given_start = jnp.cumsum(lengths) - lengths
    owners = jnp.sum(jnp.where(dealing[None, :] == numbers[:, None], numbers[None, :], 0), axis=1)
    dealt_length = pick_small(lengths, owners)
    dealt_start = jnp.cumsum(dealt_length) - dealt_length
    return (given_start, owners, dealt_start, dealt_length)


def dealt_sources(lengths, dealing, places):
    given_start, owners, dealt_start, unused = stream_tables(lengths, dealing)
    slot_ids = jnp.sum((dealt_start[None, :] <= places[:, None]).astype(jnp.int32), axis=1) - 1
    return (
        pick_small(given_start, pick_small(owners, slot_ids))
        + places
        - pick_small(dealt_start, slot_ids)
    )


def given_targets(lengths, dealing, places):
    given_start, unused, dealt_start, unused = stream_tables(lengths, dealing)
    member = jnp.sum((given_start[None, :] <= places[:, None]).astype(jnp.int32), axis=1) - 1
    return (
        pick_small(dealt_start, pick_small(dealing, member))
        + places
        - pick_small(given_start, member)
    )


def swap(values, axis, step):
    return lax.ppermute(values, axis, [(at, at ^ step) for at in range(lax.axis_size(axis))])


def spread_plane(pieces):
    return [pieces[0]] + [swap(pieces[k], "tx", k) for k in (1, 2, 3)]


def spread_line(pieces):
    return [pieces[0]] + [swap(pieces[k], "ty", k) for k in (1, 2, 3)]


def pairs_sum(parts):
    return (parts[0] + parts[1]) + (parts[2] + parts[3])


def tie(*groups):
    return lax.optimization_barrier(groups)


UPPER, LOWER = (0, 2, 5, 6), (1, 4, 3, 7)


def gather_rows(top, low, beside=None, ahead=None):
    top_x, low_y = swap(top, "tx", 1), swap(low, "tx", 2)
    low_x, top_y = swap(low, "tx", 1), swap(top, "tx", 2)
    top_x, low_y, ahead = tie(top_x, low_y, ahead)
    top_d, low_d = swap(top_x, "tx", 2), swap(low_y, "tx", 1)
    done = None if beside is None else beside([top, low, top_x, low_y], ahead)
    return [top, low, top_x, low_y, low_x, top_y, top_d, low_d], done


def scatter_products(lefts, weights, beside=None, ahead=None):
    a3, b3 = part_products((3,), [BF, BF], True, lefts, weights)
    arrays, a3, b3, ahead = tie([array for array, unused in lefts], a3, b3, ahead)
    lefts = [(array, place) for array, (unused, place) in zip(arrays, lefts)]
    a3, b3 = swap(a3, "tx", 1), swap(b3, "tx", 2)
    rest = part_products((1, 2, 0), [BF, F32, F32, F32, BF, F32], True, lefts, weights)
    a3, b3, (a1, a2, a0, b1, b2, b0) = tie(a3, b3, rest)
    a1, b2 = swap(a1, "tx", 1), swap(b2, "tx", 2)
    send_a2 = (a2 + a3.astype(F32)).astype(BF)
    send_b1 = (b1 + b3.astype(F32)).astype(BF)
    done = None if beside is None else beside((send_b1, ahead))
    a2, b1 = swap(send_a2, "tx", 2), swap(send_b1, "tx", 1)
    a1, a2, b1, b2, done = tie(a1, a2, b1, b2, done)
    return [a0, a1, a2, b0, b1, b2], done


def summed(part):
    return lax.psum_scatter(part, ("ty", "dp"), scatter_dimension=0, tiled=True)


def reduce_end(piece):
    if lax.axis_size("dp") != 2:
        return lax.all_gather(piece, "dp", axis=0, tiled=True).astype(F32)
    other = swap(piece, "dp", 1)
    lower = lax.axis_index("dp") == 0
    return jnp.concatenate(
        [jnp.where(lower, piece, other), jnp.where(lower, other, piece)], axis=0
    ).astype(F32)


def cost(flops, bytes_accessed):
    return pl.CostEstimate(flops=flops, bytes_accessed=bytes_accessed, transcendentals=0)


LIMIT = pltpu.CompilerParams(vmem_limit_bytes=50 * 2**20)
ALONE = pltpu.CompilerParams(vmem_limit_bytes=60 * 2**20)


def part_kernel(order, split, count, *refs):
    lefts, rights, outs = refs[:count], refs[count : 2 * count], refs[2 * count :]
    total = 0.0
    for left, right in zip(lefts, rights):
        rows = left[...]
        total += dot(rows.reshape(rows.shape[-2:]), right[...], NT)
    half = outs[0].shape[0] // 2
    low = min(min(UPPER[at], LOWER[at]) for at in order)

    def put(outs):
        for at, out in zip(order, outs):
            for n, place in enumerate((UPPER[at] - low, LOWER[at] - low)):
                out[n * half : (n + 1) * half, :] = total[
                    place * half : (place + 1) * half
                ].astype(out.dtype)

    if not split:
        put(outs)
        return
    step, steps = pl.program_id(0), pl.num_programs(0)

    @pl.when(step < steps // 2)
    def first():
        put(outs[: len(order)])

    @pl.when(step >= steps // 2)
    def second():
        put(outs[len(order) :])


def part_products(order, dtypes, split, lefts, weights):
    row_total, feature = lefts[0][0].shape[-2], weights[0][0].shape[0]
    piece, block = row_total // 4, 256
    steps = feature // block
    rows, first_rows = (piece, 3) if order == (3,) else (len(order) * piece, 0)
    left_specs, right_specs = [], []
    flops = 0
    for (array, place), (weight, width, at) in zip(lefts, weights):
        if array.ndim == 2:
            left_specs.append(pl.BlockSpec((rows, width), lambda i, place=place: (first_rows, place)))
        else:
            left_specs.append(
                pl.BlockSpec((1, rows, width), lambda i, place=place: (place, first_rows, 0))
            )
        right_specs.append(pl.BlockSpec((block, width), lambda i, at=at: (i, at)))
        flops += 2 * rows * feature * width
    if split:
        outs = [pl.BlockSpec((piece, block), lambda i: (0, jnp.minimum(i, steps // 2 - 1)))] * len(order)
        outs += [pl.BlockSpec((piece, block), lambda i: (0, jnp.maximum(i - steps // 2, 0)))] * len(order)
    else:
        outs = [pl.BlockSpec((piece, block), lambda i: (0, i))] * len(order)
    return pl.pallas_call(
        lambda *refs: part_kernel(order, split, len(lefts), *refs),
        grid=(steps,),
        in_specs=left_specs + right_specs,
        out_specs=outs,
        out_shape=[
            jax.ShapeDtypeStruct((piece, feature // 2 if split else feature), dtype)
            for dtype in dtypes
        ],
        compiler_params=LIMIT,
        cost_estimate=cost(flops, flops // 500),
    )(*[a for a, unused in lefts], *[w for w, *unused in weights])


def row_kernel(left, right, out):
    width = right.shape[2]
    for n in range(2):
        out[:, n * width : (n + 1) * width] = dot(left[...], right[n], TN).astype(BF)


def row_products(left, right):
    row_total, feature = left.shape
    width, block = right.shape[2], 256
    flops = 4 * row_total * feature * width
    return pl.pallas_call(
        row_kernel,
        grid=(feature // block,),
        in_specs=[
            pl.BlockSpec((row_total, block), lambda i: (0, i)),
            pl.BlockSpec(right.shape, lambda i: (0, 0, 0)),
        ],
        out_specs=pl.BlockSpec((block, 2 * width), lambda i: (i, 0)),
        out_shape=jax.ShapeDtypeStruct((feature, 2 * width), BF),
        compiler_params=LIMIT,
        cost_estimate=cost(flops, flops // 500),
    )(left, right)


def turned_kernel(left, *refs):
    out, right = refs[8:]
    join(refs[:8], right)
    out[...] = dot(left[...], right[...], TN).astype(BF)


def turned_products(left, pieces):
    row_total, feature = left.shape[0], pieces[0].shape[1]
    width, block = left.shape[1], feature // 4
    flops = 2 * row_total * feature * width
    return pl.pallas_call(
        turned_kernel,
        grid=(4,),
        in_specs=[pl.BlockSpec((row_total, width), lambda i: (0, 0))]
        + [pl.BlockSpec((p.shape[0], block), lambda i: (0, i)) for p in pieces],
        out_specs=[
            pl.BlockSpec((width, block), lambda i: (i, 0)),
            pl.BlockSpec((row_total, block), lambda i: (0, i)),
        ],
        out_shape=[
            jax.ShapeDtypeStruct((4 * width, block), BF),
            jax.ShapeDtypeStruct((row_total, feature), BF),
        ],
        compiler_params=LIMIT,
        cost_estimate=cost(flops, flops // 500),
    )(left, *pieces)


def attn_kernel(h_ref, d_ref, g_ref, y_ref, *refs):
    out, z_ref = refs[8:]
    join(refs[:8], z_ref)
    total, width = d_ref.shape[1], y_ref.shape[1]
    normed = h_ref[...]
    out[:, :total] = dot(normed, d_ref[...], TN).astype(BF)
    out[:, total : total + width] = dot(normed, g_ref[...], TN).astype(BF)
    out[:, total + width :] = dot(y_ref[...], z_ref[...], TN).astype(BF)


def attn_products(first_normed, grad_first, grad_gate, pieces, gated):
    row_total, feature = first_normed.shape
    total, width = grad_first.shape[1], gated.shape[1]
    block = feature // 4

    def column(rows):
        return pl.BlockSpec((rows, block), lambda i: (0, i))

    def whole(columns):
        return pl.BlockSpec((row_total, columns), lambda i: (0, 0))

    return pl.pallas_call(
        attn_kernel,
        grid=(4,),
        in_specs=[column(row_total), whole(total), whole(width), whole(width)]
        + [column(p.shape[0]) for p in pieces],
        out_specs=pl.BlockSpec((block, total + 2 * width), lambda i: (i, 0)),
        out_shape=jax.ShapeDtypeStruct((feature, total + 2 * width), BF),
        scratch_shapes=[pltpu.VMEM((row_total, block), BF)],
        compiler_params=LIMIT,
        cost_estimate=cost(2 * row_total * feature * (total + 2 * width), 16 * 2**20),
    )(first_normed, grad_first, grad_gate, gated, *pieces)


def place_kernel(at, *refs):
    ins, outs = refs[:4], refs[4:]
    width, half = ins[0].shape[1], outs[0].shape[0]
    for k in range(4):
        columns = pl.ds(pl.multiple_of((at[0] ^ k) * width, LANES), width)
        for n, out in enumerate(outs):
            out[:, columns] = ins[k][n * half : (n + 1) * half, :]


def placed(pieces, start):
    rows, width = pieces[0].shape
    return pl.pallas_call(
        place_kernel,
        grid_spec=pltpu.PrefetchScalarGridSpec(
            num_scalar_prefetch=1,
            grid=(1,),
            in_specs=[pl.BlockSpec((rows, width), lambda i, at: (0, 0))] * 4,
            out_specs=[pl.BlockSpec((rows // 2, 4 * width), lambda i, at: (0, 0))] * 2,
        ),
        out_shape=[jax.ShapeDtypeStruct((rows // 2, 4 * width), BF)] * 2,
        compiler_params=ALONE,
        cost_estimate=cost(1, 4 * 2**20),
    )(start.astype(jnp.int32)[None], *pieces)


def reorder_kernel(at, *refs):
    count = len(refs) // 4 - 1
    width = refs[0].shape[1]
    for k in range(4):
        for n in range(4):

            @pl.when((at[0] ^ k) == n)
            def copy(k=k, n=n):
                for m in range(count):
                    refs[4 * count + k][:, m * width : (m + 1) * width] = refs[4 * m + n][...]


def reordered(sets, start):
    rows, width = sets[0][0].shape
    total = width * len(sets)
    return pl.pallas_call(
        reorder_kernel,
        grid_spec=pltpu.PrefetchScalarGridSpec(
            num_scalar_prefetch=1,
            grid=(1,),
            in_specs=[pl.BlockSpec((rows, width), lambda i, at: (0, 0))] * (4 * len(sets)),
            out_specs=[pl.BlockSpec((rows, total), lambda i, at: (0, 0))] * 4,
        ),
        out_shape=[jax.ShapeDtypeStruct((rows, total), BF)] * 4,
        compiler_params=ALONE,
        cost_estimate=cost(1, 4 * 2**20),
    )(start.astype(jnp.int32)[None], *[p for pieces in sets for p in pieces])


def half_sums(parts):
    a0, a1, a2, b0, b1, b2 = (p[...].astype(F32) for p in parts)
    return jnp.concatenate([a0 + a1 + a2, b0 + b1 + b2], axis=1)


def mean_scale(rows):
    return lax.rsqrt(jnp.mean(rows * rows, axis=1, keepdims=True) + EPSILON)


def norm_backward(grad, rows, gain):
    scale = mean_scale(rows)
    normed = rows * scale
    grad_normed = grad * gain
    inner = jnp.mean(grad_normed * normed, axis=1, keepdims=True)
    return scale * (grad_normed - normed * inner)


def put_halves(value, top, low):
    step = pl.program_id(0)

    @pl.when(step == 0)
    def first():
        top[...] = value

    @pl.when(step == 1)
    def second():
        low[...] = value


def put_quarters(lane, value, outs, held):
    held[...] = value
    width = outs[0].shape[1]
    for k, out in enumerate(outs):
        out[...] = held[:, pl.ds(pl.multiple_of((lane ^ k) * width, LANES), width)]


def either(top, low):
    return jnp.where(pl.program_id(0) == 0, top[...].astype(F32), low[...].astype(F32))


def up_norm_kernel(where, x_top, x_low, gain_ref, *refs):
    second = either(x_top, x_low) + half_sums(refs[:6])
    refs[6][...] = second
    put_halves((second * mean_scale(second) * gain_ref[1:2, :]).astype(BF), refs[7], refs[8])


def down_norm_kernel(where, second_ref, grad_top, grad_low, gain_ref, *refs):
    grad = either(grad_top, grad_low) + norm_backward(
        half_sums(refs[:6]), second_ref[...], gain_ref[1:2, :]
    )
    refs[6][...] = grad
    put_halves(grad.astype(BF), refs[7], refs[8])


def result_kernel(where, second_ref, own_ref, one, two, three, *refs):
    result = second_ref[...] + own_ref[...]
    for part in (one, two, three):
        result += part[...].astype(F32)
    put_quarters(where[2], result.astype(BF), refs[:4], refs[4])


def input_norm_kernel(where, x_top, x_low, grad_ref, gain_ref, *refs):
    grad = grad_ref[...] + norm_backward(
        half_sums(refs[:6]), either(x_top, x_low), gain_ref[0:1, :]
    )
    put_quarters(where[2], grad.astype(BF), refs[6:10], refs[10])


def on_rows(kernel, where, rows, gains, parts, quarters):
    feature = 2 * parts[0].shape[1] if parts else rows[0].shape[1]
    row_total = rows[-1].shape[0] if not parts else parts[0].shape[0]
    block = row_total // 2

    def spec(width):
        return pl.BlockSpec((block, width), lambda i, *_: (i, 0))

    top = low = pl.BlockSpec((block, feature), lambda i, *_: (0, 0))
    ins, args = [], []
    for r in rows:
        if isinstance(r, (list, tuple)):
            ins += [top, low]
            args += list(r)
        else:
            ins.append(spec(feature))
            args.append(r)
    if gains is not None:
        ins.append(pl.BlockSpec(gains.shape, lambda i, *_: (0, 0)))
    ins += [spec(feature // 2)] * len(parts)
    if quarters:
        outs = [spec(feature // 4)] * 4
        shapes = [jax.ShapeDtypeStruct((row_total, feature // 4), BF)] * 4
        scratch = [pltpu.VMEM((block, feature), BF)]
    else:
        outs = [spec(feature), top, low]
        shapes = [jax.ShapeDtypeStruct((row_total, feature), F32)]
        shapes += [jax.ShapeDtypeStruct((block, feature), BF)] * 2
        scratch = []
    return pl.pallas_call(
        kernel,
        grid_spec=pltpu.PrefetchScalarGridSpec(
            num_scalar_prefetch=1,
            grid=(2,),
            in_specs=ins,
            out_specs=outs,
            scratch_shapes=scratch,
        ),
        out_shape=shapes,
        compiler_params=ALONE,
        cost_estimate=cost(1, 6 * 2**20),
    )(where, *args, *([] if gains is None else [gains]), *parts)


def first_kernel(heads, pieces, w_ref, v_ref, wf_ref, b_ref, h_ref, qkv_ref, keep_ref, slope_ref, gain_ref):
    step = pl.program_id(0)

    @pl.when(step == 0)
    def norm():
        turned = wf_ref[...].astype(F32).T
        for n in range(2):
            first = heads + 3 * n
            gain_ref[n : n + 1, :] = (
                turned[first : first + 1] + turned[first + 1 : first + 2] + turned[first + 2 : first + 3]
            )
        block = pieces[0].shape[0]
        for at, piece in enumerate(pieces):
            x = piece[...].astype(F32)
            h_ref[pl.ds(at * block, block), :] = (x * mean_scale(x) * gain_ref[0:1, :]).astype(BF)

    @pl.when(step < 3)
    def query_key():
        qkv_ref[...] = dot(h_ref[...], w_ref[...]).astype(BF)

    @pl.when(step >= 3)
    def value_forget():
        pre = dot(h_ref[...], v_ref[...])
        qkv_ref[...] = pre.astype(BF)

        @pl.when(step == 4)
        def forget():
            real = lanes_of(pre.shape[0]) < heads
            forget_pre = jnp.where(real, pre[:, LANES:] + b_ref[...], 0.0)
            less = jnp.exp(-jnp.abs(forget_pre))
            keep_ref[...] = jnp.minimum(forget_pre, 0.0) - jnp.log1p(less)
            slope_ref[...] = jnp.where(
                real, jnp.where(forget_pre >= 0, less, 1.0) / (1.0 + less), 0.0
            )


def first_products(heads, pieces, weights, bias):
    row_total, feature = 8 * pieces[0].shape[0], pieces[0].shape[1]
    block = 256

    def whole_block(shape):
        return pl.BlockSpec(shape, lambda i: (0, 0))

    def kernel(*refs):
        first_kernel(heads, refs[:8], *refs[8:])

    return pl.pallas_call(
        kernel,
        grid=(5,),
        in_specs=[whole_block(p.shape) for p in pieces]
        + [
            pl.BlockSpec((feature, block), lambda i: (0, jnp.minimum(i, 2))),
            pl.BlockSpec((feature, block), lambda i: (0, jnp.maximum(i - 3, 0))),
            pl.BlockSpec((feature, LANES), lambda i: (0, 3)),
            whole_block((1, LANES)),
        ],
        out_specs=[
            whole_block((row_total, feature)),
            pl.BlockSpec((row_total, block), lambda i: (0, i)),
            whole_block((row_total, LANES)),
            whole_block((row_total, LANES)),
            whole_block((8, feature)),
        ],
        out_shape=[
            jax.ShapeDtypeStruct((row_total, feature), BF),
            jax.ShapeDtypeStruct((row_total, 5 * block), BF),
            jax.ShapeDtypeStruct((row_total, LANES), F32),
            jax.ShapeDtypeStruct((row_total, LANES), F32),
            jax.ShapeDtypeStruct((8, feature), F32),
        ],
        compiler_params=ALONE,
        cost_estimate=cost(10 * row_total * feature * block, 12 * 2**20),
    )(*pieces, weights[0], weights[1], weights[1], bias)


def gate_kernel(h_ref, w_ref, att_ref, gate_ref, y_ref):
    gate = jax.nn.sigmoid(dot(h_ref[...], w_ref[...]))
    gate_ref[...] = gate
    y_ref[...] = (att_ref[...] * gate).astype(BF)


def gate_products(first_normed, weights, attended):
    row_total, feature = first_normed.shape
    width = attended.shape[1]

    def by_rows(columns):
        return pl.BlockSpec((row_total // 4, columns), lambda i: (i, 0))

    return pl.pallas_call(
        gate_kernel,
        grid=(4,),
        in_specs=[
            by_rows(feature),
            pl.BlockSpec((feature, width), lambda i: (0, 0)),
            by_rows(width),
        ],
        out_specs=[by_rows(width)] * 2,
        out_shape=[
            jax.ShapeDtypeStruct((row_total, width), F32),
            jax.ShapeDtypeStruct((row_total, width), BF),
        ],
        compiler_params=LIMIT,
        cost_estimate=cost(2 * row_total * feature * width, 10 * 2**20),
    )(first_normed, weights, attended)


def join(pieces, whole):
    block = pieces[0].shape[0]
    for at, piece in enumerate(pieces):
        whole[pl.ds(at * block, block), :] = piece[...]


def up_kernel(*refs):
    pieces, g_ref, u_ref = refs[:4], refs[4], refs[5]
    h_ref, m_ref, to_gate_ref, to_up_ref = refs[-4:]

    @pl.when(pl.program_id(0) == 0)
    def first():
        join(pieces, h_ref)

    gate = dot(h_ref[...], g_ref[...])
    up = dot(h_ref[...], u_ref[...])
    sig = jax.nn.sigmoid(gate)
    silu = gate * sig
    m_ref[...] = (silu * up).astype(BF)
    to_gate_ref[...] = (up * sig * (1.0 + gate * (1.0 - sig))).astype(to_gate_ref.dtype)
    to_up_ref[...] = silu.astype(to_up_ref.dtype)


def up_products(half, held, pieces, weights):
    rows, feature = 4 * pieces[0].shape[0], pieces[0].shape[1]
    hidden, block = weights.shape[1] // 2, 256
    steps = hidden // block
    return pl.pallas_call(
        up_kernel,
        grid=(steps,),
        in_specs=[pl.BlockSpec(p.shape, lambda i: (0, 0)) for p in pieces]
        + [
            pl.BlockSpec((feature, block), lambda i: (0, i)),
            pl.BlockSpec((feature, block), lambda i: (0, steps + i)),
        ]
        + [pl.BlockSpec(memory_space=pl.ANY)] * len(held),
        out_specs=[pl.BlockSpec((rows, feature), lambda i: (half, 0))]
        + [pl.BlockSpec((rows, block), lambda i: (half, i))] * 3,
        out_shape=[jax.ShapeDtypeStruct((2 * rows, feature), BF)]
        + [jax.ShapeDtypeStruct((2 * rows, hidden), BF)] * 3,
        input_output_aliases={6 + n: n for n in range(len(held))},
        compiler_params=ALONE,
        cost_estimate=cost(4 * rows * feature * hidden, 16 * 2**20),
    )(*pieces, weights, weights, *held)


def down_kernel(g_ref, w_ref, to_gate_ref, to_up_ref, out_ref):
    grad = dot(g_ref[...], w_ref[...])
    out_ref[0] = (grad * to_gate_ref[...]).astype(BF)
    out_ref[1] = (grad * to_up_ref[...]).astype(BF)


def down_products(grad_out, weights, to_gate, to_up):
    row_total, feature = grad_out.shape
    hidden, block = weights.shape[1], 256
    column = pl.BlockSpec((row_total, block), lambda i: (0, i))
    return pl.pallas_call(
        down_kernel,
        grid=(hidden // block,),
        in_specs=[
            pl.BlockSpec((row_total, feature), lambda i: (0, 0)),
            pl.BlockSpec((feature, block), lambda i: (0, i)),
            column,
            column,
        ],
        out_specs=pl.BlockSpec((2, row_total, block), lambda i: (0, 0, i)),
        out_shape=jax.ShapeDtypeStruct((2, row_total, hidden), BF),
        compiler_params=LIMIT,
        cost_estimate=cost(2 * row_total * feature * hidden, 16 * 2**20),
    )(grad_out, weights, to_gate, to_up)


def back_kernel(*refs):
    pieces, (w_ref, gate_ref, att_ref, datt_ref, dgate_ref, z_ref) = refs[:8], refs[8:]
    block = pieces[0].shape[0]
    for at in range(4):

        @pl.when(pl.program_id(0) == at)
        def put(at=at):
            z_ref[:block, :] = pieces[2 * at][...]
            z_ref[block:, :] = pieces[2 * at + 1][...]

    grad = dot(z_ref[...], w_ref[...])
    gate = gate_ref[...]
    datt_ref[...] = (grad * gate).astype(BF)
    dgate_ref[...] = (grad * att_ref[...] * gate * (1.0 - gate)).astype(BF)


def back_products(pieces, weights, gate, attended):
    row_total, feature = 8 * pieces[0].shape[0], pieces[0].shape[1]
    width = attended.shape[1]

    def spec(shape, at=0):
        return pl.BlockSpec(shape, lambda i: (0, at))

    def by_rows(columns):
        return pl.BlockSpec((row_total // 4, columns), lambda i: (i, 0))

    return pl.pallas_call(
        back_kernel,
        grid=(4,),
        in_specs=[spec(p.shape) for p in pieces]
        + [spec((feature, width), 1), by_rows(width), by_rows(width)],
        out_specs=[by_rows(width)] * 2,
        out_shape=[jax.ShapeDtypeStruct((row_total, width), BF)] * 2,
        scratch_shapes=[pltpu.VMEM((row_total // 4, feature), BF)],
        compiler_params=ALONE,
        cost_estimate=cost(2 * row_total * feature * width, 10 * 2**20),
    )(*pieces, weights, gate, attended)


def slot_tables(lengths, dealing, stream):
    width = lengths.shape[1]
    given, slot_of = [], []
    start = jnp.int32(0)
    for g in range(width):
        given.append(start)
        start = start + lengths[stream, g]
        slot_of.append(dealing[stream, g])
    dealt, given_at = [], []
    start = jnp.int32(0)
    for k in range(width):
        dealt.append(start)
        here = jnp.int32(0)
        for g in range(width):
            here = jnp.where(slot_of[g] == k, given[g], here)
            start = start + jnp.where(slot_of[g] == k, lengths[stream, g], 0)
        given_at.append(here)
    return given, slot_of, dealt, given_at


def pick_kernel(backward, where, lengths, dealing, *refs):
    column, row = where[0], where[1]
    block = refs[0].shape[0] // (1 if backward else 4)
    row_total = 4 * block
    step = pl.program_id(0)
    given, slot_of, dealt, given_at = slot_tables(lengths, dealing, column)
    within = lax.broadcasted_iota(jnp.int32, (block, 1), 0)
    if backward:
        places = row * row_total + step * block + within
        moves = []
        for g in range(len(given)):
            there = jnp.int32(0)
            for k in range(len(given)):
                there = jnp.where(slot_of[g] == k, dealt[k], there)
            moves.append((given[g], there - given[g]))
    else:
        places = row * row_total + (step ^ column) * block + within
        moves = [(s, g - s) for s, g in zip(dealt, given_at)]
    move = jnp.zeros_like(places) + moves[0][1]
    for first, by in moves[1:]:
        move = jnp.where(places >= first, by, move)
    near = places + move - row * row_total
    near = jnp.where(near < 0, near + 2 * row_total, near)
    if backward:
        other = jnp.where(near >= row_total, row_total, 0)
        local = near - other
        part = sum(jnp.where(local >= k * block, 1, 0) for k in (1, 2, 3))
        near = other + local + (jnp.bitwise_xor(part, column) - part) * block
    start = row * row_total + (step if backward else step ^ column) * block
    held = refs[-1]
    held[...] = jnp.zeros_like(held)
    across = lax.broadcasted_iota(jnp.int32, (block, block), 1)
    for part in range(8):
        if backward:
            place = 4 * ((part // 4) ^ row) + ((part % 4) ^ column)
        else:
            place = (part + 4 * row) & 7
        met = jnp.bool_(False)
        for n, (first, by) in enumerate(moves):
            low = jnp.maximum(start, first) + by
            high = start + block
            if n + 1 < len(moves):
                high = jnp.minimum(high, moves[n + 1][0])
            high = high + by
            met |= (low < high) & (low < (place + 1) * block) & (high > place * block)

        @pl.when(met)
        def add(part=part):
            chosen = jnp.where(across == near - part * block, 1.0, 0.0).astype(BF)
            if backward:
                held[...] += dot(chosen, refs[part][...])
            else:
                rows = pl.ds(part % 4 * block, block)
                width = refs[0].shape[1]
                for at in range(2):
                    held[:, at * width : (at + 1) * width] += dot(
                        chosen, refs[2 * at + part // 4][rows, :]
                    )

    if backward:
        refs[8][...] = held[...].astype(BF)
        return
    width = refs[0].shape[1]
    for at in range(2):
        for k in range(4):

            @pl.when(step == k)
            def put(k=k, at=at):
                refs[4 + 4 * at + k][...] = held[:, at * width : (at + 1) * width].astype(BF)


def moved_rows(backward, where, lengths, dealing, arrays):
    if backward:
        block, width = arrays[0].shape
        row_total = 4 * block
    else:
        row_total, width = arrays[0].shape
        block = row_total // 4
    if lax.axis_size("dp") != 2:
        column, row = where[0], where[1]
        local = jnp.arange(row_total, dtype=jnp.int32)
        own_lengths = lax.dynamic_index_in_dim(lengths, column, 0, keepdims=False)
        own_dealing = lax.dynamic_index_in_dim(dealing, column, 0, keepdims=False)
        if backward:
            to = given_targets(own_lengths, own_dealing, row * row_total + local)
            at = to % row_total
            to = to - at + ((at // block) ^ column) * block + at % block
            arrays = [jnp.concatenate(arrays, axis=0)]
        else:
            swapped = (((local // block) ^ column) * block) + local % block
            to = dealt_sources(own_lengths, own_dealing, row * row_total + swapped)
        moved = [jnp.take(lax.all_gather(a, "dp", axis=0, tiled=True), to, axis=0) for a in arrays]
        if backward:
            return moved
        return [m[k * block : (k + 1) * block] for m in moved for k in range(4)]
    others = [swap(a, "dp", 1) for a in arrays]
    if backward:
        outs = [pl.BlockSpec((block, width), lambda i, *_: (i, 0))]
        shapes = [jax.ShapeDtypeStruct((row_total, width), BF)]
        ins = [*arrays, *others]
    else:
        outs = [pl.BlockSpec((block, width), lambda i, *_: (0, 0))] * 8
        shapes = [jax.ShapeDtypeStruct((block, width), BF)] * 8
        ins = [arrays[0], others[0], arrays[1], others[1]]
    return pl.pallas_call(
        lambda *refs: pick_kernel(backward, *refs),
        grid_spec=pltpu.PrefetchScalarGridSpec(
            num_scalar_prefetch=3,
            grid=(4,),
            in_specs=[pl.BlockSpec(a.shape, lambda i, *_: (0, 0)) for a in ins],
            out_specs=outs,
            scratch_shapes=[pltpu.VMEM((block, width if backward else 2 * width), F32)],
        ),
        out_shape=shapes,
        compiler_params=pltpu.CompilerParams(vmem_limit_bytes=40 * 2**20),
        cost_estimate=cost(16 * row_total * row_total * width, 8 * 2**20),
    )(where, lengths, dealing, *ins)


def piece_rows(piece, half):
    rows = []
    for places in (UPPER, LOWER):
        place = jnp.int32(places[0])
        for k in (1, 2, 3):
            place = jnp.where(piece == k, places[k], place)
        rows.append(pl.ds(pl.multiple_of(place * half, half), half))
    return rows


def get_rows(ref, rows):
    return jnp.concatenate([ref[part, :] for part in rows], axis=0)


def put_rows(ref, rows, columns, value):
    half = value.shape[0] // 2
    for n, part in enumerate(rows):
        ref[part, columns] = value[n * half : (n + 1) * half]


def lanes_of(rows):
    return lax.broadcasted_iota(jnp.int32, (rows, LANES), 1)


COLUMN_SUM, ROW_SUM, SECOND = 16, 32, 24


def parts_of(values):
    one = values.astype(BF).astype(F32)
    two = (values - one).astype(BF).astype(F32)
    return one, two, values - one - two


def packed(values):
    one, two, three = parts_of(values)
    return one + pltpu.roll(two, 8, 1) + pltpu.roll(three, 16, 1)


def ordered_sums(ones, values):
    sums = dot(ones, jnp.concatenate(parts_of(values), axis=1).astype(BF))
    return sums[:, :LANES] + sums[:, LANES : 2 * LANES] + sums[:, 2 * LANES :]


def at_lane(lanes, base, offsets, value, rest):
    for offset in offsets:
        rest = jnp.where(lanes == base + offset, value, rest)
    return rest


def forward_kernel(
    where,
    lengths,
    dealing,
    q_ref,
    k_ref,
    v_ref,
    keep_ref,
    att_ref,
    qa_ref,
    ka_ref,
    log_ref,
    c_ref,
    va_ref,
):
    pair = pl.program_id(0)
    column, row, lane = where[0], where[1], where[2]
    first_length = jnp.int32(0)
    for g in range(lengths.shape[1]):
        first_length += jnp.where(dealing[lane, g] == 2 * row, lengths[lane, g], 0)
    row_total = q_ref.shape[0]
    block = row_total // 4
    lanes = lanes_of(block)

    def rows_of(at):
        return piece_rows(column ^ at, block // 2)

    @pl.when(pair == 0)
    def sum_keeps():
        below = lax.broadcasted_iota(jnp.int32, (block, block), 0)
        across = lax.broadcasted_iota(jnp.int32, (block, block), 1)
        ones = jnp.where(below >= across, 1.0, 0.0).astype(BF)
        running = jnp.zeros((1, LANES), F32)
        log_ref[...] = jnp.zeros_like(log_ref)
        for at in range(4):
            own = pl.ds(at * block, block)
            keeps = jnp.where(
                lanes < 2 * pl.num_programs(0), get_rows(keep_ref, rows_of(at)), 0.0
            )
            sums = running + ordered_sums(ones, keeps)
            running = sums[block - 1 :, :]
            places = at * block + lax.broadcasted_iota(jnp.int32, (block, LANES), 0)
            second = jnp.where((places >= first_length) & (lanes == SECOND), 1.0, 0.0)
            c_ref[own, :] = (packed(sums) + second).astype(BF)

    source = lax.broadcasted_iota(jnp.int32, (LANES, 2 * LANES), 0)
    target = lax.broadcasted_iota(jnp.int32, (LANES, 2 * LANES), 1)
    one_row = lax.broadcasted_iota(jnp.int32, (1, LANES), 1)
    for head in range(2):
        number = 2 * pair + head
        mine = (lanes < 64) if head == 0 else (lanes >= 64)
        base = 64 if head == 0 else 0
        moves = jnp.zeros((LANES, 2 * LANES), F32)
        for part in range(3):
            moves = jnp.where(
                (source == 8 * part + number) & (target == base + part), -1.0, moves
            )
        moves = jnp.where((source == SECOND) & (target == base + 3), FAR, moves)
        moves = jnp.where((source == SECOND) & (target == LANES + base + 3), 1.0, moves).astype(BF)
        k_ones = at_lane(one_row, base, (4, 5, 6, ROW_SUM + number), 1.0, 0.0)
        k_ones = at_lane(one_row, base, (3,), -FAR, k_ones)
        q_ones = at_lane(one_row, base, (0, 1, 2, COLUMN_SUM + number), 1.0, 0.0)
        for at in range(4):
            rows, own = rows_of(at), pl.ds(at * block, block)
            sides = dot(c_ref[own, :], moves)
            qa_ref[head, own, :] = jnp.where(
                mine, get_rows(q_ref, rows).astype(F32) * 0.125, sides[:, LANES:] + q_ones
            ).astype(BF)
            ka_ref[head, own, :] = jnp.where(
                mine, get_rows(k_ref, rows).astype(F32), sides[:, :LANES] + k_ones
            ).astype(BF)
            va_ref[head, own, :] = jnp.where(mine, get_rows(v_ref, rows).astype(F32), 1.0).astype(BF)

    below = lax.broadcasted_iota(jnp.int32, (block, block), 0)
    across = lax.broadcasted_iota(jnp.int32, (block, block), 1)
    for at in range(4):
        own = pl.ds(at * block, block)
        width = (at + 1) * block
        results = []
        logs = log_ref[own, :]
        for head in range(2):
            queries = qa_ref[head, own, :]
            last = jnp.where(
                below >= across, dot(queries, ka_ref[head, at * block : width, :], NT), -FAR
            )
            top = jnp.max(last, axis=1, keepdims=True)
            if at > 0:
                early = dot(queries, ka_ref[head, : at * block, :], NT)
                top = jnp.maximum(top, jnp.max(early, axis=1, keepdims=True))
            total = dot(jnp.exp(last - top).astype(BF), va_ref[head, at * block : width, :])
            if at > 0:
                total += dot(jnp.exp(early - top).astype(BF), va_ref[head, : at * block, :])
            results.append(total / pltpu.roll(total, 64, 1))
            kept = 64 * (1 - head) + 2 * pair + head
            logs = jnp.where(lanes == kept, top + jnp.log(total), logs)
        log_ref[own, :] = logs
        attended = jnp.where(lanes < 64, results[0], results[1])
        put_rows(att_ref, rows_of(at), slice(None), attended)


def attend_forward(where, lengths, dealing, qkv, keep):
    row_total, width = qkv.shape[0], qkv.shape[1] // LANES // 3 * LANES
    pairs = width // LANES
    heads = 2 * pairs

    def columns(first):
        return pl.BlockSpec((row_total, LANES), lambda p, *_: (0, first + p))

    sided = pl.BlockSpec((2, row_total, LANES), lambda p, *_: (p, 0, 0))
    return pl.pallas_call(
        forward_kernel,
        grid_spec=pltpu.PrefetchScalarGridSpec(
            num_scalar_prefetch=3,
            grid=(pairs,),
            in_specs=[
                columns(0),
                columns(pairs),
                columns(2 * pairs),
                pl.BlockSpec((row_total, LANES), lambda p, *_: (0, 0)),
            ],
            out_specs=[
                columns(0),
                sided,
                sided,
                pl.BlockSpec((row_total, LANES), lambda p, *_: (0, 0)),
            ],
            scratch_shapes=[
                pltpu.VMEM((row_total, LANES), BF),
                pltpu.VMEM((2, row_total, LANES), BF),
            ],
        ),
        out_shape=[
            jax.ShapeDtypeStruct((row_total, width), F32),
            jax.ShapeDtypeStruct((heads, row_total, LANES), BF),
            jax.ShapeDtypeStruct((heads, row_total, LANES), BF),
            jax.ShapeDtypeStruct((row_total, LANES), F32),
        ],
        compiler_params=pltpu.CompilerParams(vmem_limit_bytes=60 * 2**20),
        cost_estimate=cost(10 * 10**9, 8 * 2**20),
    )(where, lengths, dealing, qkv, qkv, qkv, keep)


def backward_kernel(
    where,
    qa_ref,
    ka_ref,
    log_ref,
    v_ref,
    datt_ref,
    att_ref,
    slope_ref,
    out_ref,
    l_ref,
    qf_ref,
    va_ref,
    da_ref,
    kt_ref,
    dk_ref,
    dv_ref,
    dq_ref,
    row_ref,
    column_ref,
):
    pair = pl.program_id(0)
    pairs = pl.num_programs(0)
    column = where[0]
    row_total = v_ref.shape[0]
    block = row_total // 4
    lanes = lanes_of(block)
    width = att_ref.shape[1] * pairs

    def rows_of(at):
        return piece_rows(column ^ at, block // 2)

    def lanes_at(group):
        return pl.ds(pl.multiple_of((group * pairs + pair) * LANES, LANES), LANES)

    @pl.when(pair == 0)
    def start():
        row_ref[...] = jnp.zeros_like(row_ref)
        column_ref[...] = jnp.zeros_like(column_ref)
        for at in range(4):
            own = pl.ds(at * block, block)
            l_ref[own, :] = packed(log_ref[own, :]).astype(BF)

    source = lax.broadcasted_iota(jnp.int32, (LANES, LANES), 0)
    target = lax.broadcasted_iota(jnp.int32, (LANES, LANES), 1)
    halves_at = lax.broadcasted_iota(jnp.int32, (2 * LANES, 2 * LANES), 0) & (LANES - 1)
    sums_at = lax.broadcasted_iota(jnp.int32, (2 * LANES, 2 * LANES), 1)
    halves = jnp.where((halves_at < 64) == (sums_at < LANES), 1.0, 0.0).astype(BF)
    moves = []
    for head in range(2):
        kept = 64 * (1 - head) + 2 * pair + head
        base = 64 if head == 0 else 0
        move = jnp.zeros((LANES, LANES), F32)
        for part in range(3):
            move = jnp.where((source == kept + 8 * part) & (target == base + 4 + part), -1.0, move)
        moves.append(move.astype(BF))

    for at in range(4):
        rows, own = rows_of(at), pl.ds(at * block, block)
        grad_att = get_rows(datt_ref, rows).astype(F32)
        inner = grad_att * get_rows(att_ref, rows)
        high = inner.astype(BF)
        rest = (inner - high.astype(F32)).astype(BF)
        deltas = dot(jnp.concatenate([high, rest], axis=1), halves)
        values = get_rows(v_ref, rows).astype(F32)
        for head in range(2):
            mine = (lanes < 64) if head == 0 else (lanes >= 64)
            base = 64 if head == 0 else 0
            one, two, three = parts_of(deltas[:, head * LANES : (head + 1) * LANES])
            side = jnp.where(lanes == base, -one, 0.0)
            side = jnp.where(lanes == base + 1, -two, side)
            side = jnp.where(lanes == base + 2, -three, side)
            da_ref[head, own, :] = jnp.where(mine, grad_att, side).astype(BF)
            va_ref[head, own, :] = jnp.where(
                mine, values, jnp.where((lanes >= base) & (lanes < base + 3), 1.0, 0.0)
            ).astype(BF)
            qf_ref[head, own, :] = (
                qa_ref[head, own, :].astype(F32) + dot(l_ref[own, :], moves[head])
            ).astype(BF)

    below = lax.broadcasted_iota(jnp.int32, (block, block), 0)
    across = lax.broadcasted_iota(jnp.int32, (block, block), 1)
    for head in range(2):
        for at in range(4):
            own = pl.ds(at * block, block)
            kt_ref[:, own] = ka_ref[head, own, :].astype(F32).T.astype(BF)
        for at in reversed(range(4)):
            own = pl.ds(at * block, block)
            queries, grads = qf_ref[head, own, :], da_ref[head, own, :]
            dq_t = jnp.zeros((LANES, block), F32)
            spans = [pl.ds(at * block, block)]
            if at > 0:
                spans.append(pl.ds(0, at * block))
            for n, keys in enumerate(spans):
                probs = jnp.exp(dot(ka_ref[head, keys, :], queries, NT))
                if n == 0:
                    probs = jnp.where(below <= across, probs, 0.0)
                grad_scores = (probs * dot(va_ref[head, keys, :], grads, NT)).astype(BF)
                dv = dot(probs.astype(BF), grads)
                dk = dot(grad_scores, queries)
                dq_t += dot(kt_ref[:, keys], grad_scores)
                if at == 3:
                    dv_ref[head, keys, :] = dv
                    dk_ref[head, keys, :] = dk
                else:
                    dv_ref[head, keys, :] += dv
                    dk_ref[head, keys, :] += dk
            dq_ref[head, own, :] = dq_t.T

    for at in range(4):
        rows, own = rows_of(at), pl.ds(at * block, block)
        for head in range(2):
            lane = 64 * (1 - head) + 2 * pair + head
            row_ref[own, :] += jnp.where(lanes == lane + ROW_SUM, dq_ref[head, own, :], 0.0)
            column_ref[own, :] += jnp.where(lanes == lane + COLUMN_SUM, dk_ref[head, own, :], 0.0)
        left = lanes < 64
        for group, ref, scale in ((0, dq_ref, 0.125), (1, dk_ref, 1.0), (2, dv_ref, 1.0)):
            both = jnp.where(left, ref[0, own, :], ref[1, own, :])
            put_rows(out_ref, rows, lanes_at(group), (both * scale).astype(BF))

    @pl.when(pair == pairs - 1)
    def finish():
        ones = jnp.where(below <= across, 1.0, 0.0).astype(BF)
        running = jnp.zeros((1, LANES), F32)
        for at in reversed(range(4)):
            own = pl.ds(at * block, block)
            change = pltpu.roll(row_ref[own, :], LANES - ROW_SUM, 1)
            change = change - pltpu.roll(column_ref[own, :], LANES - COLUMN_SUM, 1)
            change = jnp.where(lanes < 2 * pairs, change + pltpu.roll(change, 64, 1), 0.0)
            sums = running + ordered_sums(ones, change)
            running = sums[:1, :]
            rows = rows_of(at)
            put_rows(
                out_ref,
                rows,
                slice(3 * width, None),
                (sums * get_rows(slope_ref, rows)).astype(BF),
            )


def attend_backward(where, qa, ka, logs, qkv, grad_att, attended, slope):
    row_total, width = attended.shape
    pairs = width // LANES
    heads = 2 * pairs
    total = 3 * width + LANES

    def columns(first):
        return pl.BlockSpec((row_total, LANES), lambda p, *_: (0, first + p))

    sided = pl.BlockSpec((2, row_total, LANES), lambda p, *_: (p, 0, 0))
    both = (2, row_total, LANES)
    return pl.pallas_call(
        backward_kernel,
        grid_spec=pltpu.PrefetchScalarGridSpec(
            num_scalar_prefetch=1,
            grid=(pairs,),
            in_specs=[
                sided,
                sided,
                pl.BlockSpec((row_total, LANES), lambda p, *_: (0, 0)),
                columns(2 * pairs),
                columns(0),
                columns(0),
                pl.BlockSpec((row_total, LANES), lambda p, *_: (0, 0)),
            ],
            out_specs=pl.BlockSpec((row_total, total), lambda p, *_: (0, 0)),
            scratch_shapes=[
                pltpu.VMEM((row_total, LANES), BF),
                pltpu.VMEM(both, BF),
                pltpu.VMEM(both, BF),
                pltpu.VMEM(both, BF),
                pltpu.VMEM((LANES, row_total), BF),
                pltpu.VMEM(both, F32),
                pltpu.VMEM(both, F32),
                pltpu.VMEM(both, F32),
                pltpu.VMEM((row_total, LANES), F32),
                pltpu.VMEM((row_total, LANES), F32),
            ],
        ),
        out_shape=jax.ShapeDtypeStruct((row_total, total), BF),
        compiler_params=pltpu.CompilerParams(vmem_limit_bytes=60 * 2**20),
        cost_estimate=cost(12 * 10**9, 8 * 2**20),
    )(where, qa, ka, logs, qkv, grad_att, attended, slope)


def on_device(
    x_given,
    cotangent,
    seq_lengths,
    seq_deal,
    attn_gain,
    w_query,
    w_key,
    w_value,
    w_ogate,
    w_forget,
    b_forget,
    w_out,
    mlp_gain,
    w_gate,
    w_up,
    w_down,
):
    quarter = x_given.shape[1]
    piece = quarter // 4
    row, column, lane = lax.axis_index("dp"), lax.axis_index("tx"), lax.axis_index("ty")
    heads = w_forget.shape[1]
    width = w_query.shape[1]
    hidden = w_gate.shape[1]
    share = w_query.shape[0] // lax.axis_size("dp")

    def own_share(weights):
        return lax.dynamic_slice_in_dim(weights, row * share, share, axis=0)

    def whole(weights):
        return lax.all_gather(weights, ("ty", "dp"), axis=0, tiled=True)

    gains = jnp.stack(three_parts(attn_gain) + three_parts(mlp_gain), axis=1).astype(BF)
    spare = jnp.zeros((w_query.shape[0], LANES - heads - 6), BF)
    side = 3 * width
    last = side + LANES
    def side_by_side(*weights):
        return jnp.concatenate([own_share(w) for w in weights], axis=1)

    w_first = [whole(side_by_side(w_query, w_key))]

    where = jnp.stack([column, row, lane]).astype(jnp.int32)
    paired = lax.axis_size("dp") == 2

    dealt = moved_rows(False, where, seq_lengths, seq_deal, (x_given[0], cotangent[0]))
    x_parts, grad_parts = tie(spread_plane(dealt[:4]), dealt[4:])
    x_parts, grad_parts = tie(
        spread_line(reordered([x_parts], column ^ lane)), spread_plane(grad_parts)
    )
    grad_parts, x_parts = tie(reordered([grad_parts], column ^ lane), x_parts)
    w_first.append(whole(side_by_side(w_value, w_forget, gains, spare)))
    later = [side_by_side(w_ogate, w_out.T), side_by_side(w_gate, w_up)]
    x_parts, later, w_first[0] = tie(x_parts, later, w_first[0])
    w_second, w_gate_up = [whole(w) for w in later]
    grad_parts = spread_line(grad_parts)
    x_full, unused = gather_rows(*placed(x_parts, lane), ahead=(grad_parts[1], w_first[1]))

    bias = jnp.pad(b_forget, (0, LANES - heads))[None]
    first_normed, qkv, keep, slope, gains = first_products(heads, x_full, w_first, bias)
    grad_parts, qkv = tie(grad_parts, qkv)
    top, low = placed(grad_parts, lane)
    grad_rows = [top, low]
    qkv, top, low = tie(qkv, top, low)
    top_x, low_y = swap(top, "tx", 1), swap(low, "tx", 2)
    low_x, top_y = swap(low, "tx", 1), swap(top, "tx", 2)
    attended, qa, ka, logs = attend_forward(where, seq_lengths, seq_deal, qkv, keep)
    attended, top_x, low_y, low_x, top_y = tie(attended, top_x, low_y, low_x, top_y)
    top_d, low_d = swap(top_x, "tx", 2), swap(low_y, "tx", 1)
    grad_full = [top, low, top_x, low_y, low_x, top_y, top_d, low_d]
    w_down_t, attended = tie(own_share(w_down.T), attended)
    w_down_t = whole(w_down_t)
    out_gate, gated = gate_products(first_normed, w_second, attended)
    gated, grad_full[6:] = tie(gated, grad_full[6:])
    parts, unused = scatter_products([(gated, 0)], [(w_second, width, 1)])
    second, top, low = on_rows(up_norm_kernel, where, [x_full[:2]], gains, parts, False)

    def up_half(pieces, ahead):
        return up_products(0, [], pieces, w_gate_up)

    h2_parts, held = gather_rows(top, low, up_half)
    h2_full, mid, to_gate, to_up = up_products(1, held, h2_parts[4:], w_gate_up)
    part, grad_full = turned_products(mid, grad_full)
    part, grad_full = tie(part, grad_full)
    grads_down = summed(part)
    grad_gate_up = down_products(grad_full, w_down_t, to_gate, to_up)

    def gate_up_products(ready):
        left, unused = tie(h2_full, ready[0])
        return row_products(left, grad_gate_up)

    parts, part = scatter_products(
        [(grad_gate_up, 0), (grad_gate_up, 1)],
        [(w_gate_up, hidden, 0), (w_gate_up, hidden, 1)],
        gate_up_products,
    )
    part, parts = tie(part, parts)
    grads_gate_up = summed(part)
    grad_second, top, low = on_rows(
        down_norm_kernel, where, [second, grad_rows], gains, parts, False
    )

    def result_products(pieces, ahead):
        left, unused = tie(mid, pieces)
        return part_products(
            (1, 2, 3, 0), [BF, BF, BF, F32], False, [(left, 0)], [(w_down_t, hidden, 0)]
        )

    z_parts, (*sent, own) = gather_rows(top, low, result_products)

    sent = [swap(piece, "tx", k + 1) for k, piece in enumerate(sent)]
    grad_att, grad_ogate = back_products(z_parts, w_second, out_gate, attended)
    grad_first = attend_backward(where, qa, ka, logs, qkv, grad_att, attended, slope)
    grad_first, sent, grads_down = tie(grad_first, sent, grads_down)
    output = on_rows(result_kernel, where, [second, own, *sent], None, [], True)
    output, grad_first = tie(output, grad_first)
    output = spread_line(output)
    part = attn_products(first_normed, grad_first, grad_ogate, z_parts, gated)
    part, grad_first, output = tie(part, grad_first, output)
    grads_attn = summed(part)

    def given(pieces):
        return moved_rows(True, where, seq_lengths, seq_deal, pieces)[0]

    def row_dots(*sides):
        return sum(jnp.sum(w.astype(F32) * g, axis=1) for w, g in sides)

    def finish(ready):
        down, gate_up, bias, (unused, rows) = tie(
            grads_down, grads_gate_up, grad_first[:, side:], ready
        )
        bias = jnp.sum(bias.astype(F32), axis=0, keepdims=True)
        if paired:
            bias = bias + swap(bias, "dp", 1)
            bias = pairs_sum(spread_line([bias] * 4))
        else:
            bias = lax.psum(bias, ("dp", "ty"))
        down, gate_up = reduce_end(down), reduce_end(gate_up)
        mlp = [gate_up[:, :hidden], gate_up[:, hidden:], down]
        return mlp, row_dots((w_gate, mlp[0]), (w_up, mlp[1])) / mlp_gain, bias, given(rows)

    parts, (grads_mlp, own_mlp_gain, bias_grad, output) = scatter_products(
        [(grad_first, 0), (grad_first, 3), (grad_first, 4), (grad_ogate, 0)],
        [(w_first[0], 2 * width, 0), (w_first[1], 256, 0), (w_first[1], 256, 1), (w_second, width, 0)],
        finish,
        spread_plane(reordered([output], column ^ lane)),
    )
    grad_x = on_rows(input_norm_kernel, where, [x_full[:2], grad_second], gains, parts, True)

    grad_x = spread_line(grad_x)
    grad_x, grads_attn = tie(grad_x, grads_attn)
    grad_x = spread_plane(reordered([grad_x], column ^ lane))

    grad_attn = reduce_end(grads_attn)
    grads = [
        grad_attn[:, :width],
        grad_attn[:, width : 2 * width],
        grad_attn[:, 2 * width : side],
        grad_attn[:, last : last + width],
        grad_attn[:, side : side + heads],
    ]
    own_gain = row_dots(*zip((w_query, w_key, w_value, w_ogate, w_forget), grads)) / attn_gain
    grad_gains = spread_plane([jnp.stack([own_gain, own_mlp_gain])] * 4)
    grad_x, grad_gains, grads = tie(grad_x, grad_gains, grads)
    grad_gains = pairs_sum(grad_gains)
    grad_input = given(grad_x)
    return (
        output[None],
        grad_input[None],
        grad_gains[0],
        *grads,
        bias_grad[0, :heads],
        grad_attn[:, last + width :],
        grad_gains[1],
        *grads_mlp,
    )


def solution(mesh):
    tokens, feature, grid, flipped = P("tx", "dp", "ty"), P("ty"), P("ty", "tx"), P("tx", "ty")
    return jax.shard_map(
        on_device,
        mesh=mesh,
        in_specs=(
            tokens,
            tokens,
            P(),
            P(),
            feature,
            grid,
            grid,
            grid,
            grid,
            grid,
            P("tx"),
            flipped,
            feature,
            grid,
            grid,
            flipped,
        ),
        out_specs=(
            tokens,
            tokens,
            feature,
            grid,
            grid,
            grid,
            grid,
            grid,
            P("tx"),
            flipped,
            feature,
            grid,
            grid,
            flipped,
        ),
        check_vma=False,
    )
```
